512 devices in a mesh: dp: 128 (over x, z, core), mp: 4 (over y).
Axes of the slice: x: 4, y: 4, z: 16, core: 2. Of those that a mesh axis runs over, the one named last changes fastest.
Arguments:
- frames: bfloat16 [32768, 1536], P('dp')
- lengths: int32 [128], P('dp'), may hold values from 32 to 256
- send_order: int32 [128, 256], P('dp'), may hold values from 0 to 255, each once within a row
- value_weight: bfloat16 [1536, 768], P('dp', 'mp'), may hold values from -0.15625 to 0.15625
- gate_weight: bfloat16 [1536, 768], P('dp', 'mp'), may hold values from -0.15625 to 0.15625
- down_weight: bfloat16 [1536, 768], P('dp', 'mp'), may hold values from -0.21875 to 0.21875
- cotangent: bfloat16 [32768, 1536], P('dp'), may hold values from -0.125 to 0.125
Outputs:
- branch: bfloat16 [32768, 1536], P('dp')
- grad_value: float32 [1536, 768], P('dp', 'mp')
- grad_gate: float32 [1536, 768], P('dp', 'mp')
- grad_down: float32 [1536, 768], P('dp', 'mp')
The draws below stay inside these ranges and needn't reach their ends.
All inputs are finite; a program needn't handle non-finite values.
Results may differ from the reference program's by a relative error of at most 0.0059.
Values may be sent and summed in bfloat16 or wider, within the bound.
A program may use at most 64 MiB of HBM per device.

```python
import math
import jax
import jax.numpy as jnp
from jax import lax

D = 1536
H = 768
MAXLEN = 256
ROWS = 256
CAP = 2
UTTS = 128
TOKENS = 32768
N_DP = 128


def draw_frames(key, part):
    key = jax.random.fold_in(key, 11)
    k_noise, k_rows, k_cols, k_shift = jax.random.split(key, 4)
    noise = jax.random.normal(k_noise, (TOKENS, D), jnp.float32)
    rows = jnp.exp(jax.random.uniform(k_rows, (TOKENS, 1), jnp.float32, math.log(0.3), math.log(3.0)))
    cols = jnp.exp(jax.random.uniform(k_cols, (1, D), jnp.float32, math.log(0.3), math.log(3.0)))
    shift = jax.random.normal(k_shift, (TOKENS, 1), jnp.float32)
    return jnp.clip((noise * cols + shift) * rows, -64.0, 64.0).astype(jnp.bfloat16)


def set_ends(entries, stream_key, low, high):
    shape = entries.shape
    index_at = [jax.random.randint(jax.random.fold_in(stream_key, axis), (), 0, shape[axis]) for axis in range(len(shape))]
    entries = entries.at[tuple(index_at)].set(low)
    longest = shape.index(max(shape))
    index_at[longest] = (index_at[longest] + 1) % shape[longest]
    return entries.at[tuple(index_at)].set(high)


def spiked(entries, key, source, target, shards_of, factor):
    def block_of(axis_at):
        return (jnp.arange(entries.shape[axis_at]) // (entries.shape[axis_at] // shards_of)).reshape((-1,) + (1,) * (entries.ndim - 1 - axis_at))

    near = jax.random.permutation(key, shards_of)[block_of(target)]
    far = (block_of(target) + shards_of // 2) % shards_of
    return jnp.where((block_of(source) == near) | (block_of(source) == far), factor * entries, entries)


def levels(own_key, shape, shards, low, high):
    def one(position, shards_of):
        draws = jax.random.uniform(jax.random.fold_in(jax.random.fold_in(own_key, 6), position), (shards_of,), jnp.float32, low / len(shards), high / len(shards))
        return jnp.repeat(jnp.exp(draws), shape[position] // shards_of).reshape((-1,) + (1,) * (len(shape) - position - 1))

    factor_of = one(*shards[0])
    for cut in shards[1:]:
        factor_of = factor_of * one(*cut)
    return factor_of


def centred(stream_key, extent, scale, bound, shards=(), held_as=jnp.bfloat16):
    level = levels(stream_key, extent, shards, -0.22, 0.18) if shards else 1.0
    result = jax.random.normal(stream_key, extent, jnp.float32) * scale * level
    return jnp.minimum(jnp.maximum(result, -bound), bound).astype(held_as)


def bell_draw_with(rng, extent, width, most, pieces, heavy, kind=jnp.bfloat16):
    entries = width * jax.random.normal(rng, extent, jnp.float32)
    if pieces:
        entries = entries * levels(rng, extent, pieces, -0.22, 0.18)
    return jnp.clip(spiked(entries, jax.random.fold_in(rng, 3), *heavy), -most, most).astype(kind)


def setup_inputs(seed: int = 0) -> dict:
    splits = jax.random.split(jax.random.key(seed), 8)
    frames = draw_frames(jax.random.fold_in(splits[7], 71), 0)
    lengths = set_ends(jax.random.randint(splits[1], (UTTS,), MAXLEN // 8, MAXLEN + 1), jax.random.fold_in(splits[1], 1), MAXLEN // 8, MAXLEN).astype(jnp.int32)
    send_order = jax.vmap(lambda own: jax.random.permutation(own, ROWS))(jax.random.split(splits[2], N_DP)).reshape((N_DP, ROWS)).astype(jnp.int32)
    value_weight = centred(splits[3], (D, H), D ** -0.5, 0.15625, ((0, 128), (1, 4)))
    gate_weight = centred(splits[4], (D, H), D ** -0.5, 0.15625, ((0, 128), (1, 4)))
    down_weight = centred(splits[5], (D, H), H ** -0.5, 0.21875, ((0, 128), (1, 4)))
    cotangent = bell_draw_with(splits[6], (TOKENS, D), (TOKENS ** -0.5), 0.125, ((0, 128),), (0, 1, 128, 5.5))
    return dict(frames=frames, lengths=lengths, send_order=send_order, value_weight=value_weight, gate_weight=gate_weight, down_weight=down_weight, cotangent=cotangent)


def reference(frames, lengths, send_order, value_weight, gate_weight, down_weight, cotangent):
    slots = jnp.arange(TOKENS, dtype=jnp.int32)
    owner = (slots // MAXLEN).astype(jnp.int32)
    live = slots % MAXLEN < lengths[owner]
    masked = jnp.where(live[:, None], frames, jnp.zeros_like(frames))
    base = (jnp.arange(N_DP, dtype=jnp.int32) * ROWS)[:, None]
    source = (base + send_order.astype(jnp.int32)).reshape(N_DP, N_DP, CAP)
    source = jnp.transpose(source, (1, 0, 2)).reshape(-1).astype(jnp.int32)
    moved = masked[source]
    wide = moved.astype(jnp.float32)
    mean = lax.optimization_barrier(jnp.mean(wide, axis=1, keepdims=True))
    var = lax.optimization_barrier(jnp.mean(jnp.square(wide - mean), axis=1, keepdims=True))
    normed = ((wide - mean) * lax.rsqrt(var + 1e-05)).astype(jnp.bfloat16)
    value = jnp.dot(normed, value_weight, preferred_element_type=jnp.float32)
    gate = jnp.dot(normed, gate_weight, preferred_element_type=jnp.float32)
    sig = jax.nn.sigmoid(gate)
    glu = (value * sig).astype(jnp.bfloat16)
    branch = jnp.dot(glu, down_weight.T, preferred_element_type=jnp.float32).astype(jnp.bfloat16)
    dglu = jnp.dot(cotangent, down_weight, preferred_element_type=jnp.float32)
    d_value = (dglu * sig).astype(jnp.bfloat16)
    d_gate = (dglu * value * sig * (1.0 - sig)).astype(jnp.bfloat16)
    grad_value = jnp.dot(normed.T, d_value, preferred_element_type=jnp.float32)
    grad_gate = jnp.dot(normed.T, d_gate, preferred_element_type=jnp.float32)
    grad_down = jnp.dot(cotangent.T, glu, preferred_element_type=jnp.float32)
    return (branch, grad_value, grad_gate, grad_down)
```

```python
import functools

import jax
import jax.numpy as jnp
from jax import lax
from jax.experimental import pallas as pl
from jax.experimental.pallas import tpu as pltpu
from jax.sharding import PartitionSpec as P

CORES = 2
BF = jnp.bfloat16
F32 = jnp.float32


def ceil16(rows):
    return -(-rows // 16) * 16


def iota(shape, axis):
    return lax.broadcasted_iota(jnp.int32, shape, axis)


def onehot(hit):
    return jnp.where(hit, 1.0, 0.0).astype(BF)


def dot(left, right):
    return jnp.dot(left, right, preferred_element_type=F32)


def contract_rows(left, right):
    return lax.dot_general(left, right, (((0,), (0,)), ((), ())), preferred_element_type=F32)


def contract_cols(left, right):
    return lax.dot_general(left, right, (((1,), (1,)), ((), ())), preferred_element_type=F32)


def mod(value, count):
    return lax.rem(value + count, count)


class Sizes:
    def __init__(self, X, Z, Y, rows, width, own, units):
        self.X, self.Z, self.Y = X, Z, Y
        self.G = X * CORES
        self.rows, self.width, self.own, self.units = rows, width, own, units
        self.cap = rows // (X * Z * CORES)
        self.part = width // Y
        self.pad = ceil16(own)
        self.zrow = self.G * self.cap
        self.grow = self.Z * self.cap
        self.zw = self.G * own
        self.pair = CORES * own
        self.pairpad = ceil16(self.pair)
        self.cols = 3 * units
        self.half = Z // 2 * self.pair
        self.yrow = rows // Y


def kernel(
    cfg,
    lengths, send_order, frames, value_w, gate_w, down_w, cotangent,
    branch, grad_value, grad_gate, grad_down,
    out1, in1, out2, moved_parts, wide, normed,
    pack, shards, slots, weights,
    grads, pair_out, pair_in, sums, x1_out, x1_in, x2_out, x2_in, mine, z_out, z_in, final,
    terms, y1_out, y1_in, y2_out, y2_in, result,
    s_w1, r_w1, s_ring, r_ring, s_sib, r_sib,
    s_a1, r_a1, s_a2, r_a2, s_ag, r_ag,
    s_pair, r_pair, s_x, r_x, s_z, r_z, s_fin, r_fin, s_y, r_y,
):
    X, Z, Y, G = cfg.X, cfg.Z, cfg.Y, cfg.G
    U = cfg.units
    dp = lax.axis_index("dp")
    y = lax.axis_index("mp")
    core = lax.rem(dp, CORES)
    z = lax.rem(lax.div(dp, CORES), Z)
    x = lax.div(dp, CORES * Z)
    g = x * CORES + core
    other = 1 - core

    def at(x_, z_, core_, y_=None):
        return {"dp": (x_ * Z + z_) * CORES + core_, "mp": y if y_ is None else y_}

    def remote(src, dst, send, recv, where):
        return pltpu.make_async_remote_copy(
            src_ref=src, dst_ref=dst, send_sem=send, recv_sem=recv,
            device_id=where, device_id_type=pl.DeviceIdType.MESH,
        )

    def rows_of(ref, start, size, step=16):
        return ref.at[pl.ds(pl.multiple_of(start, step), size)]

    sibling = at(x, z, other)
    y_up, y_down = at(x, z, core, mod(y + 1, Y)), at(x, z, core, mod(y - 1, Y))
    x_up, x_down = at(mod(x + 1, X), z, core), at(mod(x - 1, X), z, core)

    barrier = pltpu.get_barrier_semaphore()
    partners = []
    for o in range(1, G):
        t = mod(g + o, G)
        partners.append(at(lax.div(t, CORES), z, lax.rem(t, CORES)))
    for o in range(1, Z):
        partners.append(at(x, mod(z + o, Z), core))
    partners += [y_up, y_down]
    for who in partners:
        pl.semaphore_signal(barrier, inc=1, device_id=who, device_id_type=pl.DeviceIdType.MESH)

    packed = jnp.concatenate([value_w[...], gate_w[...], down_w[...]], axis=1)
    pack[...] = jnp.zeros_like(pack)
    pack[0 : cfg.own, :] = packed

    R = cfg.rows
    r_nat, r_new = iota((R, R), 0), iota((R, R), 1)
    k_new = lax.rem(r_new, cfg.cap)
    z_new = lax.rem(lax.div(r_new, cfg.cap), Z)
    g_new = lax.div(r_new, cfg.cap * Z)
    natural = ((lax.div(g_new, CORES) * Z + z_new) * CORES + lax.rem(g_new, CORES)) * cfg.cap + k_new
    to_dest = onehot(r_nat == natural)
    order = dot(jnp.broadcast_to(send_order[...].astype(F32).astype(BF), (16, R)), to_dest)[0:1, :]
    slot = iota((R, R), 0)
    pick = onehot((slot.astype(F32) == order) & (slot < lengths[0]))
    columns = pl.ds(pl.multiple_of(y * cfg.part, 128), cfg.part)
    out1[...] = contract_rows(pick, frames[:, columns]).astype(BF)

    pl.semaphore_wait(barrier, len(partners))

    w1, a1 = [], []
    for o in range(1, G):
        t = mod(g + o, G)
        where = at(lax.div(t, CORES), z, lax.rem(t, CORES))
        w1.append(remote(pack, rows_of(shards, g * cfg.pad, cfg.pad), s_w1.at[o], r_w1.at[o], where))
        w1[-1].start()
        a1.append(remote(
            rows_of(out1, t * cfg.grow, cfg.grow), rows_of(in1, g * cfg.grow, cfg.grow),
            s_a1.at[o], r_a1.at[o], where,
        ))
        a1[-1].start()
    rows_of(shards, g * cfg.pad, cfg.pad)[...] = pack[...]
    rows_of(in1, g * cfg.grow, cfg.grow)[...] = rows_of(out1, g * cfg.grow, cfg.grow)[...]

    for copy in w1:
        copy.wait_recv()
    i_new, i_old = iota((cfg.zw, G * cfg.pad), 0), iota((cfg.zw, G * cfg.pad), 1)
    j_old = lax.rem(i_old, cfg.pad)
    squeeze = onehot((j_old < cfg.own) & (lax.div(i_old, cfg.pad) * cfg.own + j_old == i_new))
    slots[z] = dot(squeeze, shards[...]).astype(BF)

    way = 1 - 2 * core
    ring_to = at(x, mod(z + way, Z), core)
    last = Z // 2 - 1
    half_w = cfg.zw // 2

    def slot_ref(step, sign):
        ref = slots.at[mod(z - sign * way * step, Z)]
        return ref

    def half_ref(step, part):
        return rows_of(slots.at[mod(z - way * step, Z)], part * half_w, half_w)

    ring, sib = [], []

    def ring_send(step):
        if step < last:
            ref = slot_ref(step, 1)
        else:
            ref = half_ref(step, core)
        ring.append(remote(ref, ref, s_ring.at[step], r_ring.at[step], ring_to))
        ring[-1].start()

    def ring_take(step):
        ring[step].wait_recv()
        if step < last:
            ref = slot_ref(step + 1, 1)
        else:
            ref = half_ref(step + 1, core)
        if step < last:
            ring_send(step + 1)
        sib.append(remote(ref, ref, s_sib.at[step], r_sib.at[step], sibling))
        sib[-1].start()

    ring_send(0)

    for copy in a1:
        copy.wait_recv()
    r_new, r_old = iota((R, R), 0), iota((R, R), 1)
    k_new = lax.rem(r_new, cfg.cap)
    g_new = lax.rem(lax.div(r_new, cfg.cap), G)
    z_new = lax.div(r_new, cfg.zrow)
    out2[...] = dot(onehot(r_old == (g_new * Z + z_new) * cfg.cap + k_new), in1[...]).astype(BF)
    a2 = []
    for o in range(1, Z):
        t = mod(z + o, Z)
        a2.append(remote(
            rows_of(out2, t * cfg.zrow, cfg.zrow), rows_of(moved_parts.at[y], z * cfg.zrow, cfg.zrow),
            s_a2.at[o], r_a2.at[o], at(x, t, core),
        ))
        a2[-1].start()
    rows_of(moved_parts.at[y], z * cfg.zrow, cfg.zrow)[...] = rows_of(out2, z * cfg.zrow, cfg.zrow)[...]

    for step in range(last):
        ring_take(step)

    for copy in a2:
        copy.wait_recv()

    ag = []
    for i, where in enumerate((y_up, y_down)):
        ag.append(remote(moved_parts.at[y], moved_parts.at[y], s_ag.at[i], r_ag.at[i], where))
        ag[-1].start()

    ring_take(last)

    for copy in ag[:2]:
        copy.wait_recv()
    for i, where in enumerate((y_up, y_down)):
        ref = rows_of(moved_parts.at[mod(y - 1 + 2 * i, Y)], i * (R // 2), R // 2)
        ag.append(remote(ref, ref, s_ag.at[2 + i], r_ag.at[2 + i], where))
        ag[-1].start()

    for copy in sib:
        copy.wait_recv()
    for xi in range(X):
        pieces = [
            slots[zi].astype(F32)[xi * cfg.pair : (xi + 1) * cfg.pair] for zi in range(Z)
        ]
        weights[xi * Z * cfg.pair : (xi + 1) * Z * cfg.pair, :] = jnp.concatenate(pieces, axis=0).astype(BF)

    dglu = dot(cotangent[...], weights[:, 2 * U : 3 * U])

    for copy in ag[2:]:
        copy.wait_recv()

    r_new, r_old = iota((R, R), 0), iota((R, R), 1)
    k_new = lax.rem(r_new, cfg.cap)
    c_new = lax.rem(lax.div(r_new, cfg.cap), CORES)
    z_new = lax.rem(lax.div(r_new, cfg.cap * CORES), Z)
    x_new = lax.div(r_new, cfg.cap * CORES * Z)
    back = onehot(r_old == ((z_new * X + x_new) * CORES + c_new) * cfg.cap + k_new)
    for q in range(Y):
        wide[:, q * cfg.part : (q + 1) * cfg.part] = dot(back, moved_parts[q])
    lines = 32
    for i in range(R // lines):
        block = wide[i * lines : (i + 1) * lines, :]
        mean = jnp.mean(block, axis=1, keepdims=True)
        centred = block - mean
        var = jnp.mean(jnp.square(centred), axis=1, keepdims=True)
        normed[i * lines : (i + 1) * lines, :] = (centred * lax.rsqrt(var + 1e-05)).astype(BF)

    both = dot(normed[...], weights[:, : 2 * U])
    value, gate = both[:, :U], both[:, U : 2 * U]
    sig = jax.nn.sigmoid(gate)
    glu = (value * sig).astype(BF)
    d_value = (dglu * sig).astype(BF)
    d_gate = (dglu * value * sig * (1.0 - sig)).astype(BF)

    grads[:, : 2 * U] = contract_rows(normed[...], jnp.concatenate([d_value, d_gate], axis=1))
    grads[:, 2 * U :] = contract_rows(cotangent[...], glu)
    span = Z * cfg.pair
    pairs = {}
    for o in (2, 1, 3, 0):
        t = mod(x + o, X)
        pair_out[t] = rows_of(grads, t * span + other * cfg.half, cfg.half)[...].astype(BF)
        pairs[o] = remote(pair_out.at[t], pair_in.at[t], s_pair.at[o], r_pair.at[o], sibling)
        pairs[o].start()

    B = cfg.yrow
    terms[...] = contract_cols(glu, weights[:, 2 * U : 3 * U])
    far = rows_of(terms, mod(y + 2, Y) * B, B)
    y1_out[...] = far[...].astype(BF)
    y1 = []
    for i, where in enumerate((y_up, y_down)):
        y1.append(remote(
            y1_out.at[i * (B // 2) : (i + 1) * (B // 2)], y1_in.at[i], s_y.at[i], r_y.at[i], where,
        ))
        y1[-1].start()

    def paired(o):
        t = mod(x + o, X)
        pairs[o].wait_recv()
        sums[o] = rows_of(grads, t * span + core * cfg.half, cfg.half)[...] + pair_in[t].astype(F32)

    S = cfg.half
    paired(2)
    x1_out[...] = sums[2].astype(BF)
    x1 = []
    for i, where in enumerate((x_up, x_down)):
        x1.append(remote(
            x1_out.at[i * (S // 2) : (i + 1) * (S // 2)], x1_in.at[i], s_x.at[i], r_x.at[i], where,
        ))
        x1[-1].start()
    paired(1)
    paired(3)
    paired(0)

    y2 = []
    for i, where in enumerate((y_up, y_down)):
        y1[i].wait_recv()
        mid = rows_of(terms, mod(y + 1 - 2 * i, Y) * B, B)
        mid[i * (B // 2) : (i + 1) * (B // 2), :] = (
            mid[i * (B // 2) : (i + 1) * (B // 2), :] + y1_in[i].astype(F32)
        )
        y2_out[i] = mid[...].astype(BF)
        y2.append(remote(y2_out.at[i], y2_in.at[i], s_y.at[2 + i], r_y.at[2 + i], where))
        y2[-1].start()

    x2 = []
    for i, where in enumerate((x_up, x_down)):
        x1[i].wait_recv()
        lo, hi = i * (S // 2), (i + 1) * (S // 2)
        sums[1 + 2 * i, lo:hi, :] = sums[1 + 2 * i, lo:hi, :] + x1_in[i].astype(F32)
        x2_out[i] = sums[1 + 2 * i].astype(BF)
        x2.append(remote(x2_out.at[i], x2_in.at[i], s_x.at[2 + i], r_x.at[2 + i], where))
        x2[-1].start()

    for copy in y2:
        copy.wait_recv()
    own_rows = (
        rows_of(terms, y * B, B)[...] + y2_in[0].astype(F32) + y2_in[1].astype(F32)
    )
    rows_of(result, y * B, B)[...] = own_rows.astype(BF)
    yg = []
    for i, where in enumerate((y_up, y_down)):
        ref = rows_of(result, y * B, B)
        yg.append(remote(ref, ref, s_y.at[4 + i], r_y.at[4 + i], where))
        yg[-1].start()

    for copy in x2:
        copy.wait_recv()
    mine[...] = sums[0] + x2_in[0].astype(F32) + x2_in[1].astype(F32)
    Q = cfg.pair
    z_out[...] = jnp.zeros_like(z_out)
    zs = []
    for i in range(Z // 2):
        z_out[i, 0:Q, :] = mine[i * Q : (i + 1) * Q, :].astype(BF)
        t = core * (Z // 2) + i
        zs.append((t != z, remote(z_out.at[i], z_in.at[z], s_z.at[i], r_z.at[z], at(x, t, core))))
        pl.when(t != z)(zs[-1][1].start)

    for copy in yg[:2]:
        copy.wait_recv()
    for i, where in enumerate((y_up, y_down)):
        ref = rows_of(result, mod(y - 1 + 2 * i, Y) * B + i * (B // 2), B // 2)
        yg.append(remote(ref, ref, s_y.at[6 + i], r_y.at[6 + i], where))
        yg[-1].start()

    hand = remote(final, final, s_fin.at[0], r_fin.at[0], sibling)
    is_owner = lax.div(z, Z // 2) == core

    @pl.when(is_owner)
    def _():
        for o in range(1, Z):
            t = mod(z + o, Z)
            remote(z_out.at[0], z_in.at[t], s_z.at[0], r_z.at[t], sibling).wait_recv()
        total = rows_of(mine, (z - core * (Z // 2)) * Q, Q, 8)[...]
        for o in range(1, Z):
            total = total + z_in[mod(z + o, Z)][0:Q].astype(F32)
        final[...] = total
        hand.start()
        hand.wait_send()

    @pl.when(jnp.logical_not(is_owner))
    def _():
        hand.wait_recv()

    whole = final[...]
    owned = jnp.where(core == 0, whole[0 : cfg.own], whole[cfg.own : 2 * cfg.own])
    grad_value[...] = owned[:, :U]
    grad_gate[...] = owned[:, U : 2 * U]
    grad_down[...] = owned[:, 2 * U :]

    for copy in yg[2:]:
        copy.wait_recv()
    branch[...] = result[...]

    for copy in w1 + a1 + ring + sib + a2 + ag + list(pairs.values()) + y1 + x1 + y2 + x2 + yg:
        copy.wait_send()
    for needed, copy in zs:
        pl.when(needed)(copy.wait_send)


def module(cfg, frames, lengths, send_order, value_weight, gate_weight, down_weight, cotangent):
    X, Z, Y, G, R, D, U = cfg.X, cfg.Z, cfg.Y, cfg.G, cfg.rows, cfg.width, cfg.units
    C, S, B = cfg.cols, cfg.half, cfg.yrow
    vmem = pl.BlockSpec(memory_space=pltpu.VMEM)
    sem = pltpu.SemaphoreType.DMA
    buffers = [
        ((R, cfg.part), BF),
        ((R, cfg.part), BF),
        ((R, cfg.part), BF),
        ((Y, R, cfg.part), BF),
        ((R, D), F32),
        ((R, D), BF),
        ((cfg.pad, C), BF),
        ((G * cfg.pad, C), BF),
        ((Z, cfg.zw, C), BF),
        ((D, C), BF),
        ((D, C), F32),
        ((X, S, C), BF),
        ((X, S, C), BF),
        ((X, S, C), F32),
        ((S, C), BF),
        ((2, S // 2, C), BF),
        ((2, S, C), BF),
        ((2, S, C), BF),
        ((S, C), F32),
        ((Z // 2, cfg.pairpad, C), BF),
        ((Z, cfg.pairpad, C), BF),
        ((cfg.pair, C), F32),
        ((R, D), F32),
        ((B, D), BF),
        ((2, B // 2, D), BF),
        ((2, B, D), BF),
        ((2, B, D), BF),
        ((R, D), BF),
    ]
    sems = [G, Z // 2, Z // 2, G, Z, 4, X, 4, Z, 1, 8]
    return pl.pallas_call(
        functools.partial(kernel, cfg),
        out_shape=(
            jax.ShapeDtypeStruct((R, D), BF),
            jax.ShapeDtypeStruct((cfg.own, U), F32),
            jax.ShapeDtypeStruct((cfg.own, U), F32),
            jax.ShapeDtypeStruct((cfg.own, U), F32),
        ),
        in_specs=[pl.BlockSpec(memory_space=pltpu.SMEM)] + [vmem] * 6,
        out_specs=(vmem,) * 4,
        scratch_shapes=[pltpu.VMEM(shape, kind) for shape, kind in buffers]
        + [sem((n,)) for n in sems for _ in range(2)],
        compiler_params=pltpu.CompilerParams(
            collective_id=0, has_side_effects=True, vmem_limit_bytes=56 * 1024 * 1024
        ),
    )(lengths, send_order, frames, value_weight, gate_weight, down_weight, cotangent)


def build(mesh, X, Z):
    def shards(frames, lengths, send_order, value_weight, gate_weight, down_weight, cotangent):
        cfg = Sizes(
            X, Z, mesh.shape["mp"], frames.shape[0], frames.shape[1],
            value_weight.shape[0], value_weight.shape[1],
        )
        return module(
            cfg, frames, lengths, send_order, value_weight, gate_weight, down_weight, cotangent
        )

    return jax.shard_map(
        shards,
        mesh=mesh,
        in_specs=(
            P("dp", None),
            P("dp"),
            P("dp", None),
            P("dp", "mp"),
            P("dp", "mp"),
            P("dp", "mp"),
            P("dp", None),
        ),
        out_specs=(P("dp", None), P("dp", "mp"), P("dp", "mp"), P("dp", "mp")),
        check_vma=False,
    )


def solution(mesh):
    return build(mesh, 4, 16)
```

```python
import functools

import jax
import jax.numpy as jnp
from jax import lax
from jax.experimental import pallas as pl
from jax.experimental.pallas import tpu as pltpu
from jax.sharding import PartitionSpec as P

CORES = 2
BF = jnp.bfloat16
F32 = jnp.float32


def ceil16(rows):
    return -(-rows // 16) * 16


def iota(shape, axis):
    return lax.broadcasted_iota(jnp.int32, shape, axis)


def onehot(hit):
    return jnp.where(hit, 1.0, 0.0).astype(BF)


def dot(left, right):
    return jnp.dot(left, right, preferred_element_type=F32)


def contract_rows(left, right):
    return lax.dot_general(left, right, (((0,), (0,)), ((), ())), preferred_element_type=F32)


def contract_cols(left, right):
    return lax.dot_general(left, right, (((1,), (1,)), ((), ())), preferred_element_type=F32)


def mod(value, count):
    return lax.rem(value + count, count)


class Sizes:
    def __init__(self, X, Z, Y, rows, width, own, units):
        self.X, self.Z, self.Y = X, Z, Y
        self.G = X * CORES
        self.rows, self.width, self.own, self.units = rows, width, own, units
        self.cap = rows // (X * Z * CORES)
        self.part = width // Y
        self.pad = ceil16(own)
        self.zrow = self.G * self.cap
        self.grow = self.Z * self.cap
        self.zw = self.G * own
        self.pair = CORES * own
        self.pairpad = ceil16(self.pair)
        self.cols = 3 * units
        self.half = Z // 2 * self.pair
        self.yrow = rows // Y


def kernel(
    cfg,
    lengths, send_order, frames, value_w, gate_w, down_w, cotangent,
    branch, owned,
    out1, in1, out2, moved_parts, wide, normed,
    pack, shards, slots, weights,
    pair_out, pair_in, sums, x1_out, x1_in, x2_out, x2_in, mine, za_out, za_in, acc, zb_out, zb_in, final,
    terms, y1_out, y1_in, y2_out, y2_in, result,
    s_w1, r_w1, s_ring, r_ring, s_sib, r_sib,
    s_a1, r_a1, s_a2, r_a2, s_ag, r_ag,
    s_pair, r_pair, s_x, r_x, s_za, r_za, s_zb, r_zb, s_fin, r_fin, s_y, r_y,
):
    X, Z, Y, G = cfg.X, cfg.Z, cfg.Y, cfg.G
    U = cfg.units
    dp = lax.axis_index("dp")
    y = lax.axis_index("mp")
    core = lax.rem(dp, CORES)
    z = lax.rem(lax.div(dp, CORES), Z)
    x = lax.div(dp, CORES * Z)
    g = x * CORES + core
    other = 1 - core

    def at(x_, z_, core_, y_=None):
        return {"dp": (x_ * Z + z_) * CORES + core_, "mp": y if y_ is None else y_}

    def remote(src, dst, send, recv, where):
        return pltpu.make_async_remote_copy(
            src_ref=src, dst_ref=dst, send_sem=send, recv_sem=recv,
            device_id=where, device_id_type=pl.DeviceIdType.MESH,
        )

    def rows_of(ref, start, size, step=16):
        return ref.at[pl.ds(pl.multiple_of(start, step), size)]

    sibling = at(x, z, other)
    y_up, y_down = at(x, z, core, mod(y + 1, Y)), at(x, z, core, mod(y - 1, Y))
    x_up, x_down = at(mod(x + 1, X), z, core), at(mod(x - 1, X), z, core)

    barrier = pltpu.get_barrier_semaphore()
    partners = []
    for o in range(1, G):
        t = mod(g + o, G)
        partners.append(at(lax.div(t, CORES), z, lax.rem(t, CORES)))
    for o in range(1, Z):
        partners.append(at(x, mod(z + o, Z), core))
    for o in range(1, Y):
        partners.append(at(x, z, core, mod(y + o, Y)))
    for who in partners:
        pl.semaphore_signal(barrier, inc=1, device_id=who, device_id_type=pl.DeviceIdType.MESH)

    packed = jnp.concatenate([value_w[...], gate_w[...], down_w[...]], axis=1)
    pack[...] = jnp.zeros_like(pack)
    pack[0 : cfg.own, :] = packed

    R = cfg.rows
    r_nat, r_new = iota((R, R), 0), iota((R, R), 1)
    k_new = lax.rem(r_new, cfg.cap)
    z_new = lax.rem(lax.div(r_new, cfg.cap), Z)
    g_new = lax.div(r_new, cfg.cap * Z)
    natural = ((lax.div(g_new, CORES) * Z + z_new) * CORES + lax.rem(g_new, CORES)) * cfg.cap + k_new
    to_dest = onehot(r_nat == natural)
    order = dot(jnp.broadcast_to(send_order[...].astype(F32).astype(BF), (16, R)), to_dest)[0:1, :]
    slot = iota((R, R), 0)
    pick = onehot((slot.astype(F32) == order) & (slot < lengths[0]))
    columns = pl.ds(pl.multiple_of(y * cfg.part, 128), cfg.part)
    out1[...] = contract_rows(pick, frames[:, columns]).astype(BF)

    pl.semaphore_wait(barrier, len(partners))

    w1, a1 = [], []
    for o in range(1, G):
        t = mod(g + o, G)
        where = at(lax.div(t, CORES), z, lax.rem(t, CORES))
        w1.append(remote(pack, rows_of(shards, g * cfg.pad, cfg.pad), s_w1.at[o], r_w1.at[o], where))
        w1[-1].start()
        a1.append(remote(
            rows_of(out1, t * cfg.grow, cfg.grow), rows_of(in1, g * cfg.grow, cfg.grow),
            s_a1.at[o], r_a1.at[o], where,
        ))
        a1[-1].start()
    rows_of(shards, g * cfg.pad, cfg.pad)[...] = pack[...]
    rows_of(in1, g * cfg.grow, cfg.grow)[...] = rows_of(out1, g * cfg.grow, cfg.grow)[...]

    for copy in w1:
        copy.wait_recv()
    i_new, i_old = iota((cfg.zw, G * cfg.pad), 0), iota((cfg.zw, G * cfg.pad), 1)
    j_old = lax.rem(i_old, cfg.pad)
    squeeze = onehot((j_old < cfg.own) & (lax.div(i_old, cfg.pad) * cfg.own + j_old == i_new))
    slots[z] = dot(squeeze, shards[...]).astype(BF)

    way = 1 - 2 * core
    ring_to = at(x, mod(z + way, Z), core)
    last = Z // 2 - 1
    half_w = cfg.zw // 2
    cuts = [(lo, min(32, cfg.zw - lo)) for lo in range(0, cfg.zw, 32)]
    half_cuts = [(lo, min(32, half_w - lo)) for lo in range(0, half_w, 32)]

    ring, sib = {}, {}

    def piece(hop, k):
        ref = slots.at[mod(z - way * hop, Z)]
        if hop <= last:
            return rows_of(ref, *cuts[k])
        return rows_of(ref, core * half_w + half_cuts[k][0], half_cuts[k][1])

    def ring_send(hop, k):
        ref = piece(hop, k)
        if hop == last:
            lo, size = half_cuts[k]
            ref = rows_of(slots.at[mod(z - way * hop, Z)], core * half_w + lo, size)
        ring[hop, k] = remote(ref, ref, s_ring.at[hop, k], r_ring.at[hop, k], ring_to)
        ring[hop, k].start()

    def ring_take(hop):
        pieces = len(half_cuts) if hop == last + 1 else len(cuts)
        for k in range(pieces):
            ring[hop - 1, k].wait_recv()
            if hop < last:
                ring_send(hop, k)
            if hop != last:
                sib[hop, k] = remote(piece(hop, k), piece(hop, k), s_sib.at[hop - 1, k], r_sib.at[hop - 1, k], sibling)
                sib[hop, k].start()
        if hop == last:
            for k in range(len(half_cuts)):
                ring_send(hop, k)
            for k in range(pieces):
                sib[hop, k] = remote(piece(hop, k), piece(hop, k), s_sib.at[hop - 1, k], r_sib.at[hop - 1, k], sibling)
                sib[hop, k].start()

    for k in range(len(cuts)):
        ring_send(0, k)

    for copy in a1:
        copy.wait_recv()
    r_new, r_old = iota((R, R), 0), iota((R, R), 1)
    k_new = lax.rem(r_new, cfg.cap)
    g_new = lax.rem(lax.div(r_new, cfg.cap), G)
    z_new = lax.div(r_new, cfg.zrow)
    out2[...] = dot(onehot(r_old == (g_new * Z + z_new) * cfg.cap + k_new), in1[...]).astype(BF)
    here = moved_parts.at[y]
    place = [0] + [2 * o - 1 if o <= Z // 2 else 2 * (Z - o) for o in range(1, Z)]
    a2 = {}
    for o in sorted(range(1, Z), key=lambda o: place[Z - o]):
        t = mod(z + o, Z)
        a2[place[Z - o]] = remote(
            rows_of(out2, t * cfg.zrow, cfg.zrow), rows_of(here, place[Z - o] * cfg.zrow, cfg.zrow),
            s_a2.at[o], r_a2.at[o], at(x, t, core),
        )
        a2[place[Z - o]].start()
    here[0 : cfg.zrow, :] = rows_of(out2, z * cfg.zrow, cfg.zrow)[...]

    ag = []
    parcels = 4
    each = R // parcels

    def share(j):
        for p in range(j * each // cfg.zrow, (j + 1) * each // cfg.zrow):
            if p:
                a2[p].wait_recv()
        ref = rows_of(here, j * each, each)
        for d in (1, 3, 2):
            ag.append(remote(ref, ref, s_ag.at[j, d], r_ag.at[j, d], at(x, z, core, mod(y + d, Y))))
            ag[-1].start()

    ring_take(1)
    ring_take(2)
    share(0)
    ring_take(3)
    share(1)
    ring_take(4)
    share(2)
    ring_take(5)
    share(3)
    for hop in range(6, last + 2):
        ring_take(hop)

    for copy in sib.values():
        copy.wait_recv()
    for xi in range(X):
        pieces = [
            slots[zi].astype(F32)[xi * cfg.pair : (xi + 1) * cfg.pair] for zi in range(Z)
        ]
        weights[xi * Z * cfg.pair : (xi + 1) * Z * cfg.pair, :] = jnp.concatenate(pieces, axis=0).astype(BF)

    dglu = dot(cotangent[...], weights[:, 2 * U : 3 * U])

    for copy in ag:
        copy.wait_recv()

    r_new, r_old = iota((R, R), 0), iota((R, R), 1)
    k_new = lax.rem(r_new, cfg.cap)
    c_new = lax.rem(lax.div(r_new, cfg.cap), CORES)
    z_new = lax.rem(lax.div(r_new, cfg.cap * CORES), Z)
    x_new = lax.div(r_new, cfg.cap * CORES * Z)
    away = lax.rem(z_new - z + Z, Z)
    place_new = jnp.where(away > Z // 2, 2 * (Z - away), jnp.maximum(2 * away - 1, 0))
    back = onehot(r_old == ((place_new * X + x_new) * CORES + c_new) * cfg.cap + k_new)
    for q in range(Y):
        wide[:, q * cfg.part : (q + 1) * cfg.part] = dot(back, moved_parts[q])
    lines = 32
    for i in range(R // lines):
        block = wide[i * lines : (i + 1) * lines, :]
        mean = jnp.mean(block, axis=1, keepdims=True)
        centred = block - mean
        var = jnp.mean(jnp.square(centred), axis=1, keepdims=True)
        normed[i * lines : (i + 1) * lines, :] = (centred * lax.rsqrt(var + 1e-05)).astype(BF)

    both = dot(normed[...], weights[:, : 2 * U])
    value, gate = both[:, :U], both[:, U : 2 * U]
    sig = jax.nn.sigmoid(gate)
    glu = (value * sig).astype(BF)
    d_value = (dglu * sig).astype(BF)
    d_gate = (dglu * value * sig * (1.0 - sig)).astype(BF)

    d_both = jnp.concatenate([d_value, d_gate], axis=1)
    span = Z * cfg.pair
    S = cfg.half
    pairs = {}
    for o in (2, 1, 3, 0):
        t = mod(x + o, X)
        cols = pl.ds(pl.multiple_of(t * span, 128), span)
        block = jnp.concatenate(
            [contract_rows(normed[:, cols], d_both), contract_rows(cotangent[:, cols], glu)], axis=1
        )
        sums[o] = jnp.where(core == 0, block[:S], block[S:])
        pair_out[o] = jnp.where(core == 0, block[S:], block[:S]).astype(BF)
        pairs[o] = remote(pair_out.at[o], pair_in.at[o], s_pair.at[o], r_pair.at[o], sibling)
        pairs[o].start()

    B = cfg.yrow
    terms[...] = contract_cols(glu, weights[:, 2 * U : 3 * U])
    far = rows_of(terms, mod(y + 2, Y) * B, B)
    y1_out[...] = far[...].astype(BF)
    y1 = []
    for i, where in enumerate((y_up, y_down)):
        y1.append(remote(
            y1_out.at[i * (B // 2) : (i + 1) * (B // 2)], y1_in.at[i], s_y.at[i], r_y.at[i], where,
        ))
        y1[-1].start()

    def paired(o):
        pairs[o].wait_recv()
        sums[o] = sums[o] + pair_in[o].astype(F32)

    chunk = S // 2
    part = chunk // 2
    paired(2)
    x1_out[...] = sums[2].astype(BF)
    x1, x2 = {}, {}
    for q in range(2):
        for i, where in enumerate((x_up, x_down)):
            lo = q * chunk + i * part
            x1[q, i] = remote(
                x1_out.at[lo : lo + part], x1_in.at[q, i], s_x.at[q, i], r_x.at[q, i], where,
            )
            x1[q, i].start()
    paired(1)
    paired(3)
    paired(0)

    for q in range(2):
        for i, where in enumerate((x_up, x_down)):
            x1[q, i].wait_recv()
            lo = q * chunk + i * part
            sums[1 + 2 * i, lo : lo + part, :] = sums[1 + 2 * i, lo : lo + part, :] + x1_in[q, i].astype(F32)
            x2_out[q, i] = sums[1 + 2 * i, q * chunk : (q + 1) * chunk, :].astype(BF)
            x2[q, i] = remote(x2_out.at[q, i], x2_in.at[q, i], s_x.at[2 + q, i], r_x.at[2 + q, i], where)
            x2[q, i].start()

    y2 = []
    for i, where in enumerate((y_up, y_down)):
        y1[i].wait_recv()
        mid = rows_of(terms, mod(y + 1 - 2 * i, Y) * B, B)
        mid[i * (B // 2) : (i + 1) * (B // 2), :] = (
            mid[i * (B // 2) : (i + 1) * (B // 2), :] + y1_in[i].astype(F32)
        )
        y2_out[i] = mid[...].astype(BF)
        y2.append(remote(y2_out.at[i], y2_in.at[i], s_y.at[2 + i], r_y.at[2 + i], where))
        y2[-1].start()

    for copy in y2:
        copy.wait_recv()
    own_rows = (
        rows_of(terms, y * B, B)[...] + y2_in[0].astype(F32) + y2_in[1].astype(F32)
    )
    rows_of(result, y * B, B)[...] = own_rows.astype(BF)
    yg = []
    for i, where in enumerate((y_up, y_down)):
        ref = rows_of(result, y * B, B)
        yg.append(remote(ref, ref, s_y.at[4 + i], r_y.at[4 + i], where))
        yg[-1].start()

    for q in range(2):
        x2[q, 0].wait_recv()
        x2[q, 1].wait_recv()
        lo, hi = q * chunk, (q + 1) * chunk
        mine[lo:hi, :] = sums[0, lo:hi, :] + x2_in[q, 0].astype(F32) + x2_in[q, 1].astype(F32)
    Q = cfg.pair
    J = Z // 2 // 4

    def comb(r):
        return [rows_of(mine, (r + 4 * j) * Q, Q, 8)[...] for j in range(J)]

    za = []
    for k, a in enumerate((1, -1, 2)):
        za_out[k] = jnp.concatenate(comb(lax.rem(z + a + Z, 4)), axis=0).astype(BF)
        za.append(remote(za_out.at[k], za_in.at[k], s_za.at[k], r_za.at[k], at(x, mod(z + a, Z), core)))
        za[-1].start()

    for copy in yg[:2]:
        copy.wait_recv()
    for i, where in enumerate((y_up, y_down)):
        ref = rows_of(result, mod(y - 1 + 2 * i, Y) * B + i * (B // 2), B // 2)
        yg.append(remote(ref, ref, s_y.at[6 + i], r_y.at[6 + i], where))
        yg[-1].start()

    for copy in za:
        copy.wait_recv()
    mod4 = lax.rem(z, 4)
    own_comb = comb(mod4)
    arrived = za_in[0].astype(F32) + za_in[1].astype(F32) + za_in[2].astype(F32)
    zb_out[...] = jnp.zeros_like(zb_out)
    zb = []
    for j in range(J):
        part_sum = own_comb[j] + arrived[j * Q : (j + 1) * Q]
        acc[j] = part_sum
        zb_out[j, 0:Q, :] = part_sum.astype(BF)
        t = core * (Z // 2) + 4 * j + mod4
        away = lax.div(mod(z - t, Z), 4)
        zb.append((t != z, remote(zb_out.at[j], zb_in.at[away], s_zb.at[j], r_zb.at[away], at(x, t, core))))
        pl.when(t != z)(zb[-1][1].start)

    hand = remote(final, final, s_fin.at[0], r_fin.at[0], sibling)
    is_owner = lax.div(z, Z // 2) == core

    @pl.when(is_owner)
    def _():
        total = acc[lax.rem(lax.div(z, 4), J)]
        for away in range(1, Z // 4):
            remote(zb_out.at[0], zb_in.at[away], s_zb.at[0], r_zb.at[away], sibling).wait_recv()
            total = total + zb_in[away, 0:Q, :].astype(F32)
        final[...] = total
        hand.start()
        hand.wait_send()

    @pl.when(jnp.logical_not(is_owner))
    def _():
        hand.wait_recv()

    whole = final[...]
    owned[...] = jnp.where(core == 0, whole[0 : cfg.own], whole[cfg.own : 2 * cfg.own])

    for copy in yg[2:]:
        copy.wait_recv()
    branch[...] = result[...]

    for copy in w1 + a1 + ag + za + y1 + y2 + yg:
        copy.wait_send()
    for group in (ring, sib, a2, pairs, x1, x2):
        for copy in group.values():
            copy.wait_send()
    for needed, copy in zb:
        pl.when(needed)(copy.wait_send)


def place_results(units, branch_in, owned_in, branch, grad_value, grad_gate, grad_down):
    branch[...] = branch_in[...]
    grad_value[...] = owned_in[:, :units]
    grad_gate[...] = owned_in[:, units : 2 * units]
    grad_down[...] = owned_in[:, 2 * units :]


def module(cfg, frames, lengths, send_order, value_weight, gate_weight, down_weight, cotangent):
    X, Z, Y, G, R, D, U = cfg.X, cfg.Z, cfg.Y, cfg.G, cfg.rows, cfg.width, cfg.units
    C, S, B = cfg.cols, cfg.half, cfg.yrow
    vmem = pl.BlockSpec(memory_space=pltpu.VMEM)
    sem = pltpu.SemaphoreType.DMA
    buffers = [
        ((R, cfg.part), BF),
        ((R, cfg.part), BF),
        ((R, cfg.part), BF),
        ((Y, R, cfg.part), BF),
        ((R, D), F32),
        ((R, D), BF),
        ((cfg.pad, C), BF),
        ((G * cfg.pad, C), BF),
        ((Z, cfg.zw, C), BF),
        ((D, C), BF),
        ((X, S, C), BF),
        ((X, S, C), BF),
        ((X, S, C), F32),
        ((S, C), BF),
        ((2, 2, S // 4, C), BF),
        ((2, 2, S // 2, C), BF),
        ((2, 2, S // 2, C), BF),
        ((S, C), F32),
        ((3, Z // 8 * cfg.pair, C), BF),
        ((3, Z // 8 * cfg.pair, C), BF),
        ((Z // 8, cfg.pair, C), F32),
        ((Z // 8, cfg.pairpad, C), BF),
        ((Z // 4, cfg.pairpad, C), BF),
        ((cfg.pair, C), F32),
        ((R, D), F32),
        ((B, D), BF),
        ((2, B // 2, D), BF),
        ((2, B, D), BF),
        ((2, B, D), BF),
        ((R, D), BF),
    ]
    hops = (Z // 2, -(-cfg.zw // 32))
    sems = [(G,), hops, hops, (G,), (Z,), (4, 4), (X,), (4, 2), (3,), (Z // 4,), (1,), (8,)]
    branch, owned = pl.pallas_call(
        functools.partial(kernel, cfg),
        out_shape=(jax.ShapeDtypeStruct((R, D), BF), jax.ShapeDtypeStruct((cfg.own, C), F32)),
        in_specs=[pl.BlockSpec(memory_space=pltpu.SMEM)] + [vmem] * 6,
        out_specs=(vmem,) * 2,
        scratch_shapes=[pltpu.VMEM(shape, kind) for shape, kind in buffers]
        + [sem(n) for n in sems for _ in range(2)],
        compiler_params=pltpu.CompilerParams(
            collective_id=0, has_side_effects=True, vmem_limit_bytes=56 * 1024 * 1024
        ),
    )(lengths, send_order, frames, value_weight, gate_weight, down_weight, cotangent)
    return pl.pallas_call(
        functools.partial(place_results, U),
        out_shape=(jax.ShapeDtypeStruct((R, D), BF),) + (jax.ShapeDtypeStruct((cfg.own, U), F32),) * 3,
        in_specs=[vmem] * 2,
        out_specs=(vmem,) * 4,
    )(branch, owned)


def build(mesh, X, Z):
    def shards(frames, lengths, send_order, value_weight, gate_weight, down_weight, cotangent):
        cfg = Sizes(
            X, Z, mesh.shape["mp"], frames.shape[0], frames.shape[1],
            value_weight.shape[0], value_weight.shape[1],
        )
        return module(
            cfg, frames, lengths, send_order, value_weight, gate_weight, down_weight, cotangent
        )

    return jax.shard_map(
        shards,
        mesh=mesh,
        in_specs=(
            P("dp", None),
            P("dp"),
            P("dp", None),
            P("dp", "mp"),
            P("dp", "mp"),
            P("dp", "mp"),
            P("dp", None),
        ),
        out_specs=(P("dp", None), P("dp", "mp"), P("dp", "mp"), P("dp", "mp")),
        check_vma=False,
    )


def solution(mesh):
    return build(mesh, 4, 16)
```

```python
import functools

import jax
import jax.numpy as jnp
from jax import lax
from jax.experimental import pallas as pl
from jax.experimental.pallas import tpu as pltpu
from jax.sharding import PartitionSpec as P

CORES = 2
BF = jnp.bfloat16
F32 = jnp.float32


def ceil16(rows):
    return -(-rows // 16) * 16


def iota(shape, axis):
    return lax.broadcasted_iota(jnp.int32, shape, axis)


def onehot(hit):
    return jnp.where(hit, 1.0, 0.0).astype(BF)


def dot(left, right):
    return jnp.dot(left, right, preferred_element_type=F32)


def contract_rows(left, right):
    return lax.dot_general(left, right, (((0,), (0,)), ((), ())), preferred_element_type=F32)


def contract_cols(left, right):
    return lax.dot_general(left, right, (((1,), (1,)), ((), ())), preferred_element_type=F32)


def mod(value, count):
    return lax.rem(value + count, count)


class Sizes:
    def __init__(self, X, Z, Y, rows, width, own, units):
        self.X, self.Z, self.Y = X, Z, Y
        self.G = X * CORES
        self.rows, self.width, self.own, self.units = rows, width, own, units
        self.cap = rows // (X * Z * CORES)
        self.part = width // Y
        self.pad = ceil16(own)
        self.zrow = self.G * self.cap
        self.grow = self.Z * self.cap
        self.far = Z // 4
        self.comb = self.far * own
        self.pair = CORES * own
        self.pairpad = ceil16(self.pair)
        self.cols = 3 * units
        self.half = Z // 2 * self.pair
        self.yrow = rows // Y


def kernel(
    cfg,
    lengths, send_order, frames, value_w, gate_w, down_w, cotangent,
    branch, owned,
    out1, in1, out2, moved, normed, cot, glu_rows,
    shards, w_own, w_sib, weights,
    block, pair_out, pair_in, x_out, x_in, near_out, near_in, acc, far_out, far_in, final,
    y_own, y_out, y_in, result,
    s_a1, r_a1, s_a2, r_a2, s_ag, r_ag,
    s_wf, r_wf, s_wn, r_wn, s_wx, r_wx, s_sib, r_sib,
    s_pair, r_pair, s_x, r_x, s_near, r_near, s_far, r_far, s_fin, r_fin, s_y, r_y, s_yg, r_yg,
    relay,
):
    X, Z, Y, G = cfg.X, cfg.Z, cfg.Y, cfg.G
    R, U, F, cap = cfg.rows, cfg.units, cfg.far, cfg.cap
    dp = lax.axis_index("dp")
    y = lax.axis_index("mp")
    core = lax.rem(dp, CORES)
    z = lax.rem(lax.div(dp, CORES), Z)
    x = lax.div(dp, CORES * Z)
    g = x * CORES + core
    other = 1 - core
    sibling = {"dp": dp + 1 - 2 * core, "mp": y}

    def at(x_, z_, core_):
        return {"dp": (x_ * Z + z_) * CORES + core_, "mp": y}

    def at_x(o):
        return at(mod(x + o, X), z, core)

    def at_z(o):
        return at(x, mod(z + o, Z), core)

    def at_y(o):
        return {"dp": dp, "mp": mod(y + o, Y)}

    def at_g(t):
        return at(lax.div(t, CORES), z, lax.rem(t, CORES))

    def send(src, dst, sent, arrived, where):
        copy = pltpu.make_async_remote_copy(
            src_ref=src, dst_ref=dst, send_sem=sent, recv_sem=arrived,
            device_id=where, device_id_type=pl.DeviceIdType.MESH,
        )
        copy.start()

    def drain(sem, ref):
        pltpu.make_async_copy(ref, ref, sem).wait()

    def rows_of(ref, start, size, step=16):
        return ref.at[pl.ds(pl.multiple_of(start, step), size)]

    barrier = pltpu.get_barrier_semaphore()
    partners = [at_g(mod(g + o, G)) for o in range(1, G)]
    partners += [at_z(o * s) for o in range(1, 5) for s in (1, -1)]
    partners += [at_y(o) for o in range(1, Y)]
    for who in partners:
        pl.semaphore_signal(barrier, inc=1, device_id=who, device_id_type=pl.DeviceIdType.MESH)

    packed = jnp.concatenate([value_w[...], gate_w[...], down_w[...]], axis=1)
    mine = shards.at[1, 0 : cfg.pad]
    mine[...] = jnp.zeros_like(mine)
    shards[1, 0 : cfg.own, :] = packed

    row, place = iota((R, R), 0), iota((1, R), 1)
    k_of, z_of, g_of = lax.rem(place, cap), lax.rem(lax.div(place, cap), Z), lax.div(place, cap * Z)
    natural = ((lax.div(g_of, CORES) * Z + z_of) * CORES + lax.rem(g_of, CORES)) * cap + k_of
    numbers = jnp.broadcast_to(send_order[...].astype(F32).astype(BF), (16, R))
    order = dot(numbers, onehot(row == natural))[0:1, :]
    pick = onehot((row.astype(F32) == order) & (row < lengths[0]))
    columns = pl.ds(pl.multiple_of(y * cfg.part, 128), cfg.part)
    out1[...] = contract_rows(pick, frames[:, columns]).astype(BF)

    pl.semaphore_wait(barrier, len(partners))
    for o in (4, -4):
        pl.semaphore_signal(relay, inc=1, device_id=at_z(o), device_id_type=pl.DeviceIdType.MESH)

    for o in range(1, G):
        t = mod(g + o, G)
        send(
            rows_of(out1, t * cfg.grow, cfg.grow), rows_of(in1, g * cfg.grow, cfg.grow),
            s_a1, r_a1, at_g(t),
        )
    rows_of(in1, g * cfg.grow, cfg.grow)[...] = rows_of(out1, g * cfg.grow, cfg.grow)[...]

    def far_shard(f):
        send(mine, shards.at[1, f * cfg.pad : (f + 1) * cfg.pad], s_wf, r_wf, at_z(4 * f))

    for f in range(1, F):
        if 4 * f != Z // 2:
            far_shard(f)
    near = (1, -1, 2)
    for a in near:
        send(mine, shards.at[a + 1, 0 : cfg.pad], s_wn, r_wn.at[a + 1], at_z(a))

    to_new = (z_of * G + g_of) * cap + k_of
    drain(r_a1, in1.at[0 : (G - 1) * cfg.grow])
    out2[...] = dot(onehot(row == to_new), in1[...]).astype(BF)
    here = moved.at[y]
    position = [0] + [2 * o - 1 if o <= Z // 2 else 2 * (Z - o) for o in range(1, Z)]
    parcels = 4
    each = R // parcels
    per = each // cfg.zrow
    pl.semaphore_wait(relay, 2)
    for o in sorted(range(1, Z), key=lambda o: position[Z - o]):
        p = position[Z - o]
        send(
            rows_of(out2, mod(z + o, Z) * cfg.zrow, cfg.zrow), here.at[p * cfg.zrow : (p + 1) * cfg.zrow],
            s_a2, r_a2.at[p // per], at_z(o),
        )
    far_shard(F // 2)
    here[0 : cfg.zrow, :] = rows_of(out2, z * cfg.zrow, cfg.zrow)[...]

    q = iota((1, F * cfg.pad), 1)
    j = lax.rem(q, cfg.pad)
    squeeze = onehot(
        iota((cfg.comb, F * cfg.pad), 0) == jnp.where(j < cfg.own, lax.div(q, cfg.pad) * cfg.own + j, -1)
    )

    def spread(n):
        w_own[n, 0] = dot(squeeze, shards[n]).astype(BF)
        for k in (2, 1, 3):
            send(w_own.at[n, 0], w_own.at[n, k], s_wx, r_wx.at[n], at_x(k))
        send(w_own.at[n, 0], w_sib.at[n, 0], s_sib.at[0], r_sib.at[0], sibling)

    def hand_on(n):
        drain(r_wx.at[n], w_own.at[n, 1:X])
        send(w_own.at[n, 1:X], w_sib.at[n, 1:X], s_sib.at[1], r_sib.at[1], sibling)

    drain(r_wf, shards.at[1, cfg.pad :])
    for a in near:
        send(shards.at[1, cfg.pad :], shards.at[a + 1, cfg.pad :], s_wn, r_wn.at[a + 1], at_z(a))
    spread(1)

    where = lax.div(place, cfg.zrow)
    away = jnp.where(lax.rem(where, 2) == 1, lax.div(where + 1, 2), lax.rem(Z - lax.div(where, 2), Z))
    k_at, g_at = lax.rem(place, cap), lax.rem(lax.div(place, cap), G)
    natural = (
        (lax.div(g_at, CORES) * Z + lax.rem(z + away, Z)) * CORES + lax.rem(g_at, CORES)
    ) * cap + k_at
    back = onehot(row == natural)
    cot[...] = contract_rows(back, cotangent[...]).astype(BF)

    def share(j):
        drain(r_a2.at[j], here.at[(0 if j else cfg.zrow) : each])
        ref = here.at[j * each : (j + 1) * each]
        for d in (2, 1, 3):
            send(ref, ref, s_ag, r_ag.at[j], at_y(d))

    def normalize(j):
        drain(r_ag.at[j], moved.at[0, 0 : (Y - 1) * each])
        lines = 32
        for i in range(each // lines):
            span = slice(j * each + i * lines, j * each + (i + 1) * lines)
            parts = [moved[c, span, :].astype(F32) for c in range(Y)]
            mean = sum(jnp.sum(p, axis=1, keepdims=True) for p in parts) / cfg.width
            parts = [p - mean for p in parts]
            var = sum(jnp.sum(jnp.square(p), axis=1, keepdims=True) for p in parts) / cfg.width
            scale = lax.rsqrt(var + 1e-05)
            for c in range(Y):
                normed[span, c * cfg.part : (c + 1) * cfg.part] = (parts[c] * scale).astype(BF)

    share(0)
    for a in near:
        drain(r_wn.at[a + 1], shards.at[a + 1])
        spread(a + 1)
    share(1)
    hand_on(1)
    share(2)
    for a in near:
        hand_on(a + 1)
    normalize(0)
    share(3)
    normalize(1)

    q = iota((1, 2 * 4 * cfg.comb), 1)
    side = lax.div(q, 4 * cfg.comb)
    n_of = lax.rem(lax.div(q, cfg.comb), 4)
    f_of = lax.rem(lax.div(q, cfg.own), F)
    z_of = lax.rem(z - (n_of - 1) - 4 * f_of + 2 * Z, Z)
    core_of = core + side - 2 * core * side
    natural = (z_of * CORES + core_of) * cfg.own + lax.rem(q, cfg.own)
    span = Z * cfg.pair
    spot = onehot(iota((span, span), 0) == natural)
    drain(r_sib.at[0], w_sib.at[:, 0])
    drain(r_sib.at[1], w_sib.at[:, 1:X])
    for k in range(X):
        pieces = [w[n, k] for w in (w_own, w_sib) for n in range(4)]
        rows_of(weights, mod(x - k, X) * span, span)[...] = dot(
            spot, jnp.concatenate(pieces, axis=0)
        ).astype(BF)

    dglu = dot(cot[...], weights[:, 2 * U : 3 * U])
    normalize(2)
    normalize(3)

    both = dot(normed[...], weights[:, : 2 * U])
    value, gate = both[:, :U], both[:, U : 2 * U]
    sig = jax.nn.sigmoid(gate)
    glu = (value * sig).astype(BF)
    d_value = (dglu * sig).astype(BF)
    d_gate = (dglu * value * sig * (1.0 - sig)).astype(BF)

    d_both = jnp.concatenate([d_value, d_gate], axis=1)
    J = Z // 2 // 4
    steps = (2, 1, -1, 0)
    Q = cfg.pair

    def chunk(o, half, a):
        r = lax.rem(z + a + Z, 4)
        return jnp.concatenate(
            [rows_of(block.at[o], (half * (Z // 2) + r + 4 * j) * Q, Q, 8)[...] for j in range(J)], axis=0
        )

    for o in (2, 1, 3, 0):
        cols = pl.ds(pl.multiple_of(mod(x + o, X) * span, 128), span)
        block[o] = jnp.concatenate(
            [contract_rows(normed[:, cols], d_both), contract_rows(cot[:, cols], glu)], axis=1
        )
        for i, a in enumerate(steps):
            pair_out[o, i] = chunk(o, other, a).astype(BF)
        send(pair_out.at[o], pair_in.at[o], s_pair, r_pair.at[o], sibling)

    glu_rows[...] = dot(back, glu).astype(BF)
    B = cfg.yrow
    for d in (2, 1, 3):
        mine_y = rows_of(glu_rows, mod(y + d, Y) * B, B)
        y_out[d - 1] = contract_cols(mine_y[...], weights[:, 2 * U : 3 * U]).astype(BF)
        send(y_out.at[d - 1], y_in.at[d - 1], s_y, r_y, at_y(d))
    y_own[...] = contract_cols(rows_of(glu_rows, y * B, B)[...], weights[:, 2 * U : 3 * U])

    for o in (2, 1, 3):
        drain(r_pair.at[o], pair_in.at[o])
    for i, a in enumerate(steps):
        for o in (2, 1, 3):
            x_out[i, o - 1] = (chunk(o, core, a) + pair_in[o, i].astype(F32)).astype(BF)
            send(x_out.at[i, o - 1], x_in.at[i, o - 1], s_x, r_x.at[i], at_x(o))
    drain(r_pair.at[0], pair_in.at[0])

    def summed(i, a):
        drain(r_x.at[i], x_in.at[i])
        total = chunk(0, core, a) + pair_in[0, i].astype(F32)
        for k in range(X - 1):
            total = total + x_in[i, k].astype(F32)
        return total

    def to_near(i):
        near_out[i] = summed(i, steps[i]).astype(BF)
        send(near_out.at[i], near_in.at[i], s_near, r_near, at_z(steps[i]))

    to_near(0)

    drain(r_y, y_in)
    rows_of(result, y * B, B)[...] = (
        y_own[...] + y_in[0].astype(F32) + y_in[1].astype(F32) + y_in[2].astype(F32)
    ).astype(BF)
    for d in (2, 1, 3):
        send(rows_of(result, y * B, B), rows_of(result, y * B, B), s_yg, r_yg, at_y(d))

    to_near(1)
    to_near(2)
    total = summed(3, 0)
    drain(r_near, near_in)
    for i in range(3):
        total = total + near_in[i].astype(F32)

    far_out[...] = jnp.zeros_like(far_out)
    sends = []
    for j in range(J):
        part = total[j * Q : (j + 1) * Q]
        acc[j] = part
        far_out[j, 0:Q, :] = part.astype(BF)
        t = core * (Z // 2) + 4 * j + lax.rem(z, 4)
        slot = lax.div(mod(z - t, Z), 4)
        copy = pltpu.make_async_remote_copy(
            src_ref=far_out.at[j], dst_ref=far_in.at[slot], send_sem=s_far.at[j], recv_sem=r_far,
            device_id=at(x, t, core), device_id_type=pl.DeviceIdType.MESH,
        )
        sends.append((t != z, copy))
        pl.when(t != z)(copy.start)

    is_owner = lax.div(z, Z // 2) == core
    hand = pltpu.make_async_remote_copy(
        src_ref=final, dst_ref=final, send_sem=s_fin, recv_sem=r_fin,
        device_id=sibling, device_id_type=pl.DeviceIdType.MESH,
    )

    @pl.when(is_owner)
    def _():
        whole = acc[lax.rem(lax.div(z, 4), J)]
        drain(r_far, far_in.at[1:F])
        for slot in range(1, F):
            whole = whole + far_in[slot, 0:Q, :].astype(F32)
        final[...] = whole
        hand.start()
        hand.wait_send()

    @pl.when(jnp.logical_not(is_owner))
    def _():
        hand.wait_recv()

    whole = final[...]
    owned[...] = jnp.where(core == 0, whole[0 : cfg.own], whole[cfg.own : 2 * cfg.own])

    drain(r_yg, result.at[0 : (Y - 1) * B])
    branch[...] = result[...]

    drain(s_a1, out1.at[0 : (G - 1) * cfg.grow])
    drain(s_a2, out2.at[0 : (Z - 1) * cfg.zrow])
    drain(s_ag, moved.at[0 : Y - 1])
    drain(s_wf, shards.at[1, cfg.pad :])
    drain(s_wn, shards.at[0:3])
    drain(s_wx, w_own.at[:, 1:X])
    drain(s_sib.at[0], w_sib.at[:, 0])
    drain(s_sib.at[1], w_sib.at[:, 1:X])
    drain(s_pair, pair_out)
    drain(s_x, x_out)
    drain(s_near, near_out)
    drain(s_y, y_out)
    drain(s_yg, result.at[0 : (Y - 1) * B])
    for needed, copy in sends:
        pl.when(needed)(copy.wait_send)


def place_results(units, branch_in, owned_in, branch, grad_value, grad_gate, grad_down):
    branch[...] = branch_in[...]
    grad_value[...] = owned_in[:, :units]
    grad_gate[...] = owned_in[:, units : 2 * units]
    grad_down[...] = owned_in[:, 2 * units :]


def module(cfg, frames, lengths, send_order, value_weight, gate_weight, down_weight, cotangent):
    X, Z, Y, G, R, D, U = cfg.X, cfg.Z, cfg.Y, cfg.G, cfg.rows, cfg.width, cfg.units
    C, S, B = cfg.cols, cfg.half, cfg.yrow
    vmem = pl.BlockSpec(memory_space=pltpu.VMEM)
    sem = pltpu.SemaphoreType.DMA
    F, J, H = cfg.far, Z // 8, Z // 8 * cfg.pair
    buffers = [
        ((R, cfg.part), BF),
        ((R, cfg.part), BF),
        ((R, cfg.part), BF),
        ((Y, R, cfg.part), BF),
        ((R, D), BF),
        ((R, D), BF),
        ((R, U), BF),
        ((4, F * cfg.pad, C), BF),
        ((4, X, cfg.comb, C), BF),
        ((4, X, cfg.comb, C), BF),
        ((D, C), BF),
        ((X, Z * cfg.pair, C), F32),
        ((X, 4, H, C), BF),
        ((X, 4, H, C), BF),
        ((4, X - 1, H, C), BF),
        ((4, X - 1, H, C), BF),
        ((3, H, C), BF),
        ((3, H, C), BF),
        ((J, cfg.pair, C), F32),
        ((J, cfg.pairpad, C), BF),
        ((F, cfg.pairpad, C), BF),
        ((cfg.pair, C), F32),
        ((B, D), F32),
        ((Y - 1, B, D), BF),
        ((Y - 1, B, D), BF),
        ((R, D), BF),
    ]
    one = ()
    sems = [
        one, one, one, (4,), one, (4,),
        one, one, one, (4,), one, (4,), (2,), (2,),
        one, (X,), one, (4,), one, one, (J,), one, one, one,
        one, one, one, one,
    ]
    branch, owned = pl.pallas_call(
        functools.partial(kernel, cfg),
        out_shape=(jax.ShapeDtypeStruct((R, D), BF), jax.ShapeDtypeStruct((cfg.own, C), F32)),
        in_specs=[pl.BlockSpec(memory_space=pltpu.SMEM)] + [vmem] * 6,
        out_specs=(vmem,) * 2,
        scratch_shapes=[pltpu.VMEM(shape, kind) for shape, kind in buffers]
        + [sem(n) for n in sems]
        + [pltpu.SemaphoreType.REGULAR],
        compiler_params=pltpu.CompilerParams(
            collective_id=0, has_side_effects=True, vmem_limit_bytes=56 * 1024 * 1024
        ),
    )(lengths, send_order, frames, value_weight, gate_weight, down_weight, cotangent)
    return pl.pallas_call(
        functools.partial(place_results, U),
        out_shape=(jax.ShapeDtypeStruct((R, D), BF),) + (jax.ShapeDtypeStruct((cfg.own, U), F32),) * 3,
        in_specs=[vmem] * 2,
        out_specs=(vmem,) * 4,
    )(branch, owned)


def build(mesh, X, Z):
    def shards(frames, lengths, send_order, value_weight, gate_weight, down_weight, cotangent):
        cfg = Sizes(
            X, Z, mesh.shape["mp"], frames.shape[0], frames.shape[1],
            value_weight.shape[0], value_weight.shape[1],
        )
        return module(
            cfg, frames, lengths, send_order, value_weight, gate_weight, down_weight, cotangent
        )

    return jax.shard_map(
        shards,
        mesh=mesh,
        in_specs=(
            P("dp", None),
            P("dp"),
            P("dp", None),
            P("dp", "mp"),
            P("dp", "mp"),
            P("dp", "mp"),
            P("dp", None),
        ),
        out_specs=(P("dp", None), P("dp", "mp"), P("dp", "mp"), P("dp", "mp")),
        check_vma=False,
    )


def solution(mesh):
    return build(mesh, 4, 16)
```

```python
import functools

import jax
import jax.numpy as jnp
from jax import lax
from jax.experimental import pallas as pl
from jax.experimental.pallas import tpu as pltpu
from jax.sharding import PartitionSpec as P

CORES = 2
BF = jnp.bfloat16
F32 = jnp.float32


def ceil16(rows):
    return -(-rows // 16) * 16


def iota(shape, axis):
    return lax.broadcasted_iota(jnp.int32, shape, axis)


def onehot(hit):
    return jnp.where(hit, 1.0, 0.0).astype(BF)


def dot(left, right):
    return jnp.dot(left, right, preferred_element_type=F32)


def contract_rows(left, right):
    return lax.dot_general(left, right, (((0,), (0,)), ((), ())), preferred_element_type=F32)


def contract_cols(left, right):
    return lax.dot_general(left, right, (((1,), (1,)), ((), ())), preferred_element_type=F32)


def mod(value, count):
    return lax.rem(value + count, count)


class Sizes:
    def __init__(self, X, Z, Y, rows, width, own, units):
        self.X, self.Z, self.Y = X, Z, Y
        self.G = X * CORES
        self.rows, self.width, self.own, self.units = rows, width, own, units
        self.cap = rows // (X * Z * CORES)
        self.part = width // Y
        self.pad = ceil16(own)
        self.zrow = self.G * self.cap
        self.grow = self.Z * self.cap
        self.far = Z // 4
        self.comb = 4 * own
        self.pair = CORES * own
        self.pairpad = ceil16(self.pair)
        self.cols = 3 * units
        self.half = Z // 2 * self.pair
        self.yrow = rows // Y


def kernel(
    cfg,
    lengths, send_order, frames, value_w, gate_w, down_w, cotangent,
    branch, owned,
    out1, in1, out2, moved, normed, cot, glu_rows,
    shards, w_own, w_sib, weights,
    block, pair_out, pair_in, x_out, x_in, near_out, near_in, acc, far_out, far_in, final,
    y_own, y_out, y_in, result,
    s_a1, r_a1, s_a2, r_a2, s_ag, r_ag,
    s_wf, r_wf, s_wn, r_wn, s_wx, r_wx, s_sib, r_sib,
    s_pair, r_pair, s_x, r_x, s_near, r_near, s_far, r_far, s_fin, r_fin, s_y, r_y, s_yg, r_yg,
    relay,
):
    X, Z, Y, G = cfg.X, cfg.Z, cfg.Y, cfg.G
    R, U, F, cap = cfg.rows, cfg.units, cfg.far, cfg.cap
    dp = lax.axis_index("dp")
    y = lax.axis_index("mp")
    core = lax.rem(dp, CORES)
    z = lax.rem(lax.div(dp, CORES), Z)
    x = lax.div(dp, CORES * Z)
    g = x * CORES + core
    other = 1 - core
    sibling = {"dp": dp + 1 - 2 * core, "mp": y}

    def at(x_, z_, core_):
        return {"dp": (x_ * Z + z_) * CORES + core_, "mp": y}

    def at_x(o):
        return at(mod(x + o, X), z, core)

    def at_z(o):
        return at(x, mod(z + o, Z), core)

    def at_y(o):
        return {"dp": dp, "mp": mod(y + o, Y)}

    def at_g(t):
        return at(lax.div(t, CORES), z, lax.rem(t, CORES))

    def send(src, dst, sent, arrived, where):
        copy = pltpu.make_async_remote_copy(
            src_ref=src, dst_ref=dst, send_sem=sent, recv_sem=arrived,
            device_id=where, device_id_type=pl.DeviceIdType.MESH,
        )
        copy.start()

    def drain(sem, ref):
        pltpu.make_async_copy(ref, ref, sem).wait()

    def rows_of(ref, start, size, step=16):
        return ref.at[pl.ds(pl.multiple_of(start, step), size)]

    barrier = pltpu.get_barrier_semaphore()
    partners = [at_g(mod(g + o, G)) for o in range(1, G)]
    partners += [at_z(o * s) for o in range(1, 5) for s in (1, -1)]
    partners += [at_y(o) for o in range(1, Y)]
    for who in partners:
        pl.semaphore_signal(barrier, inc=1, device_id=who, device_id_type=pl.DeviceIdType.MESH)

    packed = jnp.concatenate([value_w[...], gate_w[...], down_w[...]], axis=1)
    mine = shards.at[0, cfg.pad : 2 * cfg.pad]
    mine[...] = jnp.zeros_like(mine)
    shards[0, cfg.pad : cfg.pad + cfg.own, :] = packed

    row, place = iota((R, R), 0), iota((1, R), 1)
    k_of, z_of, g_of = lax.rem(place, cap), lax.rem(lax.div(place, cap), Z), lax.div(place, cap * Z)
    natural = ((lax.div(g_of, CORES) * Z + z_of) * CORES + lax.rem(g_of, CORES)) * cap + k_of
    numbers = jnp.broadcast_to(send_order[...].astype(F32).astype(BF), (16, R))
    order = dot(numbers, onehot(row == natural))[0:1, :]
    pick = onehot((row.astype(F32) == order) & (row < lengths[0]))
    columns = pl.ds(pl.multiple_of(y * cfg.part, 128), cfg.part)
    out1[...] = contract_rows(pick, frames[:, columns]).astype(BF)

    pl.semaphore_wait(barrier, len(partners))
    for o in (4, -4):
        pl.semaphore_signal(relay, inc=1, device_id=at_z(o), device_id_type=pl.DeviceIdType.MESH)

    for o in range(1, G):
        t = mod(g + o, G)
        send(
            rows_of(out1, t * cfg.grow, cfg.grow), rows_of(in1, g * cfg.grow, cfg.grow),
            s_a1, r_a1, at_g(t),
        )
    rows_of(in1, g * cfg.grow, cfg.grow)[...] = rows_of(out1, g * cfg.grow, cfg.grow)[...]

    near = (1, -1, 2)

    def pass_near(f):
        ref = shards.at[f, cfg.pad : 2 * cfg.pad]
        for a in near:
            lo = (a + 1) * cfg.pad
            send(ref, shards.at[f, lo : lo + cfg.pad], s_wn, r_wn.at[f], at_z(a))

    def pass_far(f):
        send(mine, shards.at[f, cfg.pad : 2 * cfg.pad], s_wf, r_wf.at[f], at_z(4 * f))

    pass_near(0)
    for f in range(1, F):
        if 4 * f != Z // 2:
            pass_far(f)
    pl.semaphore_wait(relay, 2)
    pass_far(F // 2)

    to_new = (z_of * G + g_of) * cap + k_of
    drain(r_a1, in1.at[0 : (G - 1) * cfg.grow])
    out2[...] = dot(onehot(row == to_new), in1[...]).astype(BF)
    here = moved.at[y]
    position = [0] + [2 * o - 1 if o <= Z // 2 else 2 * (Z - o) for o in range(1, Z)]
    parcels = 4
    each = R // parcels
    per = each // cfg.zrow
    def to_z(parcel_range):
        for o in sorted(range(1, Z), key=lambda o: position[Z - o]):
            p = position[Z - o]
            if p // per in parcel_range:
                send(
                    rows_of(out2, mod(z + o, Z) * cfg.zrow, cfg.zrow),
                    here.at[p * cfg.zrow : (p + 1) * cfg.zrow],
                    s_a2, r_a2.at[p // per], at_z(o),
                )

    to_z((0, 1))
    here[0 : cfg.zrow, :] = rows_of(out2, z * cfg.zrow, cfg.zrow)[...]

    q = iota((1, 4 * cfg.pad), 1)
    j = lax.rem(q, cfg.pad)
    squeeze = onehot(
        iota((cfg.comb, 4 * cfg.pad), 0) == jnp.where(j < cfg.own, lax.div(q, cfg.pad) * cfg.own + j, -1)
    )

    def spread(f):
        drain(r_wn.at[f], shards.at[f, 0 : 3 * cfg.pad])
        w_own[f, 0] = dot(squeeze, shards[f]).astype(BF)
        for k in (2, 1, 3):
            send(w_own.at[f, 0], w_own.at[f, k], s_wx, r_wx.at[f], at_x(k))

    def hand_on(f):
        drain(r_wx.at[f], w_own.at[f, 1:X])
        send(w_own.at[f], w_sib.at[f], s_sib, r_sib, sibling)

    spread(0)
    for f in (1, 3, 2):
        if f < F:
            drain(r_wf.at[f], shards.at[f, cfg.pad : 2 * cfg.pad])
            pass_near(f)
    to_z((2, 3))

    where = lax.div(place, cfg.zrow)
    away = jnp.where(lax.rem(where, 2) == 1, lax.div(where + 1, 2), lax.rem(Z - lax.div(where, 2), Z))
    k_at, g_at = lax.rem(place, cap), lax.rem(lax.div(place, cap), G)
    natural = (
        (lax.div(g_at, CORES) * Z + lax.rem(z + away, Z)) * CORES + lax.rem(g_at, CORES)
    ) * cap + k_at
    back = onehot(row == natural)
    cot[...] = contract_rows(back, cotangent[...]).astype(BF)

    def share(j):
        drain(r_a2.at[j], here.at[(0 if j else cfg.zrow) : each])
        ref = here.at[j * each : (j + 1) * each]
        for d in (2, 1, 3):
            send(ref, ref, s_ag, r_ag.at[j], at_y(d))

    def normalize(j):
        drain(r_ag.at[j], moved.at[0, 0 : (Y - 1) * each])
        lines = 32
        for i in range(each // lines):
            span = slice(j * each + i * lines, j * each + (i + 1) * lines)
            parts = [moved[c, span, :].astype(F32) for c in range(Y)]
            mean = sum(jnp.sum(p, axis=1, keepdims=True) for p in parts) / cfg.width
            parts = [p - mean for p in parts]
            var = sum(jnp.sum(jnp.square(p), axis=1, keepdims=True) for p in parts) / cfg.width
            scale = lax.rsqrt(var + 1e-05)
            for c in range(Y):
                normed[span, c * cfg.part : (c + 1) * cfg.part] = (parts[c] * scale).astype(BF)

    share(0)
    for f in (1, 3, 2):
        if f < F:
            spread(f)
        if f == 3:
            share(1)
    hand_on(0)
    share(2)
    hand_on(1)
    normalize(0)
    share(3)
    for f in (3, 2):
        if f < F:
            hand_on(f)
    normalize(1)
    normalize(2)

    q = iota((1, 2 * F * cfg.comb), 1)
    side = lax.div(q, F * cfg.comb)
    f_of = lax.rem(lax.div(q, cfg.comb), F)
    n_of = lax.rem(lax.div(q, cfg.own), 4)
    z_of = lax.rem(z - (n_of - 1) - 4 * f_of + 2 * Z, Z)
    core_of = core + side - 2 * core * side
    natural = (z_of * CORES + core_of) * cfg.own + lax.rem(q, cfg.own)
    span = Z * cfg.pair
    spot = onehot(iota((span, span), 0) == natural)
    drain(r_sib, w_sib)
    for k in range(X):
        pieces = [w[f, k] for w in (w_own, w_sib) for f in range(F)]
        rows_of(weights, mod(x - k, X) * span, span)[...] = dot(
            spot, jnp.concatenate(pieces, axis=0)
        ).astype(BF)

    dglu = dot(cot[...], weights[:, 2 * U : 3 * U])
    normalize(3)

    both = dot(normed[...], weights[:, : 2 * U])
    value, gate = both[:, :U], both[:, U : 2 * U]
    sig = jax.nn.sigmoid(gate)
    glu = (value * sig).astype(BF)
    d_value = (dglu * sig).astype(BF)
    d_gate = (dglu * value * sig * (1.0 - sig)).astype(BF)

    d_both = jnp.concatenate([d_value, d_gate], axis=1)
    J = Z // 2 // 4
    steps = (2, 1, -1, 0)
    Q = cfg.pair

    def chunk(o, half, a):
        r = lax.rem(z + a + Z, 4)
        return jnp.concatenate(
            [rows_of(block.at[o], (half * (Z // 2) + r + 4 * j) * Q, Q, 8)[...] for j in range(J)], axis=0
        )

    for o in (2, 1, 3, 0):
        cols = pl.ds(pl.multiple_of(mod(x + o, X) * span, 128), span)
        block[o] = jnp.concatenate(
            [contract_rows(normed[:, cols], d_both), contract_rows(cot[:, cols], glu)], axis=1
        )
        for i, a in enumerate(steps):
            pair_out[o, i] = chunk(o, other, a).astype(BF)
        send(pair_out.at[o], pair_in.at[o], s_pair, r_pair.at[o], sibling)

    glu_rows[...] = dot(back, glu).astype(BF)
    B = cfg.yrow
    for d in (2, 1, 3):
        mine_y = rows_of(glu_rows, mod(y + d, Y) * B, B)
        y_out[d - 1] = contract_cols(mine_y[...], weights[:, 2 * U : 3 * U]).astype(BF)
        send(y_out.at[d - 1], y_in.at[d - 1], s_y, r_y, at_y(d))
    y_own[...] = contract_cols(rows_of(glu_rows, y * B, B)[...], weights[:, 2 * U : 3 * U])

    for o in (2, 1, 3):
        drain(r_pair.at[o], pair_in.at[o])
    for i, a in enumerate(steps):
        for o in (2, 1, 3):
            x_out[i, o - 1] = (chunk(o, core, a) + pair_in[o, i].astype(F32)).astype(BF)
            send(x_out.at[i, o - 1], x_in.at[i, o - 1], s_x, r_x.at[i], at_x(o))
    drain(r_pair.at[0], pair_in.at[0])

    def summed(i, a):
        drain(r_x.at[i], x_in.at[i])
        total = chunk(0, core, a) + pair_in[0, i].astype(F32)
        for k in range(X - 1):
            total = total + x_in[i, k].astype(F32)
        return total

    def to_near(i):
        near_out[i] = summed(i, steps[i]).astype(BF)
        send(near_out.at[i], near_in.at[i], s_near, r_near, at_z(steps[i]))

    to_near(0)

    drain(r_y, y_in)
    rows_of(result, y * B, B)[...] = (
        y_own[...] + y_in[0].astype(F32) + y_in[1].astype(F32) + y_in[2].astype(F32)
    ).astype(BF)
    for d in (2, 1, 3):
        send(rows_of(result, y * B, B), rows_of(result, y * B, B), s_yg, r_yg, at_y(d))

    to_near(1)
    to_near(2)
    total = summed(3, 0)
    drain(r_near, near_in)
    for i in range(3):
        total = total + near_in[i].astype(F32)

    far_out[...] = jnp.zeros_like(far_out)
    sends = []
    for j in range(J):
        part = total[j * Q : (j + 1) * Q]
        acc[j] = part
        far_out[j, 0:Q, :] = part.astype(BF)
        t = core * (Z // 2) + 4 * j + lax.rem(z, 4)
        slot = lax.div(mod(z - t, Z), 4)
        copy = pltpu.make_async_remote_copy(
            src_ref=far_out.at[j], dst_ref=far_in.at[slot], send_sem=s_far.at[j], recv_sem=r_far,
            device_id=at(x, t, core), device_id_type=pl.DeviceIdType.MESH,
        )
        sends.append((t != z, copy))
        pl.when(t != z)(copy.start)

    is_owner = lax.div(z, Z // 2) == core
    hand = pltpu.make_async_remote_copy(
        src_ref=final, dst_ref=final, send_sem=s_fin, recv_sem=r_fin,
        device_id=sibling, device_id_type=pl.DeviceIdType.MESH,
    )

    @pl.when(is_owner)
    def _():
        whole = acc[lax.rem(lax.div(z, 4), J)]
        drain(r_far, far_in.at[1:F])
        for slot in range(1, F):
            whole = whole + far_in[slot, 0:Q, :].astype(F32)
        final[...] = whole
        hand.start()
        hand.wait_send()

    @pl.when(jnp.logical_not(is_owner))
    def _():
        hand.wait_recv()

    whole = final[...]
    owned[...] = jnp.where(core == 0, whole[0 : cfg.own], whole[cfg.own : 2 * cfg.own])

    drain(r_yg, result.at[0 : (Y - 1) * B])
    branch[...] = result[...]

    drain(s_a1, out1.at[0 : (G - 1) * cfg.grow])
    drain(s_a2, out2.at[0 : (Z - 1) * cfg.zrow])
    drain(s_ag, moved.at[0 : Y - 1])
    drain(s_wf, shards.at[0, 0 : (F - 1) * cfg.pad])
    drain(s_wn, shards.at[:, 0 : 3 * cfg.pad])
    drain(s_wx, w_own.at[:, 1:X])
    drain(s_sib, w_own)
    drain(s_pair, pair_out)
    drain(s_x, x_out)
    drain(s_near, near_out)
    drain(s_y, y_out)
    drain(s_yg, result.at[0 : (Y - 1) * B])
    for needed, copy in sends:
        pl.when(needed)(copy.wait_send)


def place_results(units, branch_in, owned_in, branch, grad_value, grad_gate, grad_down):
    branch[...] = branch_in[...]
    grad_value[...] = owned_in[:, :units]
    grad_gate[...] = owned_in[:, units : 2 * units]
    grad_down[...] = owned_in[:, 2 * units :]


def module(cfg, frames, lengths, send_order, value_weight, gate_weight, down_weight, cotangent):
    X, Z, Y, G, R, D, U = cfg.X, cfg.Z, cfg.Y, cfg.G, cfg.rows, cfg.width, cfg.units
    C, S, B = cfg.cols, cfg.half, cfg.yrow
    vmem = pl.BlockSpec(memory_space=pltpu.VMEM)
    sem = pltpu.SemaphoreType.DMA
    F, J, H = cfg.far, Z // 8, Z // 8 * cfg.pair
    buffers = [
        ((R, cfg.part), BF),
        ((R, cfg.part), BF),
        ((R, cfg.part), BF),
        ((Y, R, cfg.part), BF),
        ((R, D), BF),
        ((R, D), BF),
        ((R, U), BF),
        ((F, 4 * cfg.pad, C), BF),
        ((F, X, cfg.comb, C), BF),
        ((F, X, cfg.comb, C), BF),
        ((D, C), BF),
        ((X, Z * cfg.pair, C), F32),
        ((X, 4, H, C), BF),
        ((X, 4, H, C), BF),
        ((4, X - 1, H, C), BF),
        ((4, X - 1, H, C), BF),
        ((3, H, C), BF),
        ((3, H, C), BF),
        ((J, cfg.pair, C), F32),
        ((J, cfg.pairpad, C), BF),
        ((F, cfg.pairpad, C), BF),
        ((cfg.pair, C), F32),
        ((B, D), F32),
        ((Y - 1, B, D), BF),
        ((Y - 1, B, D), BF),
        ((R, D), BF),
    ]
    one = ()
    sems = [
        one, one, one, (4,), one, (4,),
        one, (F,), one, (F,), one, (F,), one, one,
        one, (X,), one, (4,), one, one, (J,), one, one, one,
        one, one, one, one,
    ]
    branch, owned = pl.pallas_call(
        functools.partial(kernel, cfg),
        out_shape=(jax.ShapeDtypeStruct((R, D), BF), jax.ShapeDtypeStruct((cfg.own, C), F32)),
        in_specs=[pl.BlockSpec(memory_space=pltpu.SMEM)] + [vmem] * 6,
        out_specs=(vmem,) * 2,
        scratch_shapes=[pltpu.VMEM(shape, kind) for shape, kind in buffers]
        + [sem(n) for n in sems]
        + [pltpu.SemaphoreType.REGULAR],
        compiler_params=pltpu.CompilerParams(
            collective_id=0, has_side_effects=True, vmem_limit_bytes=56 * 1024 * 1024
        ),
    )(lengths, send_order, frames, value_weight, gate_weight, down_weight, cotangent)
    return pl.pallas_call(
        functools.partial(place_results, U),
        out_shape=(jax.ShapeDtypeStruct((R, D), BF),) + (jax.ShapeDtypeStruct((cfg.own, U), F32),) * 3,
        in_specs=[vmem] * 2,
        out_specs=(vmem,) * 4,
    )(branch, owned)


def build(mesh, X, Z):
    def shards(frames, lengths, send_order, value_weight, gate_weight, down_weight, cotangent):
        cfg = Sizes(
            X, Z, mesh.shape["mp"], frames.shape[0], frames.shape[1],
            value_weight.shape[0], value_weight.shape[1],
        )
        return module(
            cfg, frames, lengths, send_order, value_weight, gate_weight, down_weight, cotangent
        )

    return jax.shard_map(
        shards,
        mesh=mesh,
        in_specs=(
            P("dp", None),
            P("dp"),
            P("dp", None),
            P("dp", "mp"),
            P("dp", "mp"),
            P("dp", "mp"),
            P("dp", None),
        ),
        out_specs=(P("dp", None), P("dp", "mp"), P("dp", "mp"), P("dp", "mp")),
        check_vma=False,
    )


def solution(mesh):
    return build(mesh, 4, 16)
```

```python
import functools

import jax
import jax.numpy as jnp
from jax import lax
from jax.experimental import pallas as pl
from jax.experimental.pallas import tpu as pltpu
from jax.sharding import PartitionSpec as P

CORES = 2
BF = jnp.bfloat16
F32 = jnp.float32


def ceil16(rows):
    return -(-rows // 16) * 16


def iota(shape, axis):
    return lax.broadcasted_iota(jnp.int32, shape, axis)


def onehot(hit):
    return jnp.where(hit, 1.0, 0.0).astype(BF)


def dot(left, right):
    return jnp.dot(left, right, preferred_element_type=F32)


def contract_rows(left, right):
    return lax.dot_general(left, right, (((0,), (0,)), ((), ())), preferred_element_type=F32)


def contract_cols(left, right):
    return lax.dot_general(left, right, (((1,), (1,)), ((), ())), preferred_element_type=F32)


def mod(value, count):
    return lax.rem(value + count, count)


class Sizes:
    def __init__(self, X, Z, Y, rows, width, own, units):
        self.X, self.Z, self.Y = X, Z, Y
        self.G = X * CORES
        self.rows, self.width, self.own, self.units = rows, width, own, units
        self.cap = rows // (X * Z * CORES)
        self.part = width // Y
        self.pad = ceil16(own)
        self.zrow = self.G * self.cap
        self.grow = self.Z * self.cap
        self.far = Z // 4
        self.comb = 4 * own
        self.pair = CORES * own
        self.cols = 3 * units
        self.half = Z // 2 * self.pair
        self.yrow = rows // Y


def kernel(
    cfg,
    lengths, send_order, frames_all, value_w, gate_w, down_w, cotangent_all,
    branch, owned,
    frames, cotangent, out1, in1, out2, moved, normed, cot, glu_rows,
    shards, w_own, w_sib, weights,
    block, pair_out, pair_in, x_out, x_in, near_out, near_in, acc, far_out, far_in, final,
    y_own, y_out, y_in, result,
    s_a1, r_a1, s_a2, r_a2, s_ag, r_ag,
    s_wf, r_wf, s_wn, r_wn, s_wx, r_wx, s_sib, r_sib,
    s_pair, r_pair, s_x, r_x, s_near, r_near, s_far, r_far, s_fin, r_fin, s_y, r_y, s_yg, r_yg,
    relay, s_in,
):
    X, Z, Y, G = cfg.X, cfg.Z, cfg.Y, cfg.G
    R, U, F, cap = cfg.rows, cfg.units, cfg.far, cfg.cap
    dp = lax.axis_index("dp")
    y = lax.axis_index("mp")
    core = lax.rem(dp, CORES)
    z = lax.rem(lax.div(dp, CORES), Z)
    x = lax.div(dp, CORES * Z)
    g = x * CORES + core
    other = 1 - core
    sibling = {"dp": dp + 1 - 2 * core, "mp": y}

    def at(x_, z_, core_):
        return {"dp": (x_ * Z + z_) * CORES + core_, "mp": y}

    def at_x(o):
        return at(mod(x + o, X), z, core)

    def at_z(o):
        return at(x, mod(z + o, Z), core)

    def at_y(o):
        return {"dp": dp, "mp": mod(y + o, Y)}

    def at_g(t):
        return at(lax.div(t, CORES), z, lax.rem(t, CORES))

    def send(src, dst, sent, arrived, where):
        copy = pltpu.make_async_remote_copy(
            src_ref=src, dst_ref=dst, send_sem=sent, recv_sem=arrived,
            device_id=where, device_id_type=pl.DeviceIdType.MESH,
        )
        copy.start()

    def drain(sem, ref):
        pltpu.make_async_copy(ref, ref, sem).wait()

    def rows_of(ref, start, size, step=16):
        return ref.at[pl.ds(pl.multiple_of(start, step), size)]

    barrier = pltpu.get_barrier_semaphore()
    partners = [at_g(mod(g + o, G)) for o in range(1, G)]
    partners += [at_z(o * s) for o in range(1, 5) for s in (1, -1)]
    partners += [at_y(o) for o in range(1, Y)]
    for who in partners:
        pl.semaphore_signal(barrier, inc=1, device_id=who, device_id_type=pl.DeviceIdType.MESH)

    columns = pl.ds(pl.multiple_of(y * cfg.part, 128), cfg.part)
    get_frames = pltpu.make_async_copy(frames_all.at[:, columns], frames, s_in.at[0])
    get_frames.start()
    get_cotangent = pltpu.make_async_copy(cotangent_all, cotangent, s_in.at[1])
    get_cotangent.start()

    packed = jnp.concatenate([value_w[...], gate_w[...], down_w[...]], axis=1)
    mine = shards.at[0, cfg.pad : 2 * cfg.pad]
    mine[...] = jnp.zeros_like(mine)
    shards[0, cfg.pad : cfg.pad + cfg.own, :] = packed

    row, place = iota((R, R), 0), iota((1, R), 1)
    k_of, z_of, g_of = lax.rem(place, cap), lax.rem(lax.div(place, cap), Z), lax.div(place, cap * Z)
    natural = ((lax.div(g_of, CORES) * Z + z_of) * CORES + lax.rem(g_of, CORES)) * cap + k_of
    numbers = jnp.broadcast_to(send_order[...].astype(F32).astype(BF), (16, R))
    order = dot(numbers, onehot(row == natural))[0:1, :]
    pick = onehot((row.astype(F32) == order) & (row < lengths[0]))
    get_frames.wait()
    out1[...] = contract_rows(pick, frames[...]).astype(BF)

    pl.semaphore_wait(barrier, len(partners))
    for o in (4, -4):
        pl.semaphore_signal(relay, inc=1, device_id=at_z(o), device_id_type=pl.DeviceIdType.MESH)

    for o in range(1, G):
        t = mod(g + o, G)
        send(
            rows_of(out1, t * cfg.grow, cfg.grow), rows_of(in1, g * cfg.grow, cfg.grow),
            s_a1, r_a1, at_g(t),
        )
    rows_of(in1, g * cfg.grow, cfg.grow)[...] = rows_of(out1, g * cfg.grow, cfg.grow)[...]

    near = (1, -1, 2)

    def pass_near(f):
        ref = shards.at[f, cfg.pad : 2 * cfg.pad]
        for a in near:
            lo = (a + 1) * cfg.pad
            send(ref, shards.at[f, lo : lo + cfg.pad], s_wn, r_wn.at[f], at_z(a))

    def pass_far(f):
        send(mine, shards.at[f, cfg.pad : 2 * cfg.pad], s_wf, r_wf.at[f], at_z(4 * f))

    pass_near(0)
    for f in range(1, F):
        if 4 * f != Z // 2:
            pass_far(f)
    pl.semaphore_wait(relay, 2)
    pass_far(F // 2)

    to_new = (z_of * G + g_of) * cap + k_of
    drain(r_a1, in1.at[0 : (G - 1) * cfg.grow])
    out2[...] = dot(onehot(row == to_new), in1[...]).astype(BF)
    here = moved.at[y]
    position = [0] + [2 * o - 1 if o <= Z // 2 else 2 * (Z - o) for o in range(1, Z)]
    parcels = 4
    each = R // parcels
    per = each // cfg.zrow
    def to_z(parcel_range):
        for o in sorted(range(1, Z), key=lambda o: position[Z - o]):
            p = position[Z - o]
            if p // per in parcel_range:
                send(
                    rows_of(out2, mod(z + o, Z) * cfg.zrow, cfg.zrow),
                    here.at[p * cfg.zrow : (p + 1) * cfg.zrow],
                    s_a2, r_a2.at[p // per], at_z(o),
                )

    to_z((0, 1))
    here[0 : cfg.zrow, :] = rows_of(out2, z * cfg.zrow, cfg.zrow)[...]

    q = iota((1, 4 * cfg.pad), 1)
    j = lax.rem(q, cfg.pad)
    squeeze = onehot(
        iota((cfg.comb, 4 * cfg.pad), 0) == jnp.where(j < cfg.own, lax.div(q, cfg.pad) * cfg.own + j, -1)
    )

    def spread(f):
        drain(r_wn.at[f], shards.at[f, 0 : 3 * cfg.pad])
        w_own[f, 0] = dot(squeeze, shards[f]).astype(BF)
        for k in (2, 1, 3):
            send(w_own.at[f, 0], w_own.at[f, k], s_wx, r_wx.at[f], at_x(k))

    def hand_on(f):
        drain(r_wx.at[f], w_own.at[f, 1:X])
        send(w_own.at[f], w_sib.at[f], s_sib, r_sib, sibling)

    spread(0)
    for f in (1, 3, 2):
        if f < F:
            drain(r_wf.at[f], shards.at[f, cfg.pad : 2 * cfg.pad])
            pass_near(f)
    to_z((2, 3))

    where = lax.div(place, cfg.zrow)
    away = jnp.where(lax.rem(where, 2) == 1, lax.div(where + 1, 2), lax.rem(Z - lax.div(where, 2), Z))
    k_at, g_at = lax.rem(place, cap), lax.rem(lax.div(place, cap), G)
    natural = (
        (lax.div(g_at, CORES) * Z + lax.rem(z + away, Z)) * CORES + lax.rem(g_at, CORES)
    ) * cap + k_at
    back = onehot(row == natural)
    get_cotangent.wait()
    cot[...] = contract_rows(back, cotangent[...]).astype(BF)

    def share(j):
        drain(r_a2.at[j], here.at[(0 if j else cfg.zrow) : each])
        ref = here.at[j * each : (j + 1) * each]
        for d in (2, 1, 3):
            send(ref, ref, s_ag, r_ag.at[j], at_y(d))

    def normalize(j):
        drain(r_ag.at[j], moved.at[0, 0 : (Y - 1) * each])
        lines = 32
        for i in range(each // lines):
            span = slice(j * each + i * lines, j * each + (i + 1) * lines)
            parts = [moved[c, span, :].astype(F32) for c in range(Y)]
            mean = sum(jnp.sum(p, axis=1, keepdims=True) for p in parts) / cfg.width
            parts = [p - mean for p in parts]
            var = sum(jnp.sum(jnp.square(p), axis=1, keepdims=True) for p in parts) / cfg.width
            scale = lax.rsqrt(var + 1e-05)
            for c in range(Y):
                normed[span, c * cfg.part : (c + 1) * cfg.part] = (parts[c] * scale).astype(BF)

    share(0)
    for f in (1, 3, 2):
        if f < F:
            spread(f)
        if f == 3:
            share(1)
    hand_on(0)
    share(2)
    hand_on(1)
    normalize(0)
    share(3)
    for f in (3, 2):
        if f < F:
            hand_on(f)
    normalize(1)
    normalize(2)

    q = iota((1, 2 * F * cfg.comb), 1)
    side = lax.div(q, F * cfg.comb)
    f_of = lax.rem(lax.div(q, cfg.comb), F)
    n_of = lax.rem(lax.div(q, cfg.own), 4)
    z_of = lax.rem(z - (n_of - 1) - 4 * f_of + 2 * Z, Z)
    core_of = core + side - 2 * core * side
    natural = (z_of * CORES + core_of) * cfg.own + lax.rem(q, cfg.own)
    span = Z * cfg.pair
    spot = onehot(iota((span, span), 0) == natural)
    drain(r_sib, w_sib)
    for k in range(X):
        pieces = [w[f, k] for w in (w_own, w_sib) for f in range(F)]
        rows_of(weights, mod(x - k, X) * span, span)[...] = dot(
            spot, jnp.concatenate(pieces, axis=0)
        ).astype(BF)

    dglu = dot(cot[...], weights[:, 2 * U : 3 * U])
    normalize(3)

    both = dot(normed[...], weights[:, : 2 * U])
    value, gate = both[:, :U], both[:, U : 2 * U]
    sig = jax.nn.sigmoid(gate)
    glu = (value * sig).astype(BF)
    d_value = (dglu * sig).astype(BF)
    d_gate = (dglu * value * sig * (1.0 - sig)).astype(BF)

    d_both = jnp.concatenate([d_value, d_gate], axis=1)
    J = Z // 2 // 4
    steps = (2, 1, -1, 0)
    Q = cfg.pair

    def chunk(o, half, a):
        r = lax.rem(z + a + Z, 4)
        return jnp.concatenate(
            [rows_of(block.at[o], (half * (Z // 2) + r + 4 * j) * Q, Q, 8)[...] for j in range(J)], axis=0
        )

    for o in (2, 1, 3, 0):
        cols = pl.ds(pl.multiple_of(mod(x + o, X) * span, 128), span)
        block[o] = jnp.concatenate(
            [contract_rows(normed[:, cols], d_both), contract_rows(cot[:, cols], glu)], axis=1
        )
        for i, a in enumerate(steps):
            pair_out[o, i] = chunk(o, other, a).astype(BF)
        send(pair_out.at[o], pair_in.at[o], s_pair, r_pair.at[o], sibling)

    glu_rows[...] = dot(back, glu).astype(BF)
    B = cfg.yrow
    half_b = B // 2
    for d in (2, 1, 3):
        some = rows_of(glu_rows, mod(y + d, Y) * B, B)[...]
        theirs = contract_cols(some, weights[:, 2 * U : 3 * U]).astype(BF)
        for h in range(2):
            y_out[h, d - 1] = theirs[h * half_b : (h + 1) * half_b]
    for h in range(2):
        for d in (2, 1, 3):
            send(y_out.at[h, d - 1], y_in.at[h, d - 1], s_y, r_y.at[h], at_y(d))
    y_own[...] = contract_cols(rows_of(glu_rows, y * B, B)[...], weights[:, 2 * U : 3 * U])

    def gather(h):
        drain(r_y.at[h], y_in.at[h])
        lines = y_own[h * half_b : (h + 1) * half_b, :]
        for k in range(Y - 1):
            lines = lines + y_in[h, k].astype(F32)
        ref = rows_of(result, y * B + h * half_b, half_b)
        ref[...] = lines.astype(BF)
        for d in (2, 1, 3):
            send(ref, ref, s_yg, r_yg, at_y(d))

    for o in (2, 1, 3):
        drain(r_pair.at[o], pair_in.at[o])
    for i, a in enumerate(steps):
        for o in (2, 1, 3):
            x_out[i, o - 1] = (chunk(o, core, a) + pair_in[o, i].astype(F32)).astype(BF)
            send(x_out.at[i, o - 1], x_in.at[i, o - 1], s_x, r_x.at[i], at_x(o))
    drain(r_pair.at[0], pair_in.at[0])

    def summed(i, a):
        drain(r_x.at[i], x_in.at[i])
        total = chunk(0, core, a) + pair_in[0, i].astype(F32)
        for k in range(X - 1):
            total = total + x_in[i, k].astype(F32)
        return total

    def to_near(i):
        near_out[i] = summed(i, steps[i]).astype(BF)
        send(near_out.at[i], near_in.at[i], s_near, r_near, at_z(steps[i]))

    gather(0)
    to_near(0)
    to_near(1)
    gather(1)
    to_near(2)
    total = summed(3, 0)
    drain(r_near, near_in)
    for i in range(3):
        total = total + near_in[i].astype(F32)

    far_out[...] = jnp.zeros_like(far_out)
    sends = []
    O = cfg.own
    for j in range(J):
        t = core * (Z // 2) + 4 * j + lax.rem(z, 4)
        slot = lax.div(mod(z - t, Z), 4)
        for c in range(CORES):
            lines = total[j * Q + c * O : j * Q + (c + 1) * O]
            acc[j, c, 0:O, :] = lines
            far_out[j, c, 0:O, :] = lines.astype(BF)
            copy = pltpu.make_async_remote_copy(
                src_ref=far_out.at[j, c], dst_ref=far_in.at[slot], send_sem=s_far.at[j, c], recv_sem=r_far,
                device_id=at(x, t, c), device_id_type=pl.DeviceIdType.MESH,
            )
            sends.append((t != z, copy))
            pl.when(t != z)(copy.start)

    is_owner = lax.div(z, Z // 2) == core
    own_j = lax.rem(lax.div(z, 4), J)
    hand = pltpu.make_async_remote_copy(
        src_ref=acc.at[own_j, other], dst_ref=final, send_sem=s_fin, recv_sem=r_fin,
        device_id=sibling, device_id_type=pl.DeviceIdType.MESH,
    )

    @pl.when(is_owner)
    def _():
        hand.start()
        final[...] = acc[own_j, core]
        hand.wait_send()

    @pl.when(jnp.logical_not(is_owner))
    def _():
        hand.wait_recv()

    drain(r_far, far_in.at[1:F])
    whole = final[0:O, :]
    for slot in range(1, F):
        whole = whole + far_in[slot, 0:O, :].astype(F32)
    owned[...] = whole

    drain(r_yg, result.at[0 : (Y - 1) * B])
    put = pltpu.make_async_copy(result, branch, s_in.at[0])
    put.start()

    drain(s_a1, out1.at[0 : (G - 1) * cfg.grow])
    drain(s_a2, out2.at[0 : (Z - 1) * cfg.zrow])
    drain(s_ag, moved.at[0 : Y - 1])
    drain(s_wf, shards.at[0, 0 : (F - 1) * cfg.pad])
    drain(s_wn, shards.at[:, 0 : 3 * cfg.pad])
    drain(s_wx, w_own.at[:, 1:X])
    drain(s_sib, w_own)
    drain(s_pair, pair_out)
    drain(s_x, x_out)
    drain(s_near, near_out)
    drain(s_y, y_out)
    drain(s_yg, result.at[0 : (Y - 1) * B])
    for needed, copy in sends:
        pl.when(needed)(copy.wait_send)
    put.wait()


def place_results(units, pieces, branch_in, owned_in, branch, grad_value, grad_gate, grad_down, sems):
    size = branch_in.shape[0] // pieces
    copies = [
        pltpu.make_async_copy(
            branch_in.at[i * size : (i + 1) * size], branch.at[i * size : (i + 1) * size], sems.at[i]
        )
        for i in range(pieces)
    ]
    for copy in copies:
        copy.start()
    grad_value[...] = owned_in[:, :units]
    grad_gate[...] = owned_in[:, units : 2 * units]
    grad_down[...] = owned_in[:, 2 * units :]
    for copy in copies:
        copy.wait()


def module(cfg, frames, lengths, send_order, value_weight, gate_weight, down_weight, cotangent):
    X, Z, Y, G, R, D, U = cfg.X, cfg.Z, cfg.Y, cfg.G, cfg.rows, cfg.width, cfg.units
    C, S, B = cfg.cols, cfg.half, cfg.yrow
    vmem, hbm = pl.BlockSpec(memory_space=pltpu.VMEM), pl.BlockSpec(memory_space=pl.ANY)
    sem = pltpu.SemaphoreType.DMA
    F, J, H = cfg.far, Z // 8, Z // 8 * cfg.pair
    buffers = [
        ((R, cfg.part), BF),
        ((R, D), BF),
        ((R, cfg.part), BF),
        ((R, cfg.part), BF),
        ((R, cfg.part), BF),
        ((Y, R, cfg.part), BF),
        ((R, D), BF),
        ((R, D), BF),
        ((R, U), BF),
        ((F, 4 * cfg.pad, C), BF),
        ((F, X, cfg.comb, C), BF),
        ((F, X, cfg.comb, C), BF),
        ((D, C), BF),
        ((X, Z * cfg.pair, C), F32),
        ((X, 4, H, C), BF),
        ((X, 4, H, C), BF),
        ((4, X - 1, H, C), BF),
        ((4, X - 1, H, C), BF),
        ((3, H, C), BF),
        ((3, H, C), BF),
        ((J, CORES, cfg.pad, C), F32),
        ((J, CORES, cfg.pad, C), BF),
        ((F, cfg.pad, C), BF),
        ((cfg.pad, C), F32),
        ((B, D), F32),
        ((2, Y - 1, B // 2, D), BF),
        ((2, Y - 1, B // 2, D), BF),
        ((R, D), BF),
    ]
    one = ()
    sems = [
        one, one, one, (4,), one, (4,),
        one, (F,), one, (F,), one, (F,), one, one,
        one, (X,), one, (4,), one, one, (J, CORES), one, one, one,
        one, (2,), one, one,
    ]
    branch, owned = pl.pallas_call(
        functools.partial(kernel, cfg),
        out_shape=(jax.ShapeDtypeStruct((R, D), BF), jax.ShapeDtypeStruct((cfg.own, C), F32)),
        in_specs=[pl.BlockSpec(memory_space=pltpu.SMEM), vmem, hbm, vmem, vmem, vmem, hbm],
        out_specs=(hbm, vmem),
        scratch_shapes=[pltpu.VMEM(shape, kind) for shape, kind in buffers]
        + [sem(n) for n in sems]
        + [pltpu.SemaphoreType.REGULAR, sem((2,))],
        compiler_params=pltpu.CompilerParams(
            collective_id=0, has_side_effects=True, vmem_limit_bytes=56 * 1024 * 1024
        ),
    )(lengths, send_order, frames, value_weight, gate_weight, down_weight, cotangent)
    pieces = 8
    return pl.pallas_call(
        functools.partial(place_results, U, pieces),
        out_shape=(jax.ShapeDtypeStruct((R, D), BF),) + (jax.ShapeDtypeStruct((cfg.own, U), F32),) * 3,
        in_specs=[hbm, vmem],
        out_specs=(hbm,) + (vmem,) * 3,
        scratch_shapes=[sem((pieces,))],
    )(branch, owned)


def build(mesh, X, Z):
    def shards(frames, lengths, send_order, value_weight, gate_weight, down_weight, cotangent):
        cfg = Sizes(
            X, Z, mesh.shape["mp"], frames.shape[0], frames.shape[1],
            value_weight.shape[0], value_weight.shape[1],
        )
        return module(
            cfg, frames, lengths, send_order, value_weight, gate_weight, down_weight, cotangent
        )

    return jax.shard_map(
        shards,
        mesh=mesh,
        in_specs=(
            P("dp", None),
            P("dp"),
            P("dp", None),
            P("dp", "mp"),
            P("dp", "mp"),
            P("dp", "mp"),
            P("dp", None),
        ),
        out_specs=(P("dp", None), P("dp", "mp"), P("dp", "mp"), P("dp", "mp")),
        check_vma=False,
    )


def solution(mesh):
    return build(mesh, 4, 16)
```

```python
import functools

import jax
import jax.numpy as jnp
from jax import lax
from jax.experimental import pallas as pl
from jax.experimental.pallas import tpu as pltpu
from jax.sharding import PartitionSpec as P

CORES = 2
BF = jnp.bfloat16
F32 = jnp.float32


def ceil16(rows):
    return -(-rows // 16) * 16


def iota(shape, axis):
    return lax.broadcasted_iota(jnp.int32, shape, axis)


def onehot(hit):
    return jnp.where(hit, 1.0, 0.0).astype(BF)


def dot(left, right):
    return jnp.dot(left, right, preferred_element_type=F32)


def contract_rows(left, right):
    return lax.dot_general(left, right, (((0,), (0,)), ((), ())), preferred_element_type=F32)


def contract_cols(left, right):
    return lax.dot_general(left, right, (((1,), (1,)), ((), ())), preferred_element_type=F32)


def mod(value, count):
    return lax.rem(value + count, count)


class Sizes:
    def __init__(self, X, Z, Y, rows, width, own, units):
        self.X, self.Z, self.Y = X, Z, Y
        self.G = X * CORES
        self.rows, self.width, self.own, self.units = rows, width, own, units
        self.cap = rows // (X * Z * CORES)
        self.part = width // Y
        self.pad = ceil16(own)
        self.zrow = self.G * self.cap
        self.grow = self.Z * self.cap
        self.far = Z // 4
        self.comb = 4 * own
        self.pair = CORES * own
        self.cols = 3 * units
        self.half = Z // 2 * self.pair
        self.yrow = rows // Y


def kernel(
    cfg,
    lengths, send_order, frames_all, value_w, gate_w, down_w, cotangent_all,
    branch, owned,
    frames, cotangent, out1, in1, out2, moved, normed, cot, glu_rows,
    shards, w_own, w_sib, weights,
    block, pair_out, pair_in, x_out, x_in, near_out, near_in, acc, far_out, far_in, final,
    y_own, y_out, y_in, result,
    s_a1, r_a1, s_a2, r_a2, s_ag, r_ag,
    s_wf, r_wf, s_wn, r_wn, s_wx, r_wx, s_sib, r_sib,
    s_pair, r_pair, s_x, r_x, s_near, r_near, s_far, r_far, s_fin, r_fin, s_y, r_y, s_yg, r_yg,
    relay, s_in, s_put,
):
    X, Z, Y, G = cfg.X, cfg.Z, cfg.Y, cfg.G
    R, U, F, cap = cfg.rows, cfg.units, cfg.far, cfg.cap
    dp = lax.axis_index("dp")
    y = lax.axis_index("mp")
    core = lax.rem(dp, CORES)
    z = lax.rem(lax.div(dp, CORES), Z)
    x = lax.div(dp, CORES * Z)
    g = x * CORES + core
    other = 1 - core
    sibling = {"dp": dp + 1 - 2 * core, "mp": y}

    def at(x_, z_, core_):
        return {"dp": (x_ * Z + z_) * CORES + core_, "mp": y}

    def at_x(o):
        return at(mod(x + o, X), z, core)

    def at_z(o):
        return at(x, mod(z + o, Z), core)

    def at_y(o):
        return {"dp": dp, "mp": mod(y + o, Y)}

    def at_g(t):
        return at(lax.div(t, CORES), z, lax.rem(t, CORES))

    def send(src, dst, sent, arrived, where):
        copy = pltpu.make_async_remote_copy(
            src_ref=src, dst_ref=dst, send_sem=sent, recv_sem=arrived,
            device_id=where, device_id_type=pl.DeviceIdType.MESH,
        )
        copy.start()

    def drain(sem, ref):
        pltpu.make_async_copy(ref, ref, sem).wait()

    def rows_of(ref, start, size, step=16):
        return ref.at[pl.ds(pl.multiple_of(start, step), size)]

    barrier = pltpu.get_barrier_semaphore()
    partners = [at_g(mod(g + o, G)) for o in range(1, G)]
    partners += [at_z(o * s) for o in range(1, 5) for s in (1, -1)]
    partners += [at_y(o) for o in range(1, Y)]
    for who in partners:
        pl.semaphore_signal(barrier, inc=1, device_id=who, device_id_type=pl.DeviceIdType.MESH)

    columns = pl.ds(pl.multiple_of(y * cfg.part, 128), cfg.part)
    get_frames = pltpu.make_async_copy(frames_all.at[:, columns], frames, s_in.at[0])
    get_frames.start()
    get_cotangent = pltpu.make_async_copy(cotangent_all, cotangent, s_in.at[1])
    get_cotangent.start()

    packed = jnp.concatenate([value_w[...], gate_w[...], down_w[...]], axis=1)
    mine = shards.at[0, cfg.pad : 2 * cfg.pad]
    mine[...] = jnp.zeros_like(mine)
    shards[0, cfg.pad : cfg.pad + cfg.own, :] = packed

    row, place = iota((R, R), 0), iota((1, R), 1)
    k_of, z_of, g_of = lax.rem(place, cap), lax.rem(lax.div(place, cap), Z), lax.div(place, cap * Z)
    natural = ((lax.div(g_of, CORES) * Z + z_of) * CORES + lax.rem(g_of, CORES)) * cap + k_of
    numbers = jnp.broadcast_to(send_order[...].astype(F32).astype(BF), (16, R))
    order = dot(numbers, onehot(row == natural))[0:1, :]
    pick = onehot((row.astype(F32) == order) & (row < lengths[0]))
    get_frames.wait()
    out1[...] = contract_rows(pick, frames[...]).astype(BF)

    pl.semaphore_wait(barrier, len(partners))
    for o in (4, -4):
        pl.semaphore_signal(relay, inc=1, device_id=at_z(o), device_id_type=pl.DeviceIdType.MESH)

    for o in range(1, G):
        t = mod(g + o, G)
        send(
            rows_of(out1, t * cfg.grow, cfg.grow), rows_of(in1, g * cfg.grow, cfg.grow),
            s_a1, r_a1, at_g(t),
        )
    rows_of(in1, g * cfg.grow, cfg.grow)[...] = rows_of(out1, g * cfg.grow, cfg.grow)[...]

    near = (1, -1, 2)

    def pass_near(f):
        ref = shards.at[f, cfg.pad : 2 * cfg.pad]
        for a in near:
            lo = (a + 1) * cfg.pad
            send(ref, shards.at[f, lo : lo + cfg.pad], s_wn, r_wn.at[f], at_z(a))

    def pass_far(f):
        send(mine, shards.at[f, cfg.pad : 2 * cfg.pad], s_wf, r_wf.at[f], at_z(4 * f))

    pass_near(0)
    for f in range(1, F):
        if 4 * f != Z // 2:
            pass_far(f)
    pl.semaphore_wait(relay, 2)
    pass_far(F // 2)

    to_new = (z_of * G + g_of) * cap + k_of
    drain(r_a1, in1.at[0 : (G - 1) * cfg.grow])
    out2[...] = dot(onehot(row == to_new), in1[...]).astype(BF)
    here = moved.at[y]
    position = [0] + [2 * o - 1 if o <= Z // 2 else 2 * (Z - o) for o in range(1, Z)]
    parcels = 4
    each = R // parcels
    per = each // cfg.zrow
    def to_z(parcel_range):
        for o in sorted(range(1, Z), key=lambda o: position[Z - o]):
            p = position[Z - o]
            if p // per in parcel_range:
                send(
                    rows_of(out2, mod(z + o, Z) * cfg.zrow, cfg.zrow),
                    here.at[p * cfg.zrow : (p + 1) * cfg.zrow],
                    s_a2, r_a2.at[p // per], at_z(o),
                )

    to_z((0, 1))
    here[0 : cfg.zrow, :] = rows_of(out2, z * cfg.zrow, cfg.zrow)[...]

    q = iota((1, 4 * cfg.pad), 1)
    j = lax.rem(q, cfg.pad)
    squeeze = onehot(
        iota((cfg.comb, 4 * cfg.pad), 0) == jnp.where(j < cfg.own, lax.div(q, cfg.pad) * cfg.own + j, -1)
    )

    def spread(f):
        drain(r_wn.at[f], shards.at[f, 0 : 3 * cfg.pad])
        w_own[f, 0] = dot(squeeze, shards[f]).astype(BF)
        for k in (2, 1, 3):
            send(w_own.at[f, 0], w_own.at[f, k], s_wx, r_wx.at[f], at_x(k))

    def hand_on(f):
        drain(r_wx.at[f], w_own.at[f, 1:X])
        send(w_own.at[f], w_sib.at[f], s_sib, r_sib, sibling)

    spread(0)
    for f in (1, 3, 2):
        if f < F:
            drain(r_wf.at[f], shards.at[f, cfg.pad : 2 * cfg.pad])
            pass_near(f)
    to_z((2, 3))

    where = lax.div(place, cfg.zrow)
    away = jnp.where(lax.rem(where, 2) == 1, lax.div(where + 1, 2), lax.rem(Z - lax.div(where, 2), Z))
    k_at, g_at = lax.rem(place, cap), lax.rem(lax.div(place, cap), G)
    natural = (
        (lax.div(g_at, CORES) * Z + lax.rem(z + away, Z)) * CORES + lax.rem(g_at, CORES)
    ) * cap + k_at
    back = onehot(row == natural)
    get_cotangent.wait()
    cot[...] = contract_rows(back, cotangent[...]).astype(BF)

    def share(j):
        drain(r_a2.at[j], here.at[(0 if j else cfg.zrow) : each])
        ref = here.at[j * each : (j + 1) * each]
        for d in (2, 1, 3):
            send(ref, ref, s_ag, r_ag.at[j], at_y(d))

    def normalize(j):
        drain(r_ag.at[j], moved.at[0, 0 : (Y - 1) * each])
        lines = 32
        for i in range(each // lines):
            span = slice(j * each + i * lines, j * each + (i + 1) * lines)
            parts = [moved[c, span, :].astype(F32) for c in range(Y)]
            mean = sum(jnp.sum(p, axis=1, keepdims=True) for p in parts) / cfg.width
            parts = [p - mean for p in parts]
            var = sum(jnp.sum(jnp.square(p), axis=1, keepdims=True) for p in parts) / cfg.width
            scale = lax.rsqrt(var + 1e-05)
            for c in range(Y):
                normed[span, c * cfg.part : (c + 1) * cfg.part] = (parts[c] * scale).astype(BF)

    share(0)
    for f in (1, 3, 2):
        if f < F:
            spread(f)
        if f == 3:
            share(1)
    hand_on(0)
    share(2)
    hand_on(1)
    normalize(0)
    share(3)
    for f in (3, 2):
        if f < F:
            hand_on(f)
    normalize(1)
    normalize(2)

    q = iota((1, 2 * F * cfg.comb), 1)
    side = lax.div(q, F * cfg.comb)
    f_of = lax.rem(lax.div(q, cfg.comb), F)
    n_of = lax.rem(lax.div(q, cfg.own), 4)
    z_of = lax.rem(z - (n_of - 1) - 4 * f_of + 2 * Z, Z)
    core_of = core + side - 2 * core * side
    natural = (z_of * CORES + core_of) * cfg.own + lax.rem(q, cfg.own)
    span = Z * cfg.pair
    spot = onehot(iota((span, span), 0) == natural)
    drain(r_sib, w_sib)
    for k in range(X):
        pieces = [w[f, k] for w in (w_own, w_sib) for f in range(F)]
        rows_of(weights, mod(x - k, X) * span, span)[...] = dot(
            spot, jnp.concatenate(pieces, axis=0)
        ).astype(BF)

    dglu = dot(cot[...], weights[:, 2 * U : 3 * U])
    normalize(3)

    both = dot(normed[...], weights[:, : 2 * U])
    value, gate = both[:, :U], both[:, U : 2 * U]
    sig = jax.nn.sigmoid(gate)
    glu = (value * sig).astype(BF)
    d_value = (dglu * sig).astype(BF)
    d_gate = (dglu * value * sig * (1.0 - sig)).astype(BF)

    d_both = jnp.concatenate([d_value, d_gate], axis=1)
    J = Z // 2 // 4
    steps = (2, 1, -1, 0)
    Q = cfg.pair

    def chunk(o, half, a):
        r = lax.rem(z + a + Z, 4)
        return jnp.concatenate(
            [rows_of(block.at[o], (half * (Z // 2) + r + 4 * j) * Q, Q, 8)[...] for j in range(J)], axis=0
        )

    for o in (2, 1, 3, 0):
        cols = pl.ds(pl.multiple_of(mod(x + o, X) * span, 128), span)
        block[o] = jnp.concatenate(
            [contract_rows(normed[:, cols], d_both), contract_rows(cot[:, cols], glu)], axis=1
        )
        for i, a in enumerate(steps):
            pair_out[o, i] = chunk(o, other, a).astype(BF)
        send(pair_out.at[o], pair_in.at[o], s_pair, r_pair.at[o], sibling)

    glu_rows[...] = dot(back, glu).astype(BF)
    B = cfg.yrow
    half_b = B // 2
    for d in (2, 1, 3):
        some = rows_of(glu_rows, mod(y + d, Y) * B, B)[...]
        theirs = contract_cols(some, weights[:, 2 * U : 3 * U]).astype(BF)
        for h in range(2):
            y_out[h, d - 1] = theirs[h * half_b : (h + 1) * half_b]
    for h in range(2):
        for d in (2, 1, 3):
            send(y_out.at[h, d - 1], y_in.at[h, d - 1], s_y, r_y.at[h], at_y(d))
    y_own[...] = contract_cols(rows_of(glu_rows, y * B, B)[...], weights[:, 2 * U : 3 * U])

    def gather(h):
        drain(r_y.at[h], y_in.at[h])
        lines = y_own[h * half_b : (h + 1) * half_b, :]
        for k in range(Y - 1):
            lines = lines + y_in[h, k].astype(F32)
        ref = rows_of(result, y * B + h * half_b, half_b)
        ref[...] = lines.astype(BF)
        for d in (2, 1, 3):
            send(ref, ref, s_yg, r_yg.at[h], at_y(d))

    def put_out(h):
        drain(r_yg.at[h], result.at[0 : (Y - 1) * half_b])
        for i in range(Y):
            lo = i * B + h * half_b
            pltpu.make_async_copy(
                result.at[lo : lo + half_b], branch.at[lo : lo + half_b], s_put
            ).start()

    for o in (2, 1, 3):
        drain(r_pair.at[o], pair_in.at[o])
    for i, a in enumerate(steps):
        for o in (2, 1, 3):
            x_out[i, o - 1] = (chunk(o, core, a) + pair_in[o, i].astype(F32)).astype(BF)
            send(x_out.at[i, o - 1], x_in.at[i, o - 1], s_x, r_x.at[i], at_x(o))
    drain(r_pair.at[0], pair_in.at[0])

    def summed(i, a):
        drain(r_x.at[i], x_in.at[i])
        total = chunk(0, core, a) + pair_in[0, i].astype(F32)
        for k in range(X - 1):
            total = total + x_in[i, k].astype(F32)
        return total

    def to_near(i):
        near_out[i] = summed(i, steps[i]).astype(BF)
        send(near_out.at[i], near_in.at[i], s_near, r_near, at_z(steps[i]))

    gather(0)
    to_near(0)
    to_near(1)
    gather(1)
    to_near(2)
    total = summed(3, 0)
    drain(r_near, near_in)
    for i in range(3):
        total = total + near_in[i].astype(F32)

    far_out[...] = jnp.zeros_like(far_out)
    sends = []
    O = cfg.own
    for j in range(J):
        t = core * (Z // 2) + 4 * j + lax.rem(z, 4)
        slot = lax.div(mod(z - t, Z), 4)
        for c in range(CORES):
            lines = total[j * Q + c * O : j * Q + (c + 1) * O]
            acc[j, c, 0:O, :] = lines
            far_out[j, c, 0:O, :] = lines.astype(BF)
            copy = pltpu.make_async_remote_copy(
                src_ref=far_out.at[j, c], dst_ref=far_in.at[slot], send_sem=s_far.at[j, c], recv_sem=r_far,
                device_id=at(x, t, c), device_id_type=pl.DeviceIdType.MESH,
            )
            sends.append((t != z, copy))
            pl.when(t != z)(copy.start)

    is_owner = lax.div(z, Z // 2) == core
    own_j = lax.rem(lax.div(z, 4), J)
    hand = pltpu.make_async_remote_copy(
        src_ref=acc.at[own_j, other], dst_ref=final, send_sem=s_fin, recv_sem=r_fin,
        device_id=sibling, device_id_type=pl.DeviceIdType.MESH,
    )

    @pl.when(is_owner)
    def _():
        hand.start()
        final[...] = acc[own_j, core]
        hand.wait_send()

    @pl.when(jnp.logical_not(is_owner))
    def _():
        hand.wait_recv()

    put_out(0)
    drain(r_far, far_in.at[1:F])
    whole = final[0:O, :]
    for slot in range(1, F):
        whole = whole + far_in[slot, 0:O, :].astype(F32)
    owned[...] = whole

    put_out(1)

    drain(s_a1, out1.at[0 : (G - 1) * cfg.grow])
    drain(s_a2, out2.at[0 : (Z - 1) * cfg.zrow])
    drain(s_ag, moved.at[0 : Y - 1])
    drain(s_wf, shards.at[0, 0 : (F - 1) * cfg.pad])
    drain(s_wn, shards.at[:, 0 : 3 * cfg.pad])
    drain(s_wx, w_own.at[:, 1:X])
    drain(s_sib, w_own)
    drain(s_pair, pair_out)
    drain(s_x, x_out)
    drain(s_near, near_out)
    drain(s_y, y_out)
    drain(s_yg, result.at[0 : (Y - 1) * B])
    for needed, copy in sends:
        pl.when(needed)(copy.wait_send)
    drain(s_put, result)


def place_results(units, branch_in, owned_in, branch, grad_value, grad_gate, grad_down):
    branch[...] = branch_in[...]
    grad_value[...] = owned_in[:, :units]
    grad_gate[...] = owned_in[:, units : 2 * units]
    grad_down[...] = owned_in[:, 2 * units :]


def module(cfg, frames, lengths, send_order, value_weight, gate_weight, down_weight, cotangent):
    X, Z, Y, G, R, D, U = cfg.X, cfg.Z, cfg.Y, cfg.G, cfg.rows, cfg.width, cfg.units
    C, S, B = cfg.cols, cfg.half, cfg.yrow
    vmem, hbm = pl.BlockSpec(memory_space=pltpu.VMEM), pl.BlockSpec(memory_space=pl.ANY)
    sem = pltpu.SemaphoreType.DMA
    F, J, H = cfg.far, Z // 8, Z // 8 * cfg.pair
    buffers = [
        ((R, cfg.part), BF),
        ((R, D), BF),
        ((R, cfg.part), BF),
        ((R, cfg.part), BF),
        ((R, cfg.part), BF),
        ((Y, R, cfg.part), BF),
        ((R, D), BF),
        ((R, D), BF),
        ((R, U), BF),
        ((F, 4 * cfg.pad, C), BF),
        ((F, X, cfg.comb, C), BF),
        ((F, X, cfg.comb, C), BF),
        ((D, C), BF),
        ((X, Z * cfg.pair, C), F32),
        ((X, 4, H, C), BF),
        ((X, 4, H, C), BF),
        ((4, X - 1, H, C), BF),
        ((4, X - 1, H, C), BF),
        ((3, H, C), BF),
        ((3, H, C), BF),
        ((J, CORES, cfg.pad, C), F32),
        ((J, CORES, cfg.pad, C), BF),
        ((F, cfg.pad, C), BF),
        ((cfg.pad, C), F32),
        ((B, D), F32),
        ((2, Y - 1, B // 2, D), BF),
        ((2, Y - 1, B // 2, D), BF),
        ((R, D), BF),
    ]
    one = ()
    sems = [
        one, one, one, (4,), one, (4,),
        one, (F,), one, (F,), one, (F,), one, one,
        one, (X,), one, (4,), one, one, (J, CORES), one, one, one,
        one, (2,), one, (2,),
    ]
    branch, owned = pl.pallas_call(
        functools.partial(kernel, cfg),
        out_shape=(jax.ShapeDtypeStruct((R, D), BF), jax.ShapeDtypeStruct((cfg.own, C), F32)),
        in_specs=[pl.BlockSpec(memory_space=pltpu.SMEM), vmem, hbm, vmem, vmem, vmem, hbm],
        out_specs=(hbm, vmem),
        scratch_shapes=[pltpu.VMEM(shape, kind) for shape, kind in buffers]
        + [sem(n) for n in sems]
        + [pltpu.SemaphoreType.REGULAR, sem((2,)), sem(one)],
        compiler_params=pltpu.CompilerParams(
            collective_id=0, has_side_effects=True, vmem_limit_bytes=56 * 1024 * 1024
        ),
    )(lengths, send_order, frames, value_weight, gate_weight, down_weight, cotangent)
    return pl.pallas_call(
        functools.partial(place_results, U),
        out_shape=(jax.ShapeDtypeStruct((R, D), BF),) + (jax.ShapeDtypeStruct((cfg.own, U), F32),) * 3,
        in_specs=[vmem] * 2,
        out_specs=(vmem,) * 4,
    )(branch, owned)


def build(mesh, X, Z):
    def shards(frames, lengths, send_order, value_weight, gate_weight, down_weight, cotangent):
        cfg = Sizes(
            X, Z, mesh.shape["mp"], frames.shape[0], frames.shape[1],
            value_weight.shape[0], value_weight.shape[1],
        )
        return module(
            cfg, frames, lengths, send_order, value_weight, gate_weight, down_weight, cotangent
        )

    return jax.shard_map(
        shards,
        mesh=mesh,
        in_specs=(
            P("dp", None),
            P("dp"),
            P("dp", None),
            P("dp", "mp"),
            P("dp", "mp"),
            P("dp", "mp"),
            P("dp", None),
        ),
        out_specs=(P("dp", None), P("dp", "mp"), P("dp", "mp"), P("dp", "mp")),
        check_vma=False,
    )


def solution(mesh):
    return build(mesh, 4, 16)
```

```python
import functools

import jax
import jax.numpy as jnp
from jax import lax
from jax.experimental import pallas as pl
from jax.experimental.pallas import tpu as pltpu
from jax.sharding import PartitionSpec as P

CORES = 2
BF = jnp.bfloat16
F32 = jnp.float32


def ceil16(rows):
    return -(-rows // 16) * 16


def iota(shape, axis):
    return lax.broadcasted_iota(jnp.int32, shape, axis)


def onehot(hit):
    return jnp.where(hit, 1.0, 0.0).astype(BF)


def dot(left, right):
    return jnp.dot(left, right, preferred_element_type=F32)


def contract_rows(left, right):
    return lax.dot_general(left, right, (((0,), (0,)), ((), ())), preferred_element_type=F32)


def contract_cols(left, right):
    return lax.dot_general(left, right, (((1,), (1,)), ((), ())), preferred_element_type=F32)


def mod(value, count):
    return lax.rem(value + count, count)


class Sizes:
    def __init__(self, X, Z, Y, rows, width, own, units):
        self.X, self.Z, self.Y = X, Z, Y
        self.G = X * CORES
        self.rows, self.width, self.own, self.units = rows, width, own, units
        self.cap = rows // (X * Z * CORES)
        self.part = width // Y
        self.pad = ceil16(own)
        self.zrow = self.G * self.cap
        self.grow = self.Z * self.cap
        self.far = Z // 4
        self.comb = 4 * own
        self.pair = CORES * own
        self.cols = 3 * units
        self.main = self.cols // 128 * 128
        self.fold = own // (self.pad - own)
        self.half = Z // 2 * self.pair
        self.yrow = rows // Y


def pack(cfg, lines):
    own, pad, main, fold = cfg.own, cfg.pad, cfg.main, cfg.fold
    count = lines.shape[0] // own
    q = iota((1, count * own), 1)
    m, r = lax.div(q, own), lax.rem(q, own)
    p = iota((count * pad, count * own), 0)
    body = dot(onehot(p == m * pad + r), lines[:, :main])
    tails = [
        dot(onehot(p == jnp.where(lax.rem(r, fold) == s, m * pad + own + lax.div(r, fold), -1)), lines[:, main:])
        for s in range(fold)
    ]
    wide = -(-fold * (cfg.cols - main) // 128) * 128
    tails.append(jnp.zeros((count * pad, wide - fold * (cfg.cols - main)), F32))
    tail = jnp.concatenate(tails, axis=1)
    return jnp.concatenate([body[:, :wide] + tail, body[:, wide:]], axis=1).astype(BF)


def unpack(cfg, lines):
    own, pad, main, fold = cfg.own, cfg.pad, cfg.main, cfg.fold
    count, rest = lines.shape[0] // pad, cfg.cols - main
    q = iota((1, count * pad), 1)
    m, r = lax.div(q, pad), lax.rem(q, pad)
    p = iota((count * own, count * pad), 0)
    body = dot(onehot(p == jnp.where(r < own, m * own + r, -1)), lines)
    tail = sum(
        dot(onehot(p == jnp.where(r < own, -1, m * own + (r - own) * fold + s)), lines[:, s * rest : (s + 1) * rest])
        for s in range(fold)
    )
    return jnp.concatenate([body, tail], axis=1).astype(BF)


def kernel(
    cfg,
    lengths, send_order, frames_all, value_w, gate_w, down_w, cotangent_all,
    branch, owned,
    frames, cotangent, out1, in1, out2, moved, normed, cot, glu_rows,
    shards, w_own, w_sib, weights,
    block, pair_out, pair_in, x_out, x_in, z_out, z_in, acc, final,
    y_own, y_out, y_in, result,
    s_a1, r_a1, s_a2, r_a2, s_ag, r_ag,
    s_wf, r_wf, s_wn, r_wn, s_wx, r_wx, s_sib, r_sib,
    s_pair, r_pair, s_x, r_x, s_z, r_z, s_own, s_fin, r_fin, s_y, r_y, s_yg, r_yg,
    relay, s_in, s_put,
):
    X, Z, Y, G = cfg.X, cfg.Z, cfg.Y, cfg.G
    R, U, F, cap = cfg.rows, cfg.units, cfg.far, cfg.cap
    dp = lax.axis_index("dp")
    y = lax.axis_index("mp")
    core = lax.rem(dp, CORES)
    z = lax.rem(lax.div(dp, CORES), Z)
    x = lax.div(dp, CORES * Z)
    g = x * CORES + core
    other = 1 - core
    sibling = {"dp": dp + 1 - 2 * core, "mp": y}

    def at(x_, z_, core_):
        return {"dp": (x_ * Z + z_) * CORES + core_, "mp": y}

    def at_x(o):
        return at(mod(x + o, X), z, core)

    def at_z(o):
        return at(x, mod(z + o, Z), core)

    def at_y(o):
        return {"dp": dp, "mp": mod(y + o, Y)}

    def at_g(t):
        return at(lax.div(t, CORES), z, lax.rem(t, CORES))

    def send(src, dst, sent, arrived, where):
        copy = pltpu.make_async_remote_copy(
            src_ref=src, dst_ref=dst, send_sem=sent, recv_sem=arrived,
            device_id=where, device_id_type=pl.DeviceIdType.MESH,
        )
        copy.start()

    def drain(sem, ref):
        pltpu.make_async_copy(ref, ref, sem).wait()

    def rows_of(ref, start, size, step=16):
        return ref.at[pl.ds(pl.multiple_of(start, step), size)]

    barrier = pltpu.get_barrier_semaphore()
    partners = [at_g(mod(g + o, G)) for o in range(1, G)]
    partners += [at_z(o * s) for o in range(1, 5) for s in (1, -1)]
    partners += [at_y(o) for o in range(1, Y)]
    for who in partners:
        pl.semaphore_signal(barrier, inc=1, device_id=who, device_id_type=pl.DeviceIdType.MESH)

    columns = pl.ds(pl.multiple_of(y * cfg.part, 128), cfg.part)
    get_frames = pltpu.make_async_copy(frames_all.at[:, columns], frames, s_in.at[0])
    get_frames.start()
    get_cotangent = pltpu.make_async_copy(cotangent_all, cotangent, s_in.at[1])
    get_cotangent.start()

    packed = jnp.concatenate([value_w[...], gate_w[...], down_w[...]], axis=1)
    mine = shards.at[0, cfg.pad : 2 * cfg.pad]
    mine[...] = pack(cfg, packed)

    row, place = iota((R, R), 0), iota((1, R), 1)
    k_of, z_of, g_of = lax.rem(place, cap), lax.rem(lax.div(place, cap), Z), lax.div(place, cap * Z)
    natural = ((lax.div(g_of, CORES) * Z + z_of) * CORES + lax.rem(g_of, CORES)) * cap + k_of
    numbers = jnp.broadcast_to(send_order[...].astype(F32).astype(BF), (16, R))
    order = dot(numbers, onehot(row == natural))[0:1, :]
    pick = onehot((row.astype(F32) == order) & (row < lengths[0]))
    get_frames.wait()
    out1[...] = contract_rows(pick, frames[...]).astype(BF)

    pl.semaphore_wait(barrier, len(partners))
    for o in (4, -4):
        pl.semaphore_signal(relay, inc=1, device_id=at_z(o), device_id_type=pl.DeviceIdType.MESH)

    for o in range(1, G):
        t = mod(g + o, G)
        send(
            rows_of(out1, t * cfg.grow, cfg.grow), rows_of(in1, g * cfg.grow, cfg.grow),
            s_a1, r_a1, at_g(t),
        )
    rows_of(in1, g * cfg.grow, cfg.grow)[...] = rows_of(out1, g * cfg.grow, cfg.grow)[...]

    near = (1, -1, 2)

    def pass_near(f):
        ref = shards.at[f, cfg.pad : 2 * cfg.pad]
        for a in near:
            lo = (a + 1) * cfg.pad
            send(ref, shards.at[f, lo : lo + cfg.pad], s_wn, r_wn.at[f], at_z(a))

    def pass_far(f):
        send(mine, shards.at[f, cfg.pad : 2 * cfg.pad], s_wf, r_wf.at[f], at_z(4 * f))

    pass_near(0)
    for f in range(1, F):
        if 4 * f != Z // 2:
            pass_far(f)
    pl.semaphore_wait(relay, 2)
    pass_far(F // 2)

    to_new = (z_of * G + g_of) * cap + k_of
    drain(r_a1, in1.at[0 : (G - 1) * cfg.grow])
    out2[...] = dot(onehot(row == to_new), in1[...]).astype(BF)
    here = moved.at[y]
    position = [0] + [2 * o - 1 if o <= Z // 2 else 2 * (Z - o) for o in range(1, Z)]
    parcels = 4
    each = R // parcels
    per = each // cfg.zrow
    def to_z(parcel_range):
        for o in sorted(range(1, Z), key=lambda o: position[Z - o]):
            p = position[Z - o]
            if p // per in parcel_range:
                send(
                    rows_of(out2, mod(z + o, Z) * cfg.zrow, cfg.zrow),
                    here.at[p * cfg.zrow : (p + 1) * cfg.zrow],
                    s_a2, r_a2.at[p // per], at_z(o),
                )

    to_z((0, 1))
    here[0 : cfg.zrow, :] = rows_of(out2, z * cfg.zrow, cfg.zrow)[...]

    def spread(f):
        drain(r_wn.at[f], shards.at[f, 0 : 3 * cfg.pad])
        w_own[f, 0] = unpack(cfg, shards[f])
        for k in (2, 1, 3):
            send(w_own.at[f, 0], w_own.at[f, k], s_wx, r_wx.at[f], at_x(k))

    def hand_on(f):
        drain(r_wx.at[f], w_own.at[f, 1:X])
        send(w_own.at[f], w_sib.at[f], s_sib, r_sib, sibling)

    spread(0)
    for f in (1, 3, 2):
        if f < F:
            drain(r_wf.at[f], shards.at[f, cfg.pad : 2 * cfg.pad])
            pass_near(f)
    to_z((2, 3))

    where = lax.div(place, cfg.zrow)
    away = jnp.where(lax.rem(where, 2) == 1, lax.div(where + 1, 2), lax.rem(Z - lax.div(where, 2), Z))
    k_at, g_at = lax.rem(place, cap), lax.rem(lax.div(place, cap), G)
    natural = (
        (lax.div(g_at, CORES) * Z + lax.rem(z + away, Z)) * CORES + lax.rem(g_at, CORES)
    ) * cap + k_at
    back = onehot(row == natural)
    get_cotangent.wait()
    cot[...] = contract_rows(back, cotangent[...]).astype(BF)

    def share(j):
        drain(r_a2.at[j], here.at[(0 if j else cfg.zrow) : each])
        ref = here.at[j * each : (j + 1) * each]
        for d in (2, 1, 3):
            send(ref, ref, s_ag, r_ag.at[j], at_y(d))

    def normalize(j):
        drain(r_ag.at[j], moved.at[0, 0 : (Y - 1) * each])
        lines = 32
        for i in range(each // lines):
            span = slice(j * each + i * lines, j * each + (i + 1) * lines)
            parts = [moved[c, span, :].astype(F32) for c in range(Y)]
            mean = sum(jnp.sum(p, axis=1, keepdims=True) for p in parts) / cfg.width
            parts = [p - mean for p in parts]
            var = sum(jnp.sum(jnp.square(p), axis=1, keepdims=True) for p in parts) / cfg.width
            scale = lax.rsqrt(var + 1e-05)
            for c in range(Y):
                normed[span, c * cfg.part : (c + 1) * cfg.part] = (parts[c] * scale).astype(BF)

    share(0)
    for f in (1, 3, 2):
        if f < F:
            spread(f)
        if f == 3:
            share(1)
    hand_on(0)
    share(2)
    hand_on(1)
    normalize(0)
    share(3)
    for f in (3, 2):
        if f < F:
            hand_on(f)
    normalize(1)
    normalize(2)

    q = iota((1, 2 * F * cfg.comb), 1)
    side = lax.div(q, F * cfg.comb)
    f_of = lax.rem(lax.div(q, cfg.comb), F)
    n_of = lax.rem(lax.div(q, cfg.own), 4)
    z_of = lax.rem(z - (n_of - 1) - 4 * f_of + 2 * Z, Z)
    core_of = core + side - 2 * core * side
    natural = (z_of * CORES + core_of) * cfg.own + lax.rem(q, cfg.own)
    span = Z * cfg.pair
    spot = onehot(iota((span, span), 0) == natural)
    drain(r_sib, w_sib)
    for k in range(X):
        pieces = [w[f, k] for w in (w_own, w_sib) for f in range(F)]
        rows_of(weights, mod(x - k, X) * span, span)[...] = dot(
            spot, jnp.concatenate(pieces, axis=0)
        ).astype(BF)

    dglu = dot(cot[...], weights[:, 2 * U : 3 * U])
    normalize(3)

    both = dot(normed[...], weights[:, : 2 * U])
    value, gate = both[:, :U], both[:, U : 2 * U]
    sig = jax.nn.sigmoid(gate)
    glu = (value * sig).astype(BF)
    d_value = (dglu * sig).astype(BF)
    d_gate = (dglu * value * sig * (1.0 - sig)).astype(BF)

    d_both = jnp.concatenate([d_value, d_gate], axis=1)
    J = Z // 2 // 4
    steps = (0, 1, -1, 2)
    Q = cfg.pair

    def chunk(o, half, a):
        r = lax.rem(z + a + Z, 4)
        return jnp.concatenate(
            [rows_of(block.at[o], (half * (Z // 2) + r + 4 * j) * Q, Q, 8)[...] for j in range(J)], axis=0
        )

    for o in (2, 1, 3, 0):
        cols = pl.ds(pl.multiple_of(mod(x + o, X) * span, 128), span)
        block[o] = jnp.concatenate(
            [contract_rows(normed[:, cols], d_both), contract_rows(cot[:, cols], glu)], axis=1
        )
        for i, a in enumerate(steps):
            pair_out[o, i] = chunk(o, other, a).astype(BF)
        send(pair_out.at[o], pair_in.at[o], s_pair, r_pair.at[o], sibling)

    glu_rows[...] = dot(back, glu).astype(BF)
    B = cfg.yrow
    half_b = B // 2
    for d in (2, 1, 3):
        some = rows_of(glu_rows, mod(y + d, Y) * B, B)[...]
        theirs = contract_cols(some, weights[:, 2 * U : 3 * U]).astype(BF)
        for h in range(2):
            y_out[h, d - 1] = theirs[h * half_b : (h + 1) * half_b]
    for h in range(2):
        for d in (2, 1, 3):
            send(y_out.at[h, d - 1], y_in.at[h, d - 1], s_y, r_y.at[h], at_y(d))
    y_own[...] = contract_cols(rows_of(glu_rows, y * B, B)[...], weights[:, 2 * U : 3 * U])

    def gather(h):
        drain(r_y.at[h], y_in.at[h])
        lines = y_own[h * half_b : (h + 1) * half_b, :]
        for k in range(Y - 1):
            lines = lines + y_in[h, k].astype(F32)
        ref = rows_of(result, y * B + h * half_b, half_b)
        ref[...] = lines.astype(BF)
        for d in (2, 1, 3):
            send(ref, ref, s_yg, r_yg.at[h], at_y(d))

    def put_out(h):
        drain(r_yg.at[h], result.at[0 : (Y - 1) * half_b])
        for i in range(Y):
            lo = i * B + h * half_b
            pltpu.make_async_copy(
                result.at[lo : lo + half_b], branch.at[lo : lo + half_b], s_put
            ).start()

    for o in (2, 1, 3):
        drain(r_pair.at[o], pair_in.at[o])
    for i, a in enumerate(steps):
        for o in (2, 1, 3):
            x_out[i, o - 1] = (chunk(o, core, a) + pair_in[o, i].astype(F32)).astype(BF)
            send(x_out.at[i, o - 1], x_in.at[i, o - 1], s_x, r_x.at[i], at_x(o))
    drain(r_pair.at[0], pair_in.at[0])

    def summed(i, a):
        drain(r_x.at[i], x_in.at[i])
        total = chunk(0, core, a) + pair_in[0, i].astype(F32)
        for k in range(X - 1):
            total = total + x_in[i, k].astype(F32)
        return total

    O = cfg.own
    sends = []

    def to_owners(i):
        a = steps[i]
        total = summed(i, a)
        z_out[i] = pack(cfg, total.astype(BF))
        for j in range(J):
            t = core * (Z // 2) + 4 * j + lax.rem(z + a + Z, 4)
            for c in range(CORES):
                lo = j * CORES + c
                copy = pltpu.make_async_remote_copy(
                    src_ref=z_out.at[i, lo * cfg.pad : (lo + 1) * cfg.pad], dst_ref=z_in.at[mod(z - t, Z)],
                    send_sem=s_own.at[j, c] if a == 0 else s_z, recv_sem=r_z,
                    device_id=at(x, t, c), device_id_type=pl.DeviceIdType.MESH,
                )
                if a == 0:
                    acc[j, c, 0:O, :] = total[lo * O : (lo + 1) * O]
                    sends.append((t != z, copy))
                    pl.when(t != z)(copy.start)
                else:
                    copy.start()

    to_owners(0)
    gather(0)
    to_owners(1)
    to_owners(2)
    gather(1)
    to_owners(3)

    is_owner = lax.div(z, Z // 2) == core
    own_j = lax.rem(lax.div(z, 4), J)
    hand = pltpu.make_async_remote_copy(
        src_ref=acc.at[own_j, other], dst_ref=final, send_sem=s_fin, recv_sem=r_fin,
        device_id=sibling, device_id_type=pl.DeviceIdType.MESH,
    )

    @pl.when(is_owner)
    def _():
        hand.start()
        final[...] = acc[own_j, core]
        hand.wait_send()

    @pl.when(jnp.logical_not(is_owner))
    def _():
        hand.wait_recv()

    put_out(0)
    drain(r_z, z_in.at[1:Z])
    whole = z_in[1].astype(F32)
    for slot in range(2, Z):
        whole = whole + z_in[slot].astype(F32)
    rest = cfg.cols - cfg.main
    tail = []
    for r in range(O):
        lo, line = r % cfg.fold * rest, O + r // cfg.fold
        tail.append(whole[line : line + 1, lo : lo + rest])
    whole = jnp.concatenate([whole[0:O], jnp.concatenate(tail, axis=0)], axis=1)
    owned[...] = whole + final[0:O, :]

    put_out(1)

    drain(s_a1, out1.at[0 : (G - 1) * cfg.grow])
    drain(s_a2, out2.at[0 : (Z - 1) * cfg.zrow])
    drain(s_ag, moved.at[0 : Y - 1])
    drain(s_wf, shards.at[0, 0 : (F - 1) * cfg.pad])
    drain(s_wn, shards.at[:, 0 : 3 * cfg.pad])
    drain(s_wx, w_own.at[:, 1:X])
    drain(s_sib, w_own)
    drain(s_pair, pair_out)
    drain(s_x, x_out)
    drain(s_z, z_out.at[1:4])
    drain(s_y, y_out)
    drain(s_yg, result.at[0 : (Y - 1) * B])
    for needed, copy in sends:
        pl.when(needed)(copy.wait_send)
    drain(s_put, result)


def place_results(units, branch_in, owned_in, branch, grad_value, grad_gate, grad_down):
    branch[...] = branch_in[...]
    grad_value[...] = owned_in[:, :units]
    grad_gate[...] = owned_in[:, units : 2 * units]
    grad_down[...] = owned_in[:, 2 * units :]


def module(cfg, frames, lengths, send_order, value_weight, gate_weight, down_weight, cotangent):
    X, Z, Y, G, R, D, U = cfg.X, cfg.Z, cfg.Y, cfg.G, cfg.rows, cfg.width, cfg.units
    C, S, B = cfg.cols, cfg.half, cfg.yrow
    vmem, hbm = pl.BlockSpec(memory_space=pltpu.VMEM), pl.BlockSpec(memory_space=pl.ANY)
    sem = pltpu.SemaphoreType.DMA
    F, J, H = cfg.far, Z // 8, Z // 8 * cfg.pair
    buffers = [
        ((R, cfg.part), BF),
        ((R, D), BF),
        ((R, cfg.part), BF),
        ((R, cfg.part), BF),
        ((R, cfg.part), BF),
        ((Y, R, cfg.part), BF),
        ((R, D), BF),
        ((R, D), BF),
        ((R, U), BF),
        ((F, 4 * cfg.pad, cfg.main), BF),
        ((F, X, cfg.comb, C), BF),
        ((F, X, cfg.comb, C), BF),
        ((D, C), BF),
        ((X, Z * cfg.pair, C), F32),
        ((X, 4, H, C), BF),
        ((X, 4, H, C), BF),
        ((4, X - 1, H, C), BF),
        ((4, X - 1, H, C), BF),
        ((4, J * CORES * cfg.pad, cfg.main), BF),
        ((Z, cfg.pad, cfg.main), BF),
        ((J, CORES, cfg.pad, C), F32),
        ((cfg.pad, C), F32),
        ((B, D), F32),
        ((2, Y - 1, B // 2, D), BF),
        ((2, Y - 1, B // 2, D), BF),
        ((R, D), BF),
    ]
    one = ()
    sems = [
        one, one, one, (4,), one, (4,),
        one, (F,), one, (F,), one, (F,), one, one,
        one, (X,), one, (4,), one, one, (J, CORES), one, one,
        one, (2,), one, (2,),
    ]
    branch, owned = pl.pallas_call(
        functools.partial(kernel, cfg),
        out_shape=(jax.ShapeDtypeStruct((R, D), BF), jax.ShapeDtypeStruct((cfg.own, C), F32)),
        in_specs=[pl.BlockSpec(memory_space=pltpu.SMEM), vmem, hbm, vmem, vmem, vmem, hbm],
        out_specs=(hbm, vmem),
        scratch_shapes=[pltpu.VMEM(shape, kind) for shape, kind in buffers]
        + [sem(n) for n in sems]
        + [pltpu.SemaphoreType.REGULAR, sem((2,)), sem(one)],
        compiler_params=pltpu.CompilerParams(
            collective_id=0, has_side_effects=True, vmem_limit_bytes=56 * 1024 * 1024
        ),
    )(lengths, send_order, frames, value_weight, gate_weight, down_weight, cotangent)
    return pl.pallas_call(
        functools.partial(place_results, U),
        out_shape=(jax.ShapeDtypeStruct((R, D), BF),) + (jax.ShapeDtypeStruct((cfg.own, U), F32),) * 3,
        in_specs=[vmem] * 2,
        out_specs=(vmem,) * 4,
    )(branch, owned)


def build(mesh, X, Z):
    def shards(frames, lengths, send_order, value_weight, gate_weight, down_weight, cotangent):
        cfg = Sizes(
            X, Z, mesh.shape["mp"], frames.shape[0], frames.shape[1],
            value_weight.shape[0], value_weight.shape[1],
        )
        return module(
            cfg, frames, lengths, send_order, value_weight, gate_weight, down_weight, cotangent
        )

    return jax.shard_map(
        shards,
        mesh=mesh,
        in_specs=(
            P("dp", None),
            P("dp"),
            P("dp", None),
            P("dp", "mp"),
            P("dp", "mp"),
            P("dp", "mp"),
            P("dp", None),
        ),
        out_specs=(P("dp", None), P("dp", "mp"), P("dp", "mp"), P("dp", "mp")),
        check_vma=False,
    )


def solution(mesh):
    return build(mesh, 4, 16)
```

```python
import functools

import jax
import jax.numpy as jnp
from jax import lax
from jax.experimental import pallas as pl
from jax.experimental.pallas import tpu as pltpu
from jax.sharding import PartitionSpec as P

CORES = 2
BF = jnp.bfloat16
F32 = jnp.float32


def ceil16(rows):
    return -(-rows // 16) * 16


def iota(shape, axis):
    return lax.broadcasted_iota(jnp.int32, shape, axis)


def onehot(hit):
    return jnp.where(hit, 1.0, 0.0).astype(BF)


def dot(left, right):
    return jnp.dot(left, right, preferred_element_type=F32)


def contract_rows(left, right):
    return lax.dot_general(left, right, (((0,), (0,)), ((), ())), preferred_element_type=F32)


def contract_cols(left, right):
    return lax.dot_general(left, right, (((1,), (1,)), ((), ())), preferred_element_type=F32)


def mod(value, count):
    return lax.rem(value + count, count)


class Sizes:
    def __init__(self, X, Z, Y, rows, width, own, units):
        self.X, self.Z, self.Y = X, Z, Y
        self.G = X * CORES
        self.rows, self.width, self.own, self.units = rows, width, own, units
        self.cap = rows // (X * Z * CORES)
        self.part = width // Y
        self.pad = ceil16(own)
        self.zrow = self.G * self.cap
        self.grow = self.Z * self.cap
        self.far = Z // 4
        self.comb = 4 * own
        self.pair = CORES * own
        self.cols = 3 * units
        self.main = self.cols // 128 * 128
        self.fold = own // (self.pad - own)
        self.half = Z // 2 * self.pair
        self.yrow = rows // Y


def pack(cfg, lines):
    own, pad, main, fold = cfg.own, cfg.pad, cfg.main, cfg.fold
    count = lines.shape[0] // own
    q = iota((1, count * own), 1)
    m, r = lax.div(q, own), lax.rem(q, own)
    p = iota((count * pad, count * own), 0)
    body = dot(onehot(p == m * pad + r), lines[:, :main])
    tails = [
        dot(onehot(p == jnp.where(lax.rem(r, fold) == s, m * pad + own + lax.div(r, fold), -1)), lines[:, main:])
        for s in range(fold)
    ]
    wide = -(-fold * (cfg.cols - main) // 128) * 128
    tails.append(jnp.zeros((count * pad, wide - fold * (cfg.cols - main)), F32))
    tail = jnp.concatenate(tails, axis=1)
    return jnp.concatenate([body[:, :wide] + tail, body[:, wide:]], axis=1).astype(BF)


def unpack(cfg, lines):
    own, pad, main, fold = cfg.own, cfg.pad, cfg.main, cfg.fold
    count, rest = lines.shape[0] // pad, cfg.cols - main
    q = iota((1, count * pad), 1)
    m, r = lax.div(q, pad), lax.rem(q, pad)
    p = iota((count * own, count * pad), 0)
    body = dot(onehot(p == jnp.where(r < own, m * own + r, -1)), lines)
    tail = sum(
        dot(onehot(p == jnp.where(r < own, -1, m * own + (r - own) * fold + s)), lines[:, s * rest : (s + 1) * rest])
        for s in range(fold)
    )
    return jnp.concatenate([body, tail], axis=1).astype(BF)


def kernel(
    cfg,
    lengths, send_order, frames_all, value_w, gate_w, down_w, cotangent_all,
    branch, owned,
    frames, cotangent, out1, in1, out2, moved, normed, cot, glu_rows,
    shards, w_own, w_sib, weights,
    block, pair_out, pair_in, x_out, x_in, z_out, z_in, acc, final,
    y_own, y_out, y_in, result,
    s_a1, r_a1, s_a2, r_a2, s_ag, r_ag,
    s_wf, r_wf, s_wn, r_wn, s_wx, r_wx, s_sib, r_sib,
    s_pair, r_pair, s_x, r_x, s_z, r_z, s_own, s_fin, r_fin, s_y, r_y, s_yg, r_yg,
    relay, s_in, s_put,
):
    X, Z, Y, G = cfg.X, cfg.Z, cfg.Y, cfg.G
    R, U, F, cap = cfg.rows, cfg.units, cfg.far, cfg.cap
    dp = lax.axis_index("dp")
    y = lax.axis_index("mp")
    core = lax.rem(dp, CORES)
    z = lax.rem(lax.div(dp, CORES), Z)
    x = lax.div(dp, CORES * Z)
    g = x * CORES + core
    other = 1 - core
    sibling = {"dp": dp + 1 - 2 * core, "mp": y}

    def at(x_, z_, core_):
        return {"dp": (x_ * Z + z_) * CORES + core_, "mp": y}

    def at_x(o):
        return at(mod(x + o, X), z, core)

    def at_z(o):
        return at(x, mod(z + o, Z), core)

    def at_y(o):
        return {"dp": dp, "mp": mod(y + o, Y)}

    def at_g(t):
        return at(lax.div(t, CORES), z, lax.rem(t, CORES))

    def send(src, dst, sent, arrived, where):
        copy = pltpu.make_async_remote_copy(
            src_ref=src, dst_ref=dst, send_sem=sent, recv_sem=arrived,
            device_id=where, device_id_type=pl.DeviceIdType.MESH,
        )
        copy.start()

    def drain(sem, ref):
        pltpu.make_async_copy(ref, ref, sem).wait()

    def rows_of(ref, start, size, step=16):
        return ref.at[pl.ds(pl.multiple_of(start, step), size)]

    barrier = pltpu.get_barrier_semaphore()
    partners = [at_g(mod(g + o, G)) for o in range(1, G)]
    partners += [at_z(o * s) for o in range(1, 5) for s in (1, -1)]
    partners += [at_y(o) for o in range(1, Y)]
    for who in partners:
        pl.semaphore_signal(barrier, inc=1, device_id=who, device_id_type=pl.DeviceIdType.MESH)

    columns = pl.ds(pl.multiple_of(y * cfg.part, 128), cfg.part)
    get_frames = pltpu.make_async_copy(frames_all.at[:, columns], frames, s_in.at[0])
    get_frames.start()
    get_cotangent = pltpu.make_async_copy(cotangent_all, cotangent, s_in.at[1])
    get_cotangent.start()

    packed = jnp.concatenate([value_w[...], gate_w[...], down_w[...]], axis=1)
    mine = shards.at[0, cfg.pad : 2 * cfg.pad]
    mine[...] = pack(cfg, packed)

    row, place = iota((R, R), 0), iota((1, R), 1)
    k_of, z_of, g_of = lax.rem(place, cap), lax.rem(lax.div(place, cap), Z), lax.div(place, cap * Z)
    natural = ((lax.div(g_of, CORES) * Z + z_of) * CORES + lax.rem(g_of, CORES)) * cap + k_of
    numbers = jnp.broadcast_to(send_order[...].astype(F32).astype(BF), (16, R))
    order = dot(numbers, onehot(row == natural))[0:1, :]
    pick = onehot((row.astype(F32) == order) & (row < lengths[0]))
    get_frames.wait()
    out1[...] = contract_rows(pick, frames[...]).astype(BF)

    pl.semaphore_wait(barrier, len(partners))
    for o in (4, -4):
        pl.semaphore_signal(relay, inc=1, device_id=at_z(o), device_id_type=pl.DeviceIdType.MESH)

    for o in range(1, G):
        t = mod(g + o, G)
        send(
            rows_of(out1, t * cfg.grow, cfg.grow), rows_of(in1, g * cfg.grow, cfg.grow),
            s_a1, r_a1, at_g(t),
        )
    rows_of(in1, g * cfg.grow, cfg.grow)[...] = rows_of(out1, g * cfg.grow, cfg.grow)[...]

    near = (1, -1, 2)

    def pass_near(f):
        ref = shards.at[f, cfg.pad : 2 * cfg.pad]
        for a in near:
            lo = (a + 1) * cfg.pad
            send(ref, shards.at[f, lo : lo + cfg.pad], s_wn, r_wn.at[f], at_z(a))

    def pass_far(f):
        send(mine, shards.at[f, cfg.pad : 2 * cfg.pad], s_wf, r_wf.at[f], at_z(4 * f))

    pass_near(0)
    for f in range(1, F):
        if 4 * f != Z // 2:
            pass_far(f)
    pl.semaphore_wait(relay, 2)
    pass_far(F // 2)

    to_new = (z_of * G + g_of) * cap + k_of
    drain(r_a1, in1.at[0 : (G - 1) * cfg.grow])
    out2[...] = dot(onehot(row == to_new), in1[...]).astype(BF)
    here = moved.at[y]
    position = [0] + [2 * o - 1 if o <= Z // 2 else 2 * (Z - o) for o in range(1, Z)]
    quarter = Z // 4
    edges = [0, quarter, 2 * quarter, 3 * quarter, Z - quarter // 2, Z]
    parcel_of = [sum(p >= edge for edge in edges[1:]) for p in range(Z)]
    bounds = [(lo * cfg.zrow, hi * cfg.zrow) for lo, hi in zip(edges, edges[1:])]

    def to_z(parcel_range):
        for o in sorted(range(1, Z), key=lambda o: position[Z - o]):
            p = position[Z - o]
            if parcel_of[p] in parcel_range:
                send(
                    rows_of(out2, mod(z + o, Z) * cfg.zrow, cfg.zrow),
                    here.at[p * cfg.zrow : (p + 1) * cfg.zrow],
                    s_a2, r_a2.at[parcel_of[p]], at_z(o),
                )

    to_z((0, 1))
    here[0 : cfg.zrow, :] = rows_of(out2, z * cfg.zrow, cfg.zrow)[...]

    def spread(f):
        drain(r_wn.at[f], shards.at[f, 0 : 3 * cfg.pad])
        w_own[f, 0] = unpack(cfg, shards[f])
        for k in (2, 1, 3):
            send(w_own.at[f, 0], w_own.at[f, k], s_wx, r_wx.at[f], at_x(k))

    def hand_on(f):
        drain(r_wx.at[f], w_own.at[f, 1:X])
        send(w_own.at[f], w_sib.at[f], s_sib, r_sib, sibling)

    spread(0)
    for f in (1, 3, 2):
        drain(r_wf.at[f], shards.at[f, cfg.pad : 2 * cfg.pad])
        pass_near(f)
    to_z((2, 3, 4))

    where = lax.div(place, cfg.zrow)
    away = jnp.where(lax.rem(where, 2) == 1, lax.div(where + 1, 2), lax.rem(Z - lax.div(where, 2), Z))
    k_at, g_at = lax.rem(place, cap), lax.rem(lax.div(place, cap), G)
    natural = (
        (lax.div(g_at, CORES) * Z + lax.rem(z + away, Z)) * CORES + lax.rem(g_at, CORES)
    ) * cap + k_at
    back = onehot(row == natural)
    get_cotangent.wait()
    cot[...] = contract_rows(back, cotangent[...]).astype(BF)

    def share(j):
        lo, hi = bounds[j]
        drain(r_a2.at[j], here.at[(lo if j else cfg.zrow) : hi])
        ref = here.at[lo:hi]
        for d in (2, 1, 3):
            send(ref, ref, s_ag, r_ag.at[j], at_y(d))

    def normalize(j):
        start, stop = bounds[j]
        drain(r_ag.at[j], moved.at[0, 0 : (Y - 1) * (stop - start)])
        lines = min(32, stop - start)
        for lo in range(start, stop, lines):
            span = slice(lo, lo + lines)
            parts = [moved[c, span, :].astype(F32) for c in range(Y)]
            mean = sum(jnp.sum(p, axis=1, keepdims=True) for p in parts) / cfg.width
            parts = [p - mean for p in parts]
            var = sum(jnp.sum(jnp.square(p), axis=1, keepdims=True) for p in parts) / cfg.width
            scale = lax.rsqrt(var + 1e-05)
            for c in range(Y):
                normed[span, c * cfg.part : (c + 1) * cfg.part] = (parts[c] * scale).astype(BF)

    share(0)
    spread(1)
    spread(3)
    share(1)
    spread(2)
    hand_on(0)
    share(2)
    hand_on(1)
    normalize(0)
    share(3)
    hand_on(3)
    share(4)
    hand_on(2)
    normalize(1)
    normalize(2)

    q = iota((1, 2 * F * cfg.comb), 1)
    side = lax.div(q, F * cfg.comb)
    f_of = lax.rem(lax.div(q, cfg.comb), F)
    n_of = lax.rem(lax.div(q, cfg.own), 4)
    z_of = lax.rem(z - (n_of - 1) - 4 * f_of + 2 * Z, Z)
    core_of = core + side - 2 * core * side
    natural = (z_of * CORES + core_of) * cfg.own + lax.rem(q, cfg.own)
    span = Z * cfg.pair
    spot = onehot(iota((span, span), 0) == natural)
    drain(r_sib, w_sib)
    for k in range(X):
        pieces = [w[f, k] for w in (w_own, w_sib) for f in range(F)]
        rows_of(weights, mod(x - k, X) * span, span)[...] = dot(
            spot, jnp.concatenate(pieces, axis=0)
        ).astype(BF)

    dglu = dot(cot[...], weights[:, 2 * U : 3 * U])
    normalize(3)
    normalize(4)

    both = dot(normed[...], weights[:, : 2 * U])
    value, gate = both[:, :U], both[:, U : 2 * U]
    sig = jax.nn.sigmoid(gate)
    glu = (value * sig).astype(BF)
    d_value = (dglu * sig).astype(BF)
    d_gate = (dglu * value * sig * (1.0 - sig)).astype(BF)

    d_both = jnp.concatenate([d_value, d_gate], axis=1)
    J = Z // 2 // 4
    steps = (0, 1, -1, 2)
    Q = cfg.pair

    def chunk(o, half, a):
        r = lax.rem(z + a + Z, 4)
        return jnp.concatenate(
            [rows_of(block.at[o], (half * (Z // 2) + r + 4 * j) * Q, Q, 8)[...] for j in range(J)], axis=0
        )

    for o in (2, 1, 3, 0):
        cols = pl.ds(pl.multiple_of(mod(x + o, X) * span, 128), span)
        block[o] = jnp.concatenate(
            [contract_rows(normed[:, cols], d_both), contract_rows(cot[:, cols], glu)], axis=1
        )
        for i, a in enumerate(steps):
            pair_out[o, i] = chunk(o, other, a).astype(BF)
        send(pair_out.at[o], pair_in.at[o], s_pair, r_pair.at[o], sibling)

    B = cfg.yrow
    half_b = B // 2

    def gather(h):
        drain(r_y.at[h], y_in.at[h])
        lines = y_own[h * half_b : (h + 1) * half_b, :]
        for k in range(Y - 1):
            lines = lines + y_in[h, k].astype(F32)
        ref = rows_of(result, y * B + h * half_b, half_b)
        ref[...] = lines.astype(BF)
        for d in (2, 1, 3):
            send(ref, ref, s_yg, r_yg.at[h], at_y(d))

    def put_out(h):
        drain(r_yg.at[h], result.at[0 : (Y - 1) * half_b])
        for i in range(Y):
            lo = i * B + h * half_b
            pltpu.make_async_copy(
                result.at[lo : lo + half_b], branch.at[lo : lo + half_b], s_put
            ).start()

    def to_x(i, o):
        x_out[i, o - 1] = (chunk(o, core, steps[i]) + pair_in[o, i].astype(F32)).astype(BF)
        send(x_out.at[i, o - 1], x_in.at[i, o - 1], s_x, r_x.at[i], at_x(o))

    for o in (2, 1, 3):
        drain(r_pair.at[o], pair_in.at[o])
        to_x(0, o)

    glu_rows[...] = dot(back, glu).astype(BF)
    for d in (2, 1, 3):
        some = rows_of(glu_rows, mod(y + d, Y) * B, B)[...]
        theirs = contract_cols(some, weights[:, 2 * U : 3 * U]).astype(BF)
        for h in range(2):
            y_out[h, d - 1] = theirs[h * half_b : (h + 1) * half_b]
    for h in range(2):
        for d in (2, 1, 3):
            send(y_out.at[h, d - 1], y_in.at[h, d - 1], s_y, r_y.at[h], at_y(d))
    y_own[...] = contract_cols(rows_of(glu_rows, y * B, B)[...], weights[:, 2 * U : 3 * U])

    for i in range(1, 4):
        for o in (2, 1, 3):
            to_x(i, o)
    drain(r_pair.at[0], pair_in.at[0])

    def summed(i, a):
        drain(r_x.at[i], x_in.at[i])
        total = chunk(0, core, a) + pair_in[0, i].astype(F32)
        for k in range(X - 1):
            total = total + x_in[i, k].astype(F32)
        return total

    O = cfg.own
    sends = []

    def to_owners(i):
        a = steps[i]
        total = summed(i, a)
        z_out[i] = pack(cfg, total.astype(BF))
        for j in range(J):
            t = core * (Z // 2) + 4 * j + lax.rem(z + a + Z, 4)
            for c in range(CORES):
                lo = j * CORES + c
                copy = pltpu.make_async_remote_copy(
                    src_ref=z_out.at[i, lo * cfg.pad : (lo + 1) * cfg.pad], dst_ref=z_in.at[mod(z - t, Z)],
                    send_sem=s_own.at[j, c] if a == 0 else s_z, recv_sem=r_z,
                    device_id=at(x, t, c), device_id_type=pl.DeviceIdType.MESH,
                )
                if a == 0:
                    acc[j, c, 0:O, :] = total[lo * O : (lo + 1) * O]
                    sends.append((t != z, copy))
                    pl.when(t != z)(copy.start)
                else:
                    copy.start()

    to_owners(0)
    gather(0)
    to_owners(1)
    to_owners(2)
    gather(1)
    to_owners(3)

    is_owner = lax.div(z, Z // 2) == core
    own_j = lax.rem(lax.div(z, 4), J)
    hand = pltpu.make_async_remote_copy(
        src_ref=acc.at[own_j, other], dst_ref=final, send_sem=s_fin, recv_sem=r_fin,
        device_id=sibling, device_id_type=pl.DeviceIdType.MESH,
    )

    @pl.when(is_owner)
    def _():
        hand.start()
        final[...] = acc[own_j, core]
        hand.wait_send()

    @pl.when(jnp.logical_not(is_owner))
    def _():
        hand.wait_recv()

    put_out(0)
    drain(r_z, z_in.at[1:Z])
    whole = z_in[1].astype(F32)
    for slot in range(2, Z):
        whole = whole + z_in[slot].astype(F32)
    rest = cfg.cols - cfg.main
    tail = []
    for r in range(O):
        lo, line = r % cfg.fold * rest, O + r // cfg.fold
        tail.append(whole[line : line + 1, lo : lo + rest])
    whole = jnp.concatenate([whole[0:O], jnp.concatenate(tail, axis=0)], axis=1)
    owned[...] = whole + final[0:O, :]

    put_out(1)

    drain(s_a1, out1.at[0 : (G - 1) * cfg.grow])
    drain(s_a2, out2.at[0 : (Z - 1) * cfg.zrow])
    drain(s_ag, moved.at[0 : Y - 1])
    drain(s_wf, shards.at[0, 0 : (F - 1) * cfg.pad])
    drain(s_wn, shards.at[:, 0 : 3 * cfg.pad])
    drain(s_wx, w_own.at[:, 1:X])
    drain(s_sib, w_own)
    drain(s_pair, pair_out)
    drain(s_x, x_out)
    drain(s_z, z_out.at[1:4])
    drain(s_y, y_out)
    drain(s_yg, result.at[0 : (Y - 1) * B])
    for needed, copy in sends:
        pl.when(needed)(copy.wait_send)
    drain(s_put, result)


def place_results(units, branch_in, owned_in, branch, grad_value, grad_gate, grad_down):
    branch[...] = branch_in[...]
    grad_value[...] = owned_in[:, :units]
    grad_gate[...] = owned_in[:, units : 2 * units]
    grad_down[...] = owned_in[:, 2 * units :]


def module(cfg, frames, lengths, send_order, value_weight, gate_weight, down_weight, cotangent):
    X, Z, Y, G, R, D, U = cfg.X, cfg.Z, cfg.Y, cfg.G, cfg.rows, cfg.width, cfg.units
    C, S, B = cfg.cols, cfg.half, cfg.yrow
    vmem, hbm = pl.BlockSpec(memory_space=pltpu.VMEM), pl.BlockSpec(memory_space=pl.ANY)
    sem = pltpu.SemaphoreType.DMA
    F, J, H = cfg.far, Z // 8, Z // 8 * cfg.pair
    buffers = [
        ((R, cfg.part), BF),
        ((R, D), BF),
        ((R, cfg.part), BF),
        ((R, cfg.part), BF),
        ((R, cfg.part), BF),
        ((Y, R, cfg.part), BF),
        ((R, D), BF),
        ((R, D), BF),
        ((R, U), BF),
        ((F, 4 * cfg.pad, cfg.main), BF),
        ((F, X, cfg.comb, C), BF),
        ((F, X, cfg.comb, C), BF),
        ((D, C), BF),
        ((X, Z * cfg.pair, C), F32),
        ((X, 4, H, C), BF),
        ((X, 4, H, C), BF),
        ((4, X - 1, H, C), BF),
        ((4, X - 1, H, C), BF),
        ((4, J * CORES * cfg.pad, cfg.main), BF),
        ((Z, cfg.pad, cfg.main), BF),
        ((J, CORES, cfg.pad, C), F32),
        ((cfg.pad, C), F32),
        ((B, D), F32),
        ((2, Y - 1, B // 2, D), BF),
        ((2, Y - 1, B // 2, D), BF),
        ((R, D), BF),
    ]
    one = ()
    sems = [
        one, one, one, (5,), one, (5,),
        one, (F,), one, (F,), one, (F,), one, one,
        one, (X,), one, (4,), one, one, (J, CORES), one, one,
        one, (2,), one, (2,),
    ]
    branch, owned = pl.pallas_call(
        functools.partial(kernel, cfg),
        out_shape=(jax.ShapeDtypeStruct((R, D), BF), jax.ShapeDtypeStruct((cfg.own, C), F32)),
        in_specs=[pl.BlockSpec(memory_space=pltpu.SMEM), vmem, hbm, vmem, vmem, vmem, hbm],
        out_specs=(hbm, vmem),
        scratch_shapes=[pltpu.VMEM(shape, kind) for shape, kind in buffers]
        + [sem(n) for n in sems]
        + [pltpu.SemaphoreType.REGULAR, sem((2,)), sem(one)],
        compiler_params=pltpu.CompilerParams(
            collective_id=0, has_side_effects=True, vmem_limit_bytes=56 * 1024 * 1024
        ),
    )(lengths, send_order, frames, value_weight, gate_weight, down_weight, cotangent)
    return pl.pallas_call(
        functools.partial(place_results, U),
        out_shape=(jax.ShapeDtypeStruct((R, D), BF),) + (jax.ShapeDtypeStruct((cfg.own, U), F32),) * 3,
        in_specs=[vmem] * 2,
        out_specs=(vmem,) * 4,
    )(branch, owned)


def build(mesh, X, Z):
    def shards(frames, lengths, send_order, value_weight, gate_weight, down_weight, cotangent):
        cfg = Sizes(
            X, Z, mesh.shape["mp"], frames.shape[0], frames.shape[1],
            value_weight.shape[0], value_weight.shape[1],
        )
        return module(
            cfg, frames, lengths, send_order, value_weight, gate_weight, down_weight, cotangent
        )

    return jax.shard_map(
        shards,
        mesh=mesh,
        in_specs=(
            P("dp", None),
            P("dp"),
            P("dp", None),
            P("dp", "mp"),
            P("dp", "mp"),
            P("dp", "mp"),
            P("dp", None),
        ),
        out_specs=(P("dp", None), P("dp", "mp"), P("dp", "mp"), P("dp", "mp")),
        check_vma=False,
    )


def solution(mesh):
    return build(mesh, 4, 16)
```

```python
import functools

import jax
import jax.numpy as jnp
from jax import lax
from jax.experimental import pallas as pl
from jax.experimental.pallas import tpu as pltpu
from jax.sharding import PartitionSpec as P

CORES = 2
BF = jnp.bfloat16
F32 = jnp.float32


def ceil16(rows):
    return -(-rows // 16) * 16


def iota(shape, axis):
    return lax.broadcasted_iota(jnp.int32, shape, axis)


def onehot(hit):
    return jnp.where(hit, 1.0, 0.0).astype(BF)


def dot(left, right):
    return jnp.dot(left, right, preferred_element_type=F32)


def contract_rows(left, right):
    return lax.dot_general(left, right, (((0,), (0,)), ((), ())), preferred_element_type=F32)


def contract_cols(left, right):
    return lax.dot_general(left, right, (((1,), (1,)), ((), ())), preferred_element_type=F32)


def mod(value, count):
    return lax.rem(value + count, count)


class Sizes:
    def __init__(self, X, Z, Y, rows, width, own, units):
        self.X, self.Z, self.Y = X, Z, Y
        self.G = X * CORES
        self.rows, self.width, self.own, self.units = rows, width, own, units
        self.cap = rows // (X * Z * CORES)
        self.part = width // Y
        self.pad = ceil16(own)
        self.zrow = self.G * self.cap
        self.grow = self.Z * self.cap
        self.far = Z // 4
        self.comb = 4 * own
        self.pair = CORES * own
        self.cols = 3 * units
        self.main = self.cols // 128 * 128
        self.fold = own // (self.pad - own)
        self.half = Z // 2 * self.pair
        self.yrow = rows // Y


def pack(cfg, lines):
    own, pad, main, fold = cfg.own, cfg.pad, cfg.main, cfg.fold
    count = lines.shape[0] // own
    q = iota((1, count * own), 1)
    m, r = lax.div(q, own), lax.rem(q, own)
    p = iota((count * pad, count * own), 0)
    body = dot(onehot(p == m * pad + r), lines[:, :main])
    tails = [
        dot(onehot(p == jnp.where(lax.rem(r, fold) == s, m * pad + own + lax.div(r, fold), -1)), lines[:, main:])
        for s in range(fold)
    ]
    wide = -(-fold * (cfg.cols - main) // 128) * 128
    tails.append(jnp.zeros((count * pad, wide - fold * (cfg.cols - main)), F32))
    tail = jnp.concatenate(tails, axis=1)
    return jnp.concatenate([body[:, :wide] + tail, body[:, wide:]], axis=1).astype(BF)


def unpack(cfg, lines):
    own, pad, main, fold = cfg.own, cfg.pad, cfg.main, cfg.fold
    count, rest = lines.shape[0] // pad, cfg.cols - main
    q = iota((1, count * pad), 1)
    m, r = lax.div(q, pad), lax.rem(q, pad)
    p = iota((count * own, count * pad), 0)
    body = dot(onehot(p == jnp.where(r < own, m * own + r, -1)), lines)
    tail = sum(
        dot(onehot(p == jnp.where(r < own, -1, m * own + (r - own) * fold + s)), lines[:, s * rest : (s + 1) * rest])
        for s in range(fold)
    )
    return jnp.concatenate([body, tail], axis=1).astype(BF)


def kernel(
    cfg,
    lengths, send_order, frames_all, value_w, gate_w, down_w, cotangent_all,
    branch, owned,
    frames, cotangent, out1, in1, out2, moved, normed, cot, glu_rows,
    shards, w_own, w_sib, staged, weights,
    block, pair_out, pair_in, x_out, x_in, z_out, z_in, acc, final, last,
    y_own, y_out, y_in, result,
    s_a1, r_a1, s_a2, r_a2, s_ag, r_ag,
    s_wf, r_wf, s_wn, r_wn, s_wx, r_wx, s_sib, r_sib,
    s_pair, r_pair, s_x, r_x, s_z, r_z, s_own, s_fin, r_fin, s_y, r_y, s_yg, r_yg,
    relay, s_in, s_put,
):
    X, Z, Y, G = cfg.X, cfg.Z, cfg.Y, cfg.G
    R, U, F, cap = cfg.rows, cfg.units, cfg.far, cfg.cap
    dp = lax.axis_index("dp")
    y = lax.axis_index("mp")
    core = lax.rem(dp, CORES)
    z = lax.rem(lax.div(dp, CORES), Z)
    x = lax.div(dp, CORES * Z)
    g = x * CORES + core
    other = 1 - core
    sibling = {"dp": dp + 1 - 2 * core, "mp": y}

    def at(x_, z_, core_):
        return {"dp": (x_ * Z + z_) * CORES + core_, "mp": y}

    def at_x(o):
        return at(mod(x + o, X), z, core)

    def at_z(o):
        return at(x, mod(z + o, Z), core)

    def at_y(o):
        return {"dp": dp, "mp": mod(y + o, Y)}

    def at_g(t):
        return at(lax.div(t, CORES), z, lax.rem(t, CORES))

    def send(src, dst, sent, arrived, where):
        copy = pltpu.make_async_remote_copy(
            src_ref=src, dst_ref=dst, send_sem=sent, recv_sem=arrived,
            device_id=where, device_id_type=pl.DeviceIdType.MESH,
        )
        copy.start()

    def drain(sem, ref):
        pltpu.make_async_copy(ref, ref, sem).wait()

    def rows_of(ref, start, size, step=16):
        return ref.at[pl.ds(pl.multiple_of(start, step), size)]

    barrier = pltpu.get_barrier_semaphore()
    partners = [at_g(mod(g + o, G)) for o in range(1, G)]
    partners += [at_z(o * s) for o in range(1, 5) for s in (1, -1)]
    partners += [at_y(o) for o in range(1, Y)]
    for who in partners:
        pl.semaphore_signal(barrier, inc=1, device_id=who, device_id_type=pl.DeviceIdType.MESH)

    columns = pl.ds(pl.multiple_of(y * cfg.part, 128), cfg.part)
    get_frames = pltpu.make_async_copy(frames_all.at[:, columns], frames, s_in.at[0])
    get_frames.start()
    get_cotangent = pltpu.make_async_copy(cotangent_all, cotangent, s_in.at[1])
    get_cotangent.start()

    packed = jnp.concatenate([value_w[...], gate_w[...], down_w[...]], axis=1)
    mine = shards.at[0, cfg.pad : 2 * cfg.pad]
    mine[...] = pack(cfg, packed)

    row, place = iota((R, R), 0), iota((1, R), 1)
    k_of, z_of, g_of = lax.rem(place, cap), lax.rem(lax.div(place, cap), Z), lax.div(place, cap * Z)
    natural = ((lax.div(g_of, CORES) * Z + z_of) * CORES + lax.rem(g_of, CORES)) * cap + k_of
    numbers = jnp.broadcast_to(send_order[...].astype(F32).astype(BF), (16, R))
    order = dot(numbers, onehot(row == natural))[0:1, :]
    pick = onehot((row.astype(F32) == order) & (row < lengths[0]))
    get_frames.wait()
    out1[...] = contract_rows(pick, frames[...]).astype(BF)

    pl.semaphore_wait(barrier, len(partners))
    for o in (4, -4):
        pl.semaphore_signal(relay, inc=1, device_id=at_z(o), device_id_type=pl.DeviceIdType.MESH)

    for o in range(1, G):
        t = mod(g + o, G)
        send(
            rows_of(out1, t * cfg.grow, cfg.grow), rows_of(in1, g * cfg.grow, cfg.grow),
            s_a1, r_a1, at_g(t),
        )
    rows_of(in1, g * cfg.grow, cfg.grow)[...] = rows_of(out1, g * cfg.grow, cfg.grow)[...]

    near = (1, -1, 2)

    def pass_near(f):
        ref = shards.at[f, cfg.pad : 2 * cfg.pad]
        for a in near:
            lo = (a + 1) * cfg.pad
            send(ref, shards.at[f, lo : lo + cfg.pad], s_wn, r_wn.at[f], at_z(a))

    def pass_far(f):
        send(mine, shards.at[f, cfg.pad : 2 * cfg.pad], s_wf, r_wf.at[f], at_z(4 * f))

    pass_near(0)
    for f in range(1, F):
        if 4 * f != Z // 2:
            pass_far(f)
    pl.semaphore_wait(relay, 2)
    pass_far(F // 2)

    to_new = (z_of * G + g_of) * cap + k_of
    drain(r_a1, in1.at[0 : (G - 1) * cfg.grow])
    out2[...] = dot(onehot(row == to_new), in1[...]).astype(BF)
    here = moved.at[y]
    position = [0] + [2 * o - 1 if o <= Z // 2 else 2 * (Z - o) for o in range(1, Z)]
    quarter = Z // 4
    edges = [0, quarter, 2 * quarter, 3 * quarter, Z - quarter // 2, Z]
    parcel_of = [sum(p >= edge for edge in edges[1:]) for p in range(Z)]
    bounds = [(lo * cfg.zrow, hi * cfg.zrow) for lo, hi in zip(edges, edges[1:])]

    def to_z(parcel_range):
        for o in sorted(range(1, Z), key=lambda o: position[Z - o]):
            p = position[Z - o]
            if parcel_of[p] in parcel_range:
                send(
                    rows_of(out2, mod(z + o, Z) * cfg.zrow, cfg.zrow),
                    here.at[p * cfg.zrow : (p + 1) * cfg.zrow],
                    s_a2, r_a2.at[parcel_of[p]], at_z(o),
                )

    to_z((0, 1))
    here[0 : cfg.zrow, :] = rows_of(out2, z * cfg.zrow, cfg.zrow)[...]

    def spread(f):
        drain(r_wn.at[f], shards.at[f, 0 : 3 * cfg.pad])
        w_own[f, 0] = unpack(cfg, shards[f])
        for k in (2, 1, 3):
            send(w_own.at[f, 0], w_own.at[f, k], s_wx, r_wx.at[f], at_x(k))

    def hand_on(f):
        drain(r_wx.at[f], w_own.at[f, 1:X])
        send(w_own.at[f], w_sib.at[f], s_sib, r_sib.at[f], sibling)

    spread(0)
    for f in (1, 3, 2):
        drain(r_wf.at[f], shards.at[f, cfg.pad : 2 * cfg.pad])
        pass_near(f)
    to_z((2, 3, 4))

    where = lax.div(place, cfg.zrow)
    away = jnp.where(lax.rem(where, 2) == 1, lax.div(where + 1, 2), lax.rem(Z - lax.div(where, 2), Z))
    k_at, g_at = lax.rem(place, cap), lax.rem(lax.div(place, cap), G)
    natural = (
        (lax.div(g_at, CORES) * Z + lax.rem(z + away, Z)) * CORES + lax.rem(g_at, CORES)
    ) * cap + k_at
    back = onehot(row == natural)
    get_cotangent.wait()
    cot[...] = contract_rows(back, cotangent[...]).astype(BF)

    def share(j):
        lo, hi = bounds[j]
        drain(r_a2.at[j], here.at[(lo if j else cfg.zrow) : hi])
        ref = here.at[lo:hi]
        for d in (2, 1, 3):
            send(ref, ref, s_ag, r_ag.at[j], at_y(d))

    def normalize(j):
        start, stop = bounds[j]
        drain(r_ag.at[j], moved.at[0, 0 : (Y - 1) * (stop - start)])
        lines = min(32, stop - start)
        for lo in range(start, stop, lines):
            span = slice(lo, lo + lines)
            parts = [moved[c, span, :].astype(F32) for c in range(Y)]
            mean = sum(jnp.sum(p, axis=1, keepdims=True) for p in parts) / cfg.width
            parts = [p - mean for p in parts]
            var = sum(jnp.sum(jnp.square(p), axis=1, keepdims=True) for p in parts) / cfg.width
            scale = lax.rsqrt(var + 1e-05)
            for c in range(Y):
                normed[span, c * cfg.part : (c + 1) * cfg.part] = (parts[c] * scale).astype(BF)

    q = iota((1, CORES * cfg.comb), 1)
    side = lax.div(q, cfg.comb)
    core_of = core + side - 2 * core * side
    line = lax.div(lax.rem(q, cfg.comb), cfg.own) * cfg.pair + core_of * cfg.own + lax.rem(q, cfg.own)
    spot = onehot(iota((CORES * cfg.comb, CORES * cfg.comb), 0) == line)
    span = Z * cfg.pair

    def put_weights(f):
        drain(r_sib.at[f], w_sib.at[f])
        for k in range(X):
            lines = dot(spot, jnp.concatenate([w_own[f, k], w_sib[f, k]], axis=0))
            for n in range(4):
                chip = mod(x - k, X) * Z + lax.rem(z - (n - 1) - 4 * f + 2 * Z, Z)
                rows_of(staged, chip * cfg.pair, cfg.pair, 8)[...] = lines[n * cfg.pair : (n + 1) * cfg.pair]

    share(0)
    spread(1)
    spread(3)
    share(1)
    spread(2)
    hand_on(0)
    share(2)
    hand_on(1)
    normalize(0)
    share(3)
    hand_on(3)
    share(4)
    hand_on(2)
    normalize(1)
    put_weights(0)
    put_weights(1)
    normalize(2)
    put_weights(3)
    put_weights(2)
    weights[...] = staged[...].astype(BF)

    dglu = dot(cot[...], weights[:, 2 * U : 3 * U])
    normalize(3)
    normalize(4)

    both = dot(normed[...], weights[:, : 2 * U])
    value, gate = both[:, :U], both[:, U : 2 * U]
    sig = jax.nn.sigmoid(gate)
    glu = (value * sig).astype(BF)
    d_value = (dglu * sig).astype(BF)
    d_gate = (dglu * value * sig * (1.0 - sig)).astype(BF)

    d_both = jnp.concatenate([d_value, d_gate], axis=1)
    J = Z // 2 // 4
    steps = (0, 1, -1, 2)
    Q = cfg.pair

    def chunk(o, half, a):
        r = lax.rem(z + a + Z, 4)
        return jnp.concatenate(
            [rows_of(block.at[o], (half * (Z // 2) + r + 4 * j) * Q, Q, 8)[...] for j in range(J)], axis=0
        )

    for o in (2, 1, 3, 0):
        cols = pl.ds(pl.multiple_of(mod(x + o, X) * span, 128), span)
        block[o] = jnp.concatenate(
            [contract_rows(normed[:, cols], d_both), contract_rows(cot[:, cols], glu)], axis=1
        )
        for i, a in enumerate(steps):
            pair_out[o, i] = chunk(o, other, a).astype(BF)
        send(pair_out.at[o], pair_in.at[o], s_pair, r_pair.at[o], sibling)

    B = cfg.yrow
    half_b = B // 2

    def gather(h):
        drain(r_y.at[h], y_in.at[h])
        lines = y_own[h * half_b : (h + 1) * half_b, :]
        for k in range(Y - 1):
            lines = lines + y_in[h, k].astype(F32)
        ref = rows_of(result, y * B + h * half_b, half_b)
        ref[...] = lines.astype(BF)
        for d in (2, 1, 3):
            send(ref, ref, s_yg, r_yg.at[h], at_y(d))

    def put_out(h):
        drain(r_yg.at[h], result.at[0 : (Y - 1) * half_b])
        for i in range(Y):
            lo = i * B + h * half_b
            pltpu.make_async_copy(
                result.at[lo : lo + half_b], branch.at[lo : lo + half_b], s_put
            ).start()

    def to_x(i, o):
        x_out[i, o - 1] = (chunk(o, core, steps[i]) + pair_in[o, i].astype(F32)).astype(BF)
        send(x_out.at[i, o - 1], x_in.at[i, o - 1], s_x, r_x.at[i], at_x(o))

    for o in (2, 1, 3):
        drain(r_pair.at[o], pair_in.at[o])
        to_x(0, o)

    glu_rows[...] = dot(back, glu).astype(BF)
    for d in (2, 1, 3):
        some = rows_of(glu_rows, mod(y + d, Y) * B, B)[...]
        theirs = contract_cols(some, weights[:, 2 * U : 3 * U]).astype(BF)
        for h in range(2):
            y_out[h, d - 1] = theirs[h * half_b : (h + 1) * half_b]
    for h in range(2):
        for d in (2, 1, 3):
            send(y_out.at[h, d - 1], y_in.at[h, d - 1], s_y, r_y.at[h], at_y(d))
    y_own[...] = contract_cols(rows_of(glu_rows, y * B, B)[...], weights[:, 2 * U : 3 * U])

    for i in range(1, 4):
        for o in (2, 1, 3):
            to_x(i, o)
    drain(r_pair.at[0], pair_in.at[0])

    def summed(i, a):
        drain(r_x.at[i], x_in.at[i])
        total = chunk(0, core, a) + pair_in[0, i].astype(F32)
        for k in range(X - 1):
            total = total + x_in[i, k].astype(F32)
        return total

    O = cfg.own
    sends = []

    def to_owners(i):
        a = steps[i]
        total = summed(i, a)
        z_out[i] = pack(cfg, total.astype(BF))
        for j in range(J):
            t = core * (Z // 2) + 4 * j + lax.rem(z + a + Z, 4)
            for c in range(CORES):
                lo = j * CORES + c
                copy = pltpu.make_async_remote_copy(
                    src_ref=z_out.at[i, lo * cfg.pad : (lo + 1) * cfg.pad], dst_ref=z_in.at[mod(z - t, Z)],
                    send_sem=s_own.at[j, c] if a == 0 else s_z, recv_sem=r_z,
                    device_id=at(x, t, c), device_id_type=pl.DeviceIdType.MESH,
                )
                if a == 0:
                    acc[j, c, 0:O, :] = total[lo * O : (lo + 1) * O]
                    sends.append((t != z, copy))
                    pl.when(t != z)(copy.start)
                else:
                    copy.start()

    to_owners(0)
    gather(0)
    to_owners(1)
    to_owners(2)
    gather(1)
    to_owners(3)

    is_owner = lax.div(z, Z // 2) == core
    own_j = lax.rem(lax.div(z, 4), J)
    hand = pltpu.make_async_remote_copy(
        src_ref=acc.at[own_j, other], dst_ref=final, send_sem=s_fin, recv_sem=r_fin,
        device_id=sibling, device_id_type=pl.DeviceIdType.MESH,
    )

    @pl.when(is_owner)
    def _():
        hand.start()
        final[...] = acc[own_j, core]
        hand.wait_send()

    @pl.when(jnp.logical_not(is_owner))
    def _():
        hand.wait_recv()

    put_out(0)
    drain(r_z, z_in.at[1:Z])
    whole = z_in[1].astype(F32)
    for slot in range(2, Z):
        whole = whole + z_in[slot].astype(F32)
    rest = cfg.cols - cfg.main
    tail = []
    for r in range(O):
        lo, line = r % cfg.fold * rest, O + r // cfg.fold
        tail.append(whole[line : line + 1, lo : lo + rest])
    whole = jnp.concatenate([whole[0:O], jnp.concatenate(tail, axis=0)], axis=1)
    last[...] = whole + final[0:O, :]
    put_last = pltpu.make_async_copy(last, owned, s_in.at[0])
    put_last.start()

    put_out(1)

    drain(s_a1, out1.at[0 : (G - 1) * cfg.grow])
    drain(s_a2, out2.at[0 : (Z - 1) * cfg.zrow])
    drain(s_ag, moved.at[0 : Y - 1])
    drain(s_wf, shards.at[0, 0 : (F - 1) * cfg.pad])
    drain(s_wn, shards.at[:, 0 : 3 * cfg.pad])
    drain(s_wx, w_own.at[:, 1:X])
    drain(s_sib, w_own)
    drain(s_pair, pair_out)
    drain(s_x, x_out)
    drain(s_z, z_out.at[1:4])
    drain(s_y, y_out)
    drain(s_yg, result.at[0 : (Y - 1) * B])
    for needed, copy in sends:
        pl.when(needed)(copy.wait_send)
    drain(s_put, result)
    put_last.wait()


def place_results(units, branch_in, owned_in, branch, grad_value, grad_gate, grad_down):
    branch[...] = branch_in[...]
    grad_value[...] = owned_in[:, :units]
    grad_gate[...] = owned_in[:, units : 2 * units]
    grad_down[...] = owned_in[:, 2 * units :]


def module(cfg, frames, lengths, send_order, value_weight, gate_weight, down_weight, cotangent):
    X, Z, Y, G, R, D, U = cfg.X, cfg.Z, cfg.Y, cfg.G, cfg.rows, cfg.width, cfg.units
    C, S, B = cfg.cols, cfg.half, cfg.yrow
    vmem, hbm = pl.BlockSpec(memory_space=pltpu.VMEM), pl.BlockSpec(memory_space=pl.ANY)
    sem = pltpu.SemaphoreType.DMA
    F, J, H = cfg.far, Z // 8, Z // 8 * cfg.pair
    buffers = [
        ((R, cfg.part), BF),
        ((R, D), BF),
        ((R, cfg.part), BF),
        ((R, cfg.part), BF),
        ((R, cfg.part), BF),
        ((Y, R, cfg.part), BF),
        ((R, D), BF),
        ((R, D), BF),
        ((R, U), BF),
        ((F, 4 * cfg.pad, cfg.main), BF),
        ((F, X, cfg.comb, C), BF),
        ((F, X, cfg.comb, C), BF),
        ((D, C), F32),
        ((D, C), BF),
        ((X, Z * cfg.pair, C), F32),
        ((X, 4, H, C), BF),
        ((X, 4, H, C), BF),
        ((4, X - 1, H, C), BF),
        ((4, X - 1, H, C), BF),
        ((4, J * CORES * cfg.pad, cfg.main), BF),
        ((Z, cfg.pad, cfg.main), BF),
        ((J, CORES, cfg.pad, C), F32),
        ((cfg.pad, C), F32),
        ((cfg.own, C), F32),
        ((B, D), F32),
        ((2, Y - 1, B // 2, D), BF),
        ((2, Y - 1, B // 2, D), BF),
        ((R, D), BF),
    ]
    one = ()
    sems = [
        one, one, one, (5,), one, (5,),
        one, (F,), one, (F,), one, (F,), one, (F,),
        one, (X,), one, (4,), one, one, (J, CORES), one, one,
        one, (2,), one, (2,),
    ]
    branch, owned = pl.pallas_call(
        functools.partial(kernel, cfg),
        out_shape=(jax.ShapeDtypeStruct((R, D), BF), jax.ShapeDtypeStruct((cfg.own, C), F32)),
        in_specs=[pl.BlockSpec(memory_space=pltpu.SMEM), vmem, hbm, vmem, vmem, vmem, hbm],
        out_specs=(hbm, hbm),
        scratch_shapes=[pltpu.VMEM(shape, kind) for shape, kind in buffers]
        + [sem(n) for n in sems]
        + [pltpu.SemaphoreType.REGULAR, sem((2,)), sem(one)],
        compiler_params=pltpu.CompilerParams(
            collective_id=0, has_side_effects=True, vmem_limit_bytes=56 * 1024 * 1024
        ),
    )(lengths, send_order, frames, value_weight, gate_weight, down_weight, cotangent)
    return pl.pallas_call(
        functools.partial(place_results, U),
        out_shape=(jax.ShapeDtypeStruct((R, D), BF),) + (jax.ShapeDtypeStruct((cfg.own, U), F32),) * 3,
        in_specs=[vmem] * 2,
        out_specs=(vmem,) * 4,
    )(branch, owned)


def build(mesh, X, Z):
    def shards(frames, lengths, send_order, value_weight, gate_weight, down_weight, cotangent):
        cfg = Sizes(
            X, Z, mesh.shape["mp"], frames.shape[0], frames.shape[1],
            value_weight.shape[0], value_weight.shape[1],
        )
        return module(
            cfg, frames, lengths, send_order, value_weight, gate_weight, down_weight, cotangent
        )

    return jax.shard_map(
        shards,
        mesh=mesh,
        in_specs=(
            P("dp", None),
            P("dp"),
            P("dp", None),
            P("dp", "mp"),
            P("dp", "mp"),
            P("dp", "mp"),
            P("dp", None),
        ),
        out_specs=(P("dp", None), P("dp", "mp"), P("dp", "mp"), P("dp", "mp")),
        check_vma=False,
    )


def solution(mesh):
    return build(mesh, 4, 16)
```

```python
import functools

import jax
import jax.numpy as jnp
from jax import lax
from jax.experimental import pallas as pl
from jax.experimental.pallas import tpu as pltpu
from jax.sharding import PartitionSpec as P

CORES = 2
BF = jnp.bfloat16
F32 = jnp.float32


def ceil16(rows):
    return -(-rows // 16) * 16


def iota(shape, axis):
    return lax.broadcasted_iota(jnp.int32, shape, axis)


def onehot(hit):
    return jnp.where(hit, 1.0, 0.0).astype(BF)


def dot(left, right):
    return jnp.dot(left, right, preferred_element_type=F32)


def contract_rows(left, right):
    return lax.dot_general(left, right, (((0,), (0,)), ((), ())), preferred_element_type=F32)


def contract_cols(left, right):
    return lax.dot_general(left, right, (((1,), (1,)), ((), ())), preferred_element_type=F32)


def mod(value, count):
    return lax.rem(value + count, count)


class Sizes:
    def __init__(self, X, Z, Y, rows, width, own, units):
        self.X, self.Z, self.Y = X, Z, Y
        self.G = X * CORES
        self.rows, self.width, self.own, self.units = rows, width, own, units
        self.cap = rows // (X * Z * CORES)
        self.part = width // Y
        self.pad = ceil16(own)
        self.zrow = self.G * self.cap
        self.grow = self.Z * self.cap
        self.far = Z // 4
        self.comb = 4 * own
        self.pair = CORES * own
        self.cols = 3 * units
        self.main = self.cols // 128 * 128
        self.fold = own // (self.pad - own)
        self.half = Z // 2 * self.pair
        self.yrow = rows // Y


def pack(cfg, lines):
    own, pad, main, fold = cfg.own, cfg.pad, cfg.main, cfg.fold
    count = lines.shape[0] // own
    q = iota((1, count * own), 1)
    m, r = lax.div(q, own), lax.rem(q, own)
    p = iota((count * pad, count * own), 0)
    body = dot(onehot(p == m * pad + r), lines[:, :main])
    tails = [
        dot(onehot(p == jnp.where(lax.rem(r, fold) == s, m * pad + own + lax.div(r, fold), -1)), lines[:, main:])
        for s in range(fold)
    ]
    wide = -(-fold * (cfg.cols - main) // 128) * 128
    tails.append(jnp.zeros((count * pad, wide - fold * (cfg.cols - main)), F32))
    tail = jnp.concatenate(tails, axis=1)
    return jnp.concatenate([body[:, :wide] + tail, body[:, wide:]], axis=1).astype(BF)


def unpack(cfg, lines):
    own, pad, main, fold = cfg.own, cfg.pad, cfg.main, cfg.fold
    count, rest = lines.shape[0] // pad, cfg.cols - main
    q = iota((1, count * pad), 1)
    m, r = lax.div(q, pad), lax.rem(q, pad)
    p = iota((count * own, count * pad), 0)
    body = dot(onehot(p == jnp.where(r < own, m * own + r, -1)), lines)
    tail = sum(
        dot(onehot(p == jnp.where(r < own, -1, m * own + (r - own) * fold + s)), lines[:, s * rest : (s + 1) * rest])
        for s in range(fold)
    )
    return jnp.concatenate([body, tail], axis=1).astype(BF)


def kernel(
    cfg,
    lengths, send_order, frames_all, value_w, gate_w, down_w, cotangent_all,
    branch, owned,
    frames, cotangent, out1, in1, out2, moved, normed, cot, glu_rows,
    shards, w_own, w_sib, staged, weights,
    block, pair_out, pair_in, x_out, x_in, z_out, z_in, acc, final, last,
    y_own, y_out, y_in, result,
    s_a1, r_a1, s_a2, r_a2, s_ag, r_ag,
    s_wf, r_wf, s_wn, r_wn, s_wx, r_wx, s_sib, r_sib,
    s_pair, r_pair, s_x, r_x, s_z, r_z, s_own, s_fin, r_fin, s_y, r_y, s_yg, r_yg,
    relay, s_in, s_put,
):
    X, Z, Y, G = cfg.X, cfg.Z, cfg.Y, cfg.G
    R, U, F, cap = cfg.rows, cfg.units, cfg.far, cfg.cap
    dp = lax.axis_index("dp")
    y = lax.axis_index("mp")
    core = lax.rem(dp, CORES)
    z = lax.rem(lax.div(dp, CORES), Z)
    x = lax.div(dp, CORES * Z)
    g = x * CORES + core
    other = 1 - core
    sibling = {"dp": dp + 1 - 2 * core, "mp": y}

    def at(x_, z_, core_):
        return {"dp": (x_ * Z + z_) * CORES + core_, "mp": y}

    def at_x(o):
        return at(mod(x + o, X), z, core)

    def at_z(o):
        return at(x, mod(z + o, Z), core)

    def at_y(o):
        return {"dp": dp, "mp": mod(y + o, Y)}

    def at_g(t):
        return at(lax.div(t, CORES), z, lax.rem(t, CORES))

    def send(src, dst, sent, arrived, where):
        copy = pltpu.make_async_remote_copy(
            src_ref=src, dst_ref=dst, send_sem=sent, recv_sem=arrived,
            device_id=where, device_id_type=pl.DeviceIdType.MESH,
        )
        copy.start()

    def drain(sem, ref):
        pltpu.make_async_copy(ref, ref, sem).wait()

    def rows_of(ref, start, size, step=16):
        return ref.at[pl.ds(pl.multiple_of(start, step), size)]

    barrier = pltpu.get_barrier_semaphore()
    partners = [at_g(mod(g + o, G)) for o in range(1, G)]
    partners += [at_z(o * s) for o in range(1, 5) for s in (1, -1)]
    partners += [at_y(o) for o in range(1, Y)]
    for who in partners:
        pl.semaphore_signal(barrier, inc=1, device_id=who, device_id_type=pl.DeviceIdType.MESH)

    columns = pl.ds(pl.multiple_of(y * cfg.part, 128), cfg.part)
    get_frames = pltpu.make_async_copy(frames_all.at[:, columns], frames, s_in.at[0])
    get_frames.start()
    get_cotangent = pltpu.make_async_copy(cotangent_all, cotangent, s_in.at[1])
    get_cotangent.start()

    packed = jnp.concatenate([value_w[...], gate_w[...], down_w[...]], axis=1)
    mine = shards.at[0, cfg.pad : 2 * cfg.pad]
    mine[...] = pack(cfg, packed)

    row, place = iota((R, R), 0), iota((1, R), 1)
    k_of, z_of, g_of = lax.rem(place, cap), lax.rem(lax.div(place, cap), Z), lax.div(place, cap * Z)
    natural = ((lax.div(g_of, CORES) * Z + z_of) * CORES + lax.rem(g_of, CORES)) * cap + k_of
    numbers = jnp.broadcast_to(send_order[...].astype(F32).astype(BF), (16, R))
    order = dot(numbers, onehot(row == natural))[0:1, :]
    pick = onehot((row.astype(F32) == order) & (row < lengths[0]))
    get_frames.wait()
    out1[...] = contract_rows(pick, frames[...]).astype(BF)

    pl.semaphore_wait(barrier, len(partners))
    for o in (4, -4):
        pl.semaphore_signal(relay, inc=1, device_id=at_z(o), device_id_type=pl.DeviceIdType.MESH)

    for o in range(1, G):
        t = mod(g + o, G)
        send(
            rows_of(out1, t * cfg.grow, cfg.grow), rows_of(in1, g * cfg.grow, cfg.grow),
            s_a1, r_a1, at_g(t),
        )
    rows_of(in1, g * cfg.grow, cfg.grow)[...] = rows_of(out1, g * cfg.grow, cfg.grow)[...]

    near = (1, -1, 2)

    def pass_near(f):
        ref = shards.at[f, cfg.pad : 2 * cfg.pad]
        for a in near:
            lo = (a + 1) * cfg.pad
            send(ref, shards.at[f, lo : lo + cfg.pad], s_wn, r_wn.at[f], at_z(a))

    def pass_far(f):
        send(mine, shards.at[f, cfg.pad : 2 * cfg.pad], s_wf, r_wf.at[f], at_z(4 * f))

    pass_near(0)
    for f in range(1, F):
        if 4 * f != Z // 2:
            pass_far(f)
    pl.semaphore_wait(relay, 2)
    pass_far(F // 2)

    to_new = (z_of * G + g_of) * cap + k_of
    drain(r_a1, in1.at[0 : (G - 1) * cfg.grow])
    out2[...] = dot(onehot(row == to_new), in1[...]).astype(BF)
    here = moved.at[y]
    position = [0] + [2 * o - 1 if o <= Z // 2 else 2 * (Z - o) for o in range(1, Z)]
    quarter = Z // 4
    edges = [0, quarter, 2 * quarter, 3 * quarter, Z - quarter // 2, Z]
    parcel_of = [sum(p >= edge for edge in edges[1:]) for p in range(Z)]
    bounds = [(lo * cfg.zrow, hi * cfg.zrow) for lo, hi in zip(edges, edges[1:])]

    def to_z(parcel_range):
        for o in sorted(range(1, Z), key=lambda o: position[Z - o]):
            p = position[Z - o]
            if parcel_of[p] in parcel_range:
                send(
                    rows_of(out2, mod(z + o, Z) * cfg.zrow, cfg.zrow),
                    here.at[p * cfg.zrow : (p + 1) * cfg.zrow],
                    s_a2, r_a2.at[parcel_of[p]], at_z(o),
                )

    to_z((0, 1))
    here[0 : cfg.zrow, :] = rows_of(out2, z * cfg.zrow, cfg.zrow)[...]

    def spread(f):
        drain(r_wn.at[f], shards.at[f, 0 : 3 * cfg.pad])
        w_own[f, 0] = unpack(cfg, shards[f])
        for k in (2, 1, 3):
            send(w_own.at[f, 0], w_own.at[f, k], s_wx, r_wx.at[f], at_x(k))

    def hand_on(f):
        drain(r_wx.at[f], w_own.at[f, 1:X])
        send(w_own.at[f], w_sib.at[f], s_sib, r_sib.at[f], sibling)

    spread(0)
    for f in (1, 3, 2):
        drain(r_wf.at[f], shards.at[f, cfg.pad : 2 * cfg.pad])
        pass_near(f)
    to_z((2, 3, 4))

    where = lax.div(place, cfg.zrow)
    away = jnp.where(lax.rem(where, 2) == 1, lax.div(where + 1, 2), lax.rem(Z - lax.div(where, 2), Z))
    k_at, g_at = lax.rem(place, cap), lax.rem(lax.div(place, cap), G)
    natural = (
        (lax.div(g_at, CORES) * Z + lax.rem(z + away, Z)) * CORES + lax.rem(g_at, CORES)
    ) * cap + k_at
    back = onehot(row == natural)
    get_cotangent.wait()
    cot[...] = contract_rows(back, cotangent[...]).astype(BF)

    def share(j):
        lo, hi = bounds[j]
        drain(r_a2.at[j], here.at[(lo if j else cfg.zrow) : hi])
        ref = here.at[lo:hi]
        for d in (2, 1, 3):
            send(ref, ref, s_ag, r_ag.at[j], at_y(d))

    def normalize(j):
        start, stop = bounds[j]
        drain(r_ag.at[j], moved.at[0, 0 : (Y - 1) * (stop - start)])
        lines = min(32, stop - start)
        for lo in range(start, stop, lines):
            span = slice(lo, lo + lines)
            parts = [moved[c, span, :].astype(F32) for c in range(Y)]
            mean = sum(jnp.sum(p, axis=1, keepdims=True) for p in parts) / cfg.width
            parts = [p - mean for p in parts]
            var = sum(jnp.sum(jnp.square(p), axis=1, keepdims=True) for p in parts) / cfg.width
            scale = lax.rsqrt(var + 1e-05)
            for c in range(Y):
                normed[span, c * cfg.part : (c + 1) * cfg.part] = (parts[c] * scale).astype(BF)

    q = iota((1, CORES * cfg.comb), 1)
    side = lax.div(q, cfg.comb)
    core_of = core + side - 2 * core * side
    line = lax.div(lax.rem(q, cfg.comb), cfg.own) * cfg.pair + core_of * cfg.own + lax.rem(q, cfg.own)
    spot = onehot(iota((CORES * cfg.comb, CORES * cfg.comb), 0) == line)
    span = Z * cfg.pair

    def put_weights(f):
        drain(r_sib.at[f], w_sib.at[f])
        for k in range(X):
            lines = dot(spot, jnp.concatenate([w_own[f, k], w_sib[f, k]], axis=0))
            for n in range(4):
                chip = mod(x - k, X) * Z + lax.rem(z - (n - 1) - 4 * f + 2 * Z, Z)
                rows_of(staged, chip * cfg.pair, cfg.pair, 8)[...] = lines[n * cfg.pair : (n + 1) * cfg.pair]

    share(0)
    spread(1)
    spread(3)
    share(1)
    spread(2)
    hand_on(0)
    share(2)
    hand_on(1)
    normalize(0)
    share(3)
    hand_on(3)
    share(4)
    hand_on(2)
    normalize(1)
    put_weights(0)
    put_weights(1)
    normalize(2)
    put_weights(3)
    put_weights(2)
    weights[...] = staged[...].astype(BF)

    dglu = dot(cot[...], weights[:, 2 * U : 3 * U])
    normalize(3)
    normalize(4)

    both = dot(normed[...], weights[:, : 2 * U])
    value, gate = both[:, :U], both[:, U : 2 * U]
    sig = jax.nn.sigmoid(gate)
    glu = (value * sig).astype(BF)
    d_value = (dglu * sig).astype(BF)
    d_gate = (dglu * value * sig * (1.0 - sig)).astype(BF)

    d_both = jnp.concatenate([d_value, d_gate], axis=1)
    J = Z // 2 // 4
    steps = (0, 1, -1, 2)
    Q = cfg.pair

    def chunk(o, half, a):
        r = lax.rem(z + a + Z, 4)
        return jnp.concatenate(
            [rows_of(block.at[o], (half * (Z // 2) + r + 4 * j) * Q, Q, 8)[...] for j in range(J)], axis=0
        )

    def gradients(o):
        cols = pl.ds(pl.multiple_of(mod(x + o, X) * span, 128), span)
        block[o] = jnp.concatenate(
            [contract_rows(normed[:, cols], d_both), contract_rows(cot[:, cols], glu)], axis=1
        )
        for i, a in enumerate(steps):
            pair_out[o, i] = chunk(o, other, a).astype(BF)
        send(pair_out.at[o], pair_in.at[o], s_pair, r_pair.at[o], sibling)

    for o in (2, 1, 3):
        gradients(o)

    B = cfg.yrow
    half_b = B // 2

    glu_rows[...] = dot(back, glu).astype(BF)
    for d in (2, 1, 3):
        some = rows_of(glu_rows, mod(y + d, Y) * B, B)[...]
        theirs = contract_cols(some, weights[:, 2 * U : 3 * U]).astype(BF)
        for h in range(2):
            y_out[h, d - 1] = theirs[h * half_b : (h + 1) * half_b]
    for h in range(2):
        for d in (2, 1, 3):
            send(y_out.at[h, d - 1], y_in.at[h, d - 1], s_y, r_y.at[h], at_y(d))
    y_own[...] = contract_cols(rows_of(glu_rows, y * B, B)[...], weights[:, 2 * U : 3 * U])

    gradients(0)

    def gather(h):
        drain(r_y.at[h], y_in.at[h])
        lines = y_own[h * half_b : (h + 1) * half_b, :]
        for k in range(Y - 1):
            lines = lines + y_in[h, k].astype(F32)
        ref = rows_of(result, y * B + h * half_b, half_b)
        ref[...] = lines.astype(BF)
        for d in (2, 1, 3):
            send(ref, ref, s_yg, r_yg.at[h], at_y(d))

    def put_out(h):
        drain(r_yg.at[h], result.at[0 : (Y - 1) * half_b])
        for i in range(Y):
            lo = i * B + h * half_b
            pltpu.make_async_copy(
                result.at[lo : lo + half_b], branch.at[lo : lo + half_b], s_put
            ).start()

    def to_x(i, o):
        x_out[i, o - 1] = (chunk(o, core, steps[i]) + pair_in[o, i].astype(F32)).astype(BF)
        send(x_out.at[i, o - 1], x_in.at[i, o - 1], s_x, r_x.at[i], at_x(o))

    for o in (2, 1, 3):
        drain(r_pair.at[o], pair_in.at[o])
        to_x(0, o)

    for i in range(1, 4):
        for o in (2, 1, 3):
            to_x(i, o)
    drain(r_pair.at[0], pair_in.at[0])

    def summed(i, a):
        drain(r_x.at[i], x_in.at[i])
        total = chunk(0, core, a) + pair_in[0, i].astype(F32)
        for k in range(X - 1):
            total = total + x_in[i, k].astype(F32)
        return total

    O = cfg.own
    sends = []

    def to_owners(i):
        a = steps[i]
        total = summed(i, a)
        z_out[i] = pack(cfg, total.astype(BF))
        for j in range(J):
            t = core * (Z // 2) + 4 * j + lax.rem(z + a + Z, 4)
            for c in range(CORES):
                lo = j * CORES + c
                copy = pltpu.make_async_remote_copy(
                    src_ref=z_out.at[i, lo * cfg.pad : (lo + 1) * cfg.pad], dst_ref=z_in.at[mod(z - t, Z)],
                    send_sem=s_own.at[j, c] if a == 0 else s_z, recv_sem=r_z,
                    device_id=at(x, t, c), device_id_type=pl.DeviceIdType.MESH,
                )
                if a == 0:
                    acc[j, c, 0:O, :] = total[lo * O : (lo + 1) * O]
                    sends.append((t != z, copy))
                    pl.when(t != z)(copy.start)
                else:
                    copy.start()

    to_owners(0)
    gather(0)
    to_owners(1)
    to_owners(2)
    gather(1)
    to_owners(3)

    is_owner = lax.div(z, Z // 2) == core
    own_j = lax.rem(lax.div(z, 4), J)
    hand = pltpu.make_async_remote_copy(
        src_ref=acc.at[own_j, other], dst_ref=final, send_sem=s_fin, recv_sem=r_fin,
        device_id=sibling, device_id_type=pl.DeviceIdType.MESH,
    )

    @pl.when(is_owner)
    def _():
        hand.start()
        final[...] = acc[own_j, core]
        hand.wait_send()

    @pl.when(jnp.logical_not(is_owner))
    def _():
        hand.wait_recv()

    put_out(0)
    drain(r_z, z_in.at[1:Z])
    whole = z_in[1].astype(F32)
    for slot in range(2, Z):
        whole = whole + z_in[slot].astype(F32)
    rest = cfg.cols - cfg.main
    tail = []
    for r in range(O):
        lo, line = r % cfg.fold * rest, O + r // cfg.fold
        tail.append(whole[line : line + 1, lo : lo + rest])
    whole = jnp.concatenate([whole[0:O], jnp.concatenate(tail, axis=0)], axis=1)
    last[...] = whole + final[0:O, :]
    put_last = pltpu.make_async_copy(last, owned, s_in.at[0])
    put_last.start()

    put_out(1)

    drain(s_a1, out1.at[0 : (G - 1) * cfg.grow])
    drain(s_a2, out2.at[0 : (Z - 1) * cfg.zrow])
    drain(s_ag, moved.at[0 : Y - 1])
    drain(s_wf, shards.at[0, 0 : (F - 1) * cfg.pad])
    drain(s_wn, shards.at[:, 0 : 3 * cfg.pad])
    drain(s_wx, w_own.at[:, 1:X])
    drain(s_sib, w_own)
    drain(s_pair, pair_out)
    drain(s_x, x_out)
    drain(s_z, z_out.at[1:4])
    drain(s_y, y_out)
    drain(s_yg, result.at[0 : (Y - 1) * B])
    for needed, copy in sends:
        pl.when(needed)(copy.wait_send)
    drain(s_put, result)
    put_last.wait()


def place_results(units, branch_in, owned_in, branch, grad_value, grad_gate, grad_down):
    branch[...] = branch_in[...]
    grad_value[...] = owned_in[:, :units]
    grad_gate[...] = owned_in[:, units : 2 * units]
    grad_down[...] = owned_in[:, 2 * units :]


def module(cfg, frames, lengths, send_order, value_weight, gate_weight, down_weight, cotangent):
    X, Z, Y, G, R, D, U = cfg.X, cfg.Z, cfg.Y, cfg.G, cfg.rows, cfg.width, cfg.units
    C, S, B = cfg.cols, cfg.half, cfg.yrow
    vmem, hbm = pl.BlockSpec(memory_space=pltpu.VMEM), pl.BlockSpec(memory_space=pl.ANY)
    sem = pltpu.SemaphoreType.DMA
    F, J, H = cfg.far, Z // 8, Z // 8 * cfg.pair
    buffers = [
        ((R, cfg.part), BF),
        ((R, D), BF),
        ((R, cfg.part), BF),
        ((R, cfg.part), BF),
        ((R, cfg.part), BF),
        ((Y, R, cfg.part), BF),
        ((R, D), BF),
        ((R, D), BF),
        ((R, U), BF),
        ((F, 4 * cfg.pad, cfg.main), BF),
        ((F, X, cfg.comb, C), BF),
        ((F, X, cfg.comb, C), BF),
        ((D, C), F32),
        ((D, C), BF),
        ((X, Z * cfg.pair, C), F32),
        ((X, 4, H, C), BF),
        ((X, 4, H, C), BF),
        ((4, X - 1, H, C), BF),
        ((4, X - 1, H, C), BF),
        ((4, J * CORES * cfg.pad, cfg.main), BF),
        ((Z, cfg.pad, cfg.main), BF),
        ((J, CORES, cfg.pad, C), F32),
        ((cfg.pad, C), F32),
        ((cfg.own, C), F32),
        ((B, D), F32),
        ((2, Y - 1, B // 2, D), BF),
        ((2, Y - 1, B // 2, D), BF),
        ((R, D), BF),
    ]
    one = ()
    sems = [
        one, one, one, (5,), one, (5,),
        one, (F,), one, (F,), one, (F,), one, (F,),
        one, (X,), one, (4,), one, one, (J, CORES), one, one,
        one, (2,), one, (2,),
    ]
    branch, owned = pl.pallas_call(
        functools.partial(kernel, cfg),
        out_shape=(jax.ShapeDtypeStruct((R, D), BF), jax.ShapeDtypeStruct((cfg.own, C), F32)),
        in_specs=[pl.BlockSpec(memory_space=pltpu.SMEM), vmem, hbm, vmem, vmem, vmem, hbm],
        out_specs=(hbm, hbm),
        scratch_shapes=[pltpu.VMEM(shape, kind) for shape, kind in buffers]
        + [sem(n) for n in sems]
        + [pltpu.SemaphoreType.REGULAR, sem((2,)), sem(one)],
        compiler_params=pltpu.CompilerParams(
            collective_id=0, has_side_effects=True, vmem_limit_bytes=56 * 1024 * 1024
        ),
    )(lengths, send_order, frames, value_weight, gate_weight, down_weight, cotangent)
    return pl.pallas_call(
        functools.partial(place_results, U),
        out_shape=(jax.ShapeDtypeStruct((R, D), BF),) + (jax.ShapeDtypeStruct((cfg.own, U), F32),) * 3,
        in_specs=[vmem] * 2,
        out_specs=(vmem,) * 4,
    )(branch, owned)


def build(mesh, X, Z):
    def shards(frames, lengths, send_order, value_weight, gate_weight, down_weight, cotangent):
        cfg = Sizes(
            X, Z, mesh.shape["mp"], frames.shape[0], frames.shape[1],
            value_weight.shape[0], value_weight.shape[1],
        )
        return module(
            cfg, frames, lengths, send_order, value_weight, gate_weight, down_weight, cotangent
        )

    return jax.shard_map(
        shards,
        mesh=mesh,
        in_specs=(
            P("dp", None),
            P("dp"),
            P("dp", None),
            P("dp", "mp"),
            P("dp", "mp"),
            P("dp", "mp"),
            P("dp", None),
        ),
        out_specs=(P("dp", None), P("dp", "mp"), P("dp", "mp"), P("dp", "mp")),
        check_vma=False,
    )


def solution(mesh):
    return build(mesh, 4, 16)
```

```python
import functools

import jax
import jax.numpy as jnp
from jax import lax
from jax.experimental import pallas as pl
from jax.experimental.pallas import tpu as pltpu
from jax.sharding import PartitionSpec as P

CORES = 2
BF = jnp.bfloat16
F32 = jnp.float32


def ceil16(rows):
    return -(-rows // 16) * 16


def iota(shape, axis):
    return lax.broadcasted_iota(jnp.int32, shape, axis)


def onehot(hit):
    return jnp.where(hit, 1.0, 0.0).astype(BF)


def dot(left, right):
    return jnp.dot(left, right, preferred_element_type=F32)


def contract_rows(left, right):
    return lax.dot_general(left, right, (((0,), (0,)), ((), ())), preferred_element_type=F32)


def contract_cols(left, right):
    return lax.dot_general(left, right, (((1,), (1,)), ((), ())), preferred_element_type=F32)


def mod(value, count):
    return lax.rem(value + count, count)


class Sizes:
    def __init__(self, X, Z, Y, rows, width, own, units):
        self.X, self.Z, self.Y = X, Z, Y
        self.G = X * CORES
        self.rows, self.width, self.own, self.units = rows, width, own, units
        self.cap = rows // (X * Z * CORES)
        self.part = width // Y
        self.pad = ceil16(own)
        self.zrow = self.G * self.cap
        self.grow = self.Z * self.cap
        self.far = Z // 4
        self.comb = 4 * own
        self.pair = CORES * own
        self.cols = 3 * units
        self.main = self.cols // 128 * 128
        self.fold = own // (self.pad - own)
        self.half = Z // 2 * self.pair
        self.yrow = rows // Y


def pack(cfg, lines):
    own, pad, main, fold = cfg.own, cfg.pad, cfg.main, cfg.fold
    count = lines.shape[0] // own
    q = iota((1, count * own), 1)
    m, r = lax.div(q, own), lax.rem(q, own)
    p = iota((count * pad, count * own), 0)
    body = dot(onehot(p == m * pad + r), lines[:, :main])
    tails = [
        dot(onehot(p == jnp.where(lax.rem(r, fold) == s, m * pad + own + lax.div(r, fold), -1)), lines[:, main:])
        for s in range(fold)
    ]
    wide = -(-fold * (cfg.cols - main) // 128) * 128
    tails.append(jnp.zeros((count * pad, wide - fold * (cfg.cols - main)), F32))
    tail = jnp.concatenate(tails, axis=1)
    return jnp.concatenate([body[:, :wide] + tail, body[:, wide:]], axis=1).astype(BF)


def unpack(cfg, lines):
    own, pad, main, fold = cfg.own, cfg.pad, cfg.main, cfg.fold
    count, rest = lines.shape[0] // pad, cfg.cols - main
    q = iota((1, count * pad), 1)
    m, r = lax.div(q, pad), lax.rem(q, pad)
    p = iota((count * own, count * pad), 0)
    body = dot(onehot(p == jnp.where(r < own, m * own + r, -1)), lines)
    tail = sum(
        dot(onehot(p == jnp.where(r < own, -1, m * own + (r - own) * fold + s)), lines[:, s * rest : (s + 1) * rest])
        for s in range(fold)
    )
    return jnp.concatenate([body, tail], axis=1).astype(BF)


def kernel(
    cfg,
    lengths, send_order, frames_all, value_w, gate_w, down_w, cotangent_all,
    branch, owned,
    frames, cotangent, out1, in1, out2, moved, normed, cot, glu_rows,
    shards, w_own, w_sib, staged, weights, down,
    block, pair_out, pair_in, x_out, x_in, z_out, z_in, acc, final, last,
    y_own, y_out, y_in, result,
    s_a1, r_a1, s_a2, r_a2, s_ag, r_ag,
    s_wf, r_wf, s_wn, r_wn, s_wx, r_wx, s_sib, r_sib,
    s_pair, r_pair, s_x, r_x, s_z, r_z, s_own, s_fin, r_fin, s_y, r_y, s_yg, r_yg,
    relay, s_in, s_put,
):
    X, Z, Y, G = cfg.X, cfg.Z, cfg.Y, cfg.G
    R, U, F, cap = cfg.rows, cfg.units, cfg.far, cfg.cap
    dp = lax.axis_index("dp")
    y = lax.axis_index("mp")
    core = lax.rem(dp, CORES)
    z = lax.rem(lax.div(dp, CORES), Z)
    x = lax.div(dp, CORES * Z)
    g = x * CORES + core
    other = 1 - core
    sibling = {"dp": dp + 1 - 2 * core, "mp": y}

    def at(x_, z_, core_):
        return {"dp": (x_ * Z + z_) * CORES + core_, "mp": y}

    def at_x(o):
        return at(mod(x + o, X), z, core)

    def at_z(o):
        return at(x, mod(z + o, Z), core)

    def at_y(o):
        return {"dp": dp, "mp": mod(y + o, Y)}

    def at_g(t):
        return at(lax.div(t, CORES), z, lax.rem(t, CORES))

    def send(src, dst, sent, arrived, where):
        copy = pltpu.make_async_remote_copy(
            src_ref=src, dst_ref=dst, send_sem=sent, recv_sem=arrived,
            device_id=where, device_id_type=pl.DeviceIdType.MESH,
        )
        copy.start()

    def drain(sem, ref):
        pltpu.make_async_copy(ref, ref, sem).wait()

    def rows_of(ref, start, size, step=16):
        return ref.at[pl.ds(pl.multiple_of(start, step), size)]

    barrier = pltpu.get_barrier_semaphore()
    around = (4, 5, 2, 3, 6, 7, 1)
    partners = [at_z(o * s) for o in (4, 3) for s in (1, -1)]
    partners += [at_g(mod(g + o, G)) for o in around]
    partners += [at_z(o * s) for o in (2, 1) for s in (1, -1)]
    partners += [at_y(o) for o in range(1, Y)]
    for who in partners:
        pl.semaphore_signal(barrier, inc=1, device_id=who, device_id_type=pl.DeviceIdType.MESH)

    columns = pl.ds(pl.multiple_of(y * cfg.part, 128), cfg.part)
    get_frames = pltpu.make_async_copy(frames_all.at[:, columns], frames, s_in.at[0])
    get_frames.start()
    get_cotangent = pltpu.make_async_copy(cotangent_all, cotangent, s_in.at[1])
    get_cotangent.start()

    packed = jnp.concatenate([value_w[...], gate_w[...], down_w[...]], axis=1)
    mine = shards.at[0, cfg.pad : 2 * cfg.pad]
    mine[...] = pack(cfg, packed)

    row, place = iota((R, R), 0), iota((1, R), 1)
    k_of, z_of, g_of = lax.rem(place, cap), lax.rem(lax.div(place, cap), Z), lax.div(place, cap * Z)
    natural = ((lax.div(g_of, CORES) * Z + z_of) * CORES + lax.rem(g_of, CORES)) * cap + k_of
    numbers = jnp.broadcast_to(send_order[...].astype(F32).astype(BF), (16, R))
    order = dot(numbers, onehot(row == natural))[0:1, :]
    pick = onehot((row.astype(F32) == order) & (row < lengths[0]))
    get_frames.wait()
    out1[...] = contract_rows(pick, frames[...]).astype(BF)

    pl.semaphore_wait(barrier, len(partners))
    for o in (4, -4):
        pl.semaphore_signal(relay, inc=1, device_id=at_z(o), device_id_type=pl.DeviceIdType.MESH)

    for o in around:
        t = mod(g + o, G)
        send(
            rows_of(out1, t * cfg.grow, cfg.grow), rows_of(in1, g * cfg.grow, cfg.grow),
            s_a1, r_a1, at_g(t),
        )
    rows_of(in1, g * cfg.grow, cfg.grow)[...] = rows_of(out1, g * cfg.grow, cfg.grow)[...]

    near = (1, -1, 2)

    def pass_near(f):
        ref = shards.at[f, cfg.pad : 2 * cfg.pad]
        for a in near:
            lo = (a + 1) * cfg.pad
            send(ref, shards.at[f, lo : lo + cfg.pad], s_wn, r_wn.at[f], at_z(a))

    def pass_far(f):
        send(mine, shards.at[f, cfg.pad : 2 * cfg.pad], s_wf, r_wf.at[f], at_z(4 * f))

    pass_near(0)
    for f in range(1, F):
        if 4 * f != Z // 2:
            pass_far(f)
    pl.semaphore_wait(relay, 2)
    pass_far(F // 2)

    to_new = (z_of * G + g_of) * cap + k_of
    drain(r_a1, in1.at[0 : (G - 1) * cfg.grow])
    out2[...] = dot(onehot(row == to_new), in1[...]).astype(BF)
    here = moved.at[y]
    position = [0] + [2 * o - 1 if o <= Z // 2 else 2 * (Z - o) for o in range(1, Z)]
    quarter = Z // 4
    edges = [0, quarter, 2 * quarter, 3 * quarter, Z - quarter // 2, Z]
    parcel_of = [sum(p >= edge for edge in edges[1:]) for p in range(Z)]
    bounds = [(lo * cfg.zrow, hi * cfg.zrow) for lo, hi in zip(edges, edges[1:])]

    def to_z(parcel_range):
        for o in sorted(range(1, Z), key=lambda o: position[Z - o]):
            p = position[Z - o]
            if parcel_of[p] in parcel_range:
                send(
                    rows_of(out2, mod(z + o, Z) * cfg.zrow, cfg.zrow),
                    here.at[p * cfg.zrow : (p + 1) * cfg.zrow],
                    s_a2, r_a2.at[parcel_of[p]], at_z(o),
                )

    to_z((0, 1))
    here[0 : cfg.zrow, :] = rows_of(out2, z * cfg.zrow, cfg.zrow)[...]

    def spread(f):
        drain(r_wn.at[f], shards.at[f, 0 : 3 * cfg.pad])
        w_own[f, 0] = unpack(cfg, shards[f])
        for k in (2, 1, 3):
            send(w_own.at[f, 0], w_own.at[f, k], s_wx, r_wx.at[f], at_x(k))

    def hand_on(f):
        drain(r_wx.at[f], w_own.at[f, 1:X])
        send(w_own.at[f], w_sib.at[f], s_sib, r_sib.at[f], sibling)

    spread(0)
    for f in (1, 3, 2):
        drain(r_wf.at[f], shards.at[f, cfg.pad : 2 * cfg.pad])
        pass_near(f)
    to_z((2, 3, 4))

    where = lax.div(place, cfg.zrow)
    away = jnp.where(lax.rem(where, 2) == 1, lax.div(where + 1, 2), lax.rem(Z - lax.div(where, 2), Z))
    k_at, g_at = lax.rem(place, cap), lax.rem(lax.div(place, cap), G)
    natural = (
        (lax.div(g_at, CORES) * Z + lax.rem(z + away, Z)) * CORES + lax.rem(g_at, CORES)
    ) * cap + k_at
    back = onehot(row == natural)
    get_cotangent.wait()
    cot[...] = contract_rows(back, cotangent[...]).astype(BF)

    def share(j):
        lo, hi = bounds[j]
        drain(r_a2.at[j], here.at[(lo if j else cfg.zrow) : hi])
        ref = here.at[lo:hi]
        for d in (2, 1, 3):
            send(ref, ref, s_ag, r_ag.at[j], at_y(d))

    def normalize(j):
        start, stop = bounds[j]
        drain(r_ag.at[j], moved.at[0, 0 : (Y - 1) * (stop - start)])
        lines = min(32, stop - start)
        for lo in range(start, stop, lines):
            span = slice(lo, lo + lines)
            parts = [moved[c, span, :].astype(F32) for c in range(Y)]
            mean = sum(jnp.sum(p, axis=1, keepdims=True) for p in parts) / cfg.width
            parts = [p - mean for p in parts]
            var = sum(jnp.sum(jnp.square(p), axis=1, keepdims=True) for p in parts) / cfg.width
            scale = lax.rsqrt(var + 1e-05)
            for c in range(Y):
                normed[span, c * cfg.part : (c + 1) * cfg.part] = (parts[c] * scale).astype(BF)

    q = iota((1, CORES * cfg.comb), 1)
    side = lax.div(q, cfg.comb)
    core_of = core + side - 2 * core * side
    line = lax.div(lax.rem(q, cfg.comb), cfg.own) * cfg.pair + core_of * cfg.own + lax.rem(q, cfg.own)
    spot = onehot(iota((CORES * cfg.comb, CORES * cfg.comb), 0) == line)
    span = Z * cfg.pair

    def put_weights(f):
        drain(r_sib.at[f], w_sib.at[f])
        for k in range(X):
            lines = dot(spot, jnp.concatenate([w_own[f, k], w_sib[f, k]], axis=0))
            for n in range(4):
                chip = mod(x - k, X) * Z + lax.rem(z - (n - 1) - 4 * f + 2 * Z, Z)
                rows_of(staged, chip * cfg.pair, cfg.pair, 8)[...] = lines[n * cfg.pair : (n + 1) * cfg.pair]

    share(0)
    spread(1)
    spread(3)
    share(1)
    spread(2)
    hand_on(0)
    share(2)
    hand_on(1)
    normalize(0)
    share(3)
    hand_on(3)
    share(4)
    hand_on(2)
    normalize(1)
    put_weights(0)
    put_weights(1)
    normalize(2)
    put_weights(3)
    put_weights(2)
    weights[...] = staged[:, : 2 * U].astype(BF)

    normalize(3)
    normalize(4)

    both = dot(normed[...], weights[...])
    down[...] = staged[:, 2 * U :].astype(BF)
    dglu = dot(cot[...], down[...])
    value, gate = both[:, :U], both[:, U : 2 * U]
    sig = jax.nn.sigmoid(gate)
    glu = (value * sig).astype(BF)
    d_value = (dglu * sig).astype(BF)
    d_gate = (dglu * value * sig * (1.0 - sig)).astype(BF)

    d_both = jnp.concatenate([d_value, d_gate], axis=1)
    J = Z // 2 // 4
    steps = (0, 1, -1, 2)
    Q = cfg.pair

    def chunk(o, half, a):
        r = lax.rem(z + a + Z, 4)
        return jnp.concatenate(
            [rows_of(block.at[o], (half * (Z // 2) + r + 4 * j) * Q, Q, 8)[...] for j in range(J)], axis=0
        )

    for o in (2, 1, 3, 0):
        cols = pl.ds(pl.multiple_of(mod(x + o, X) * span, 128), span)
        block[o] = jnp.concatenate(
            [contract_rows(normed[:, cols], d_both), contract_rows(cot[:, cols], glu)], axis=1
        )
        for i, a in enumerate(steps):
            pair_out[o, i] = chunk(o, other, a).astype(BF)
        send(pair_out.at[o], pair_in.at[o], s_pair, r_pair.at[o], sibling)

    B = cfg.yrow
    half_b = B // 2

    def gather(h):
        drain(r_y.at[h], y_in.at[h])
        lines = y_own[h * half_b : (h + 1) * half_b, :]
        for k in range(Y - 1):
            lines = lines + y_in[h, k].astype(F32)
        ref = rows_of(result, y * B + h * half_b, half_b)
        ref[...] = lines.astype(BF)
        for d in (2, 1, 3):
            send(ref, ref, s_yg, r_yg.at[h], at_y(d))

    def put_out(h):
        drain(r_yg.at[h], result.at[0 : (Y - 1) * half_b])
        for i in range(Y):
            lo = i * B + h * half_b
            pltpu.make_async_copy(
                result.at[lo : lo + half_b], branch.at[lo : lo + half_b], s_put
            ).start()

    def to_x(i, o):
        x_out[i, o - 1] = (chunk(o, core, steps[i]) + pair_in[o, i].astype(F32)).astype(BF)
        send(x_out.at[i, o - 1], x_in.at[i, o - 1], s_x, r_x.at[i], at_x(o))

    for o in (2, 1, 3):
        drain(r_pair.at[o], pair_in.at[o])
        to_x(0, o)

    glu_rows[...] = dot(back, glu).astype(BF)
    for d in (2, 1, 3):
        some = rows_of(glu_rows, mod(y + d, Y) * B, B)[...]
        theirs = contract_cols(some, down[...]).astype(BF)
        for h in range(2):
            y_out[h, d - 1] = theirs[h * half_b : (h + 1) * half_b]
    for h in range(2):
        for d in (2, 1, 3):
            send(y_out.at[h, d - 1], y_in.at[h, d - 1], s_y, r_y.at[h], at_y(d))
    y_own[...] = contract_cols(rows_of(glu_rows, y * B, B)[...], down[...])

    for i in range(1, 4):
        for o in (2, 1, 3):
            to_x(i, o)
    drain(r_pair.at[0], pair_in.at[0])

    def summed(i, a):
        drain(r_x.at[i], x_in.at[i])
        total = chunk(0, core, a) + pair_in[0, i].astype(F32)
        for k in range(X - 1):
            total = total + x_in[i, k].astype(F32)
        return total

    O = cfg.own
    sends = []

    def to_owners(i):
        a = steps[i]
        total = summed(i, a)
        z_out[i] = pack(cfg, total.astype(BF))
        for j in range(J):
            t = core * (Z // 2) + 4 * j + lax.rem(z + a + Z, 4)
            for c in range(CORES):
                lo = j * CORES + c
                copy = pltpu.make_async_remote_copy(
                    src_ref=z_out.at[i, lo * cfg.pad : (lo + 1) * cfg.pad], dst_ref=z_in.at[mod(z - t, Z)],
                    send_sem=s_own.at[j, c] if a == 0 else s_z, recv_sem=r_z,
                    device_id=at(x, t, c), device_id_type=pl.DeviceIdType.MESH,
                )
                if a == 0:
                    acc[j, c, 0:O, :] = total[lo * O : (lo + 1) * O]
                    sends.append((t != z, copy))
                    pl.when(t != z)(copy.start)
                else:
                    copy.start()

    to_owners(0)
    gather(0)
    to_owners(1)
    to_owners(2)
    gather(1)
    to_owners(3)

    is_owner = lax.div(z, Z // 2) == core
    own_j = lax.rem(lax.div(z, 4), J)
    hand = pltpu.make_async_remote_copy(
        src_ref=acc.at[own_j, other], dst_ref=final, send_sem=s_fin, recv_sem=r_fin,
        device_id=sibling, device_id_type=pl.DeviceIdType.MESH,
    )

    @pl.when(is_owner)
    def _():
        hand.start()
        final[...] = acc[own_j, core]
        hand.wait_send()

    @pl.when(jnp.logical_not(is_owner))
    def _():
        hand.wait_recv()

    put_out(0)
    drain(r_z, z_in.at[1:Z])
    whole = z_in[1].astype(F32)
    for slot in range(2, Z):
        whole = whole + z_in[slot].astype(F32)
    rest = cfg.cols - cfg.main
    tail = []
    for r in range(O):
        lo, line = r % cfg.fold * rest, O + r // cfg.fold
        tail.append(whole[line : line + 1, lo : lo + rest])
    whole = jnp.concatenate([whole[0:O], jnp.concatenate(tail, axis=0)], axis=1)
    last[...] = whole + final[0:O, :]
    put_last = pltpu.make_async_copy(last, owned, s_in.at[0])
    put_last.start()

    put_out(1)

    drain(s_a1, out1.at[0 : (G - 1) * cfg.grow])
    drain(s_a2, out2.at[0 : (Z - 1) * cfg.zrow])
    drain(s_ag, moved.at[0 : Y - 1])
    drain(s_wf, shards.at[0, 0 : (F - 1) * cfg.pad])
    drain(s_wn, shards.at[:, 0 : 3 * cfg.pad])
    drain(s_wx, w_own.at[:, 1:X])
    drain(s_sib, w_own)
    drain(s_pair, pair_out)
    drain(s_x, x_out)
    drain(s_z, z_out.at[1:4])
    drain(s_y, y_out)
    drain(s_yg, result.at[0 : (Y - 1) * B])
    for needed, copy in sends:
        pl.when(needed)(copy.wait_send)
    drain(s_put, result)
    put_last.wait()


def place_results(units, branch_in, owned_in, branch, grad_value, grad_gate, grad_down):
    branch[...] = branch_in[...]
    grad_value[...] = owned_in[:, :units]
    grad_gate[...] = owned_in[:, units : 2 * units]
    grad_down[...] = owned_in[:, 2 * units :]


def module(cfg, frames, lengths, send_order, value_weight, gate_weight, down_weight, cotangent):
    X, Z, Y, G, R, D, U = cfg.X, cfg.Z, cfg.Y, cfg.G, cfg.rows, cfg.width, cfg.units
    C, S, B = cfg.cols, cfg.half, cfg.yrow
    vmem, hbm = pl.BlockSpec(memory_space=pltpu.VMEM), pl.BlockSpec(memory_space=pl.ANY)
    sem = pltpu.SemaphoreType.DMA
    F, J, H = cfg.far, Z // 8, Z // 8 * cfg.pair
    buffers = [
        ((R, cfg.part), BF),
        ((R, D), BF),
        ((R, cfg.part), BF),
        ((R, cfg.part), BF),
        ((R, cfg.part), BF),
        ((Y, R, cfg.part), BF),
        ((R, D), BF),
        ((R, D), BF),
        ((R, U), BF),
        ((F, 4 * cfg.pad, cfg.main), BF),
        ((F, X, cfg.comb, C), BF),
        ((F, X, cfg.comb, C), BF),
        ((D, C), F32),
        ((D, 2 * U), BF),
        ((D, U), BF),
        ((X, Z * cfg.pair, C), F32),
        ((X, 4, H, C), BF),
        ((X, 4, H, C), BF),
        ((4, X - 1, H, C), BF),
        ((4, X - 1, H, C), BF),
        ((4, J * CORES * cfg.pad, cfg.main), BF),
        ((Z, cfg.pad, cfg.main), BF),
        ((J, CORES, cfg.pad, C), F32),
        ((cfg.pad, C), F32),
        ((cfg.own, C), F32),
        ((B, D), F32),
        ((2, Y - 1, B // 2, D), BF),
        ((2, Y - 1, B // 2, D), BF),
        ((R, D), BF),
    ]
    one = ()
    sems = [
        one, one, one, (5,), one, (5,),
        one, (F,), one, (F,), one, (F,), one, (F,),
        one, (X,), one, (4,), one, one, (J, CORES), one, one,
        one, (2,), one, (2,),
    ]
    branch, owned = pl.pallas_call(
        functools.partial(kernel, cfg),
        out_shape=(jax.ShapeDtypeStruct((R, D), BF), jax.ShapeDtypeStruct((cfg.own, C), F32)),
        in_specs=[pl.BlockSpec(memory_space=pltpu.SMEM), vmem, hbm, vmem, vmem, vmem, hbm],
        out_specs=(hbm, hbm),
        scratch_shapes=[pltpu.VMEM(shape, kind) for shape, kind in buffers]
        + [sem(n) for n in sems]
        + [pltpu.SemaphoreType.REGULAR, sem((2,)), sem(one)],
        compiler_params=pltpu.CompilerParams(
            collective_id=0, has_side_effects=True, vmem_limit_bytes=56 * 1024 * 1024
        ),
    )(lengths, send_order, frames, value_weight, gate_weight, down_weight, cotangent)
    return pl.pallas_call(
        functools.partial(place_results, U),
        out_shape=(jax.ShapeDtypeStruct((R, D), BF),) + (jax.ShapeDtypeStruct((cfg.own, U), F32),) * 3,
        in_specs=[vmem] * 2,
        out_specs=(vmem,) * 4,
    )(branch, owned)


def build(mesh, X, Z):
    def shards(frames, lengths, send_order, value_weight, gate_weight, down_weight, cotangent):
        cfg = Sizes(
            X, Z, mesh.shape["mp"], frames.shape[0], frames.shape[1],
            value_weight.shape[0], value_weight.shape[1],
        )
        return module(
            cfg, frames, lengths, send_order, value_weight, gate_weight, down_weight, cotangent
        )

    return jax.shard_map(
        shards,
        mesh=mesh,
        in_specs=(
            P("dp", None),
            P("dp"),
            P("dp", None),
            P("dp", "mp"),
            P("dp", "mp"),
            P("dp", "mp"),
            P("dp", None),
        ),
        out_specs=(P("dp", None), P("dp", "mp"), P("dp", "mp"), P("dp", "mp")),
        check_vma=False,
    )


def solution(mesh):
    return build(mesh, 4, 16)
```

```python
import functools

import jax
import jax.numpy as jnp
from jax import lax
from jax.experimental import pallas as pl
from jax.experimental.pallas import tpu as pltpu
from jax.sharding import PartitionSpec as P

CORES = 2
BF = jnp.bfloat16
F32 = jnp.float32


def ceil16(rows):
    return -(-rows // 16) * 16


def iota(shape, axis):
    return lax.broadcasted_iota(jnp.int32, shape, axis)


def onehot(hit):
    return jnp.where(hit, 1.0, 0.0).astype(BF)


def dot(left, right):
    return jnp.dot(left, right, preferred_element_type=F32)


def contract_rows(left, right):
    return lax.dot_general(left, right, (((0,), (0,)), ((), ())), preferred_element_type=F32)


def contract_cols(left, right):
    return lax.dot_general(left, right, (((1,), (1,)), ((), ())), preferred_element_type=F32)


def mod(value, count):
    return lax.rem(value + count, count)


class Sizes:
    def __init__(self, X, Z, Y, rows, width, own, units):
        self.X, self.Z, self.Y = X, Z, Y
        self.G = X * CORES
        self.rows, self.width, self.own, self.units = rows, width, own, units
        self.cap = rows // (X * Z * CORES)
        self.part = width // Y
        self.pad = ceil16(own)
        self.zrow = self.G * self.cap
        self.grow = self.Z * self.cap
        self.far = Z // 4
        self.comb = 4 * own
        self.pair = CORES * own
        self.cols = 3 * units
        self.main = self.cols // 128 * 128
        self.fold = own // (self.pad - own)
        self.half = Z // 2 * self.pair
        self.yrow = rows // Y


def pack(cfg, lines):
    own, pad, main, fold = cfg.own, cfg.pad, cfg.main, cfg.fold
    count = lines.shape[0] // own
    q = iota((1, count * own), 1)
    m, r = lax.div(q, own), lax.rem(q, own)
    p = iota((count * pad, count * own), 0)
    body = dot(onehot(p == m * pad + r), lines[:, :main])
    tails = [
        dot(onehot(p == jnp.where(lax.rem(r, fold) == s, m * pad + own + lax.div(r, fold), -1)), lines[:, main:])
        for s in range(fold)
    ]
    wide = -(-fold * (cfg.cols - main) // 128) * 128
    tails.append(jnp.zeros((count * pad, wide - fold * (cfg.cols - main)), F32))
    tail = jnp.concatenate(tails, axis=1)
    return jnp.concatenate([body[:, :wide] + tail, body[:, wide:]], axis=1).astype(BF)


def unpack(cfg, lines):
    own, pad, main, fold = cfg.own, cfg.pad, cfg.main, cfg.fold
    count, rest = lines.shape[0] // pad, cfg.cols - main
    q = iota((1, count * pad), 1)
    m, r = lax.div(q, pad), lax.rem(q, pad)
    p = iota((count * own, count * pad), 0)
    body = dot(onehot(p == jnp.where(r < own, m * own + r, -1)), lines)
    tail = sum(
        dot(onehot(p == jnp.where(r < own, -1, m * own + (r - own) * fold + s)), lines[:, s * rest : (s + 1) * rest])
        for s in range(fold)
    )
    return jnp.concatenate([body, tail], axis=1).astype(BF)


def kernel(
    cfg,
    lengths, send_order, frames_all, value_w, gate_w, down_w, cotangent_all,
    branch, owned,
    frames, cotangent, out1, in1, out2, moved, normed, cot, glu_rows,
    shards, w_own, w_sib, staged, weights, down,
    block, pair_out, pair_in, x_out, x_in, z_out, z_in, acc, final, last,
    y_own, y_out, y_in, result,
    s_a1, r_a1, s_a2, r_a2, s_ag, r_ag,
    s_wf, r_wf, s_wn, r_wn, s_wx, r_wx, s_sib, r_sib,
    s_pair, r_pair, s_x, r_x, s_z, r_z, s_own, s_fin, r_fin, s_y, r_y, s_yg, r_yg,
    relay, s_in, s_put,
):
    X, Z, Y, G = cfg.X, cfg.Z, cfg.Y, cfg.G
    R, U, F, cap = cfg.rows, cfg.units, cfg.far, cfg.cap
    dp = lax.axis_index("dp")
    y = lax.axis_index("mp")
    core = lax.rem(dp, CORES)
    z = lax.rem(lax.div(dp, CORES), Z)
    x = lax.div(dp, CORES * Z)
    g = x * CORES + core
    other = 1 - core
    sibling = {"dp": dp + 1 - 2 * core, "mp": y}

    def at(x_, z_, core_):
        return {"dp": (x_ * Z + z_) * CORES + core_, "mp": y}

    def at_x(o):
        return at(mod(x + o, X), z, core)

    def at_z(o):
        return at(x, mod(z + o, Z), core)

    def at_y(o):
        return {"dp": dp, "mp": mod(y + o, Y)}

    def at_g(t):
        return at(lax.div(t, CORES), z, lax.rem(t, CORES))

    def send(src, dst, sent, arrived, where):
        copy = pltpu.make_async_remote_copy(
            src_ref=src, dst_ref=dst, send_sem=sent, recv_sem=arrived,
            device_id=where, device_id_type=pl.DeviceIdType.MESH,
        )
        copy.start()

    def drain(sem, ref):
        pltpu.make_async_copy(ref, ref, sem).wait()

    def rows_of(ref, start, size, step=16):
        return ref.at[pl.ds(pl.multiple_of(start, step), size)]

    barrier = pltpu.get_barrier_semaphore()
    around = (4, 5, 2, 3, 6, 7, 1)
    partners = [at_z(o * s) for o in (4, 3) for s in (1, -1)]
    partners += [at_g(mod(g + o, G)) for o in around]
    partners += [at_z(o * s) for o in (2, 1) for s in (1, -1)]
    partners += [at_y(o) for o in range(1, Y)]
    for who in partners:
        pl.semaphore_signal(barrier, inc=1, device_id=who, device_id_type=pl.DeviceIdType.MESH)

    columns = pl.ds(pl.multiple_of(y * cfg.part, 128), cfg.part)
    get_frames = pltpu.make_async_copy(frames_all.at[:, columns], frames, s_in.at[0])
    get_frames.start()
    get_cotangent = pltpu.make_async_copy(cotangent_all, cotangent, s_in.at[1])
    get_cotangent.start()

    packed = jnp.concatenate([value_w[...], gate_w[...], down_w[...]], axis=1)
    mine = shards.at[0, cfg.pad : 2 * cfg.pad]
    mine[...] = pack(cfg, packed)

    row, place = iota((R, R), 0), iota((1, R), 1)
    k_of, z_of, g_of = lax.rem(place, cap), lax.rem(lax.div(place, cap), Z), lax.div(place, cap * Z)
    natural = ((lax.div(g_of, CORES) * Z + z_of) * CORES + lax.rem(g_of, CORES)) * cap + k_of
    numbers = jnp.broadcast_to(send_order[...].astype(F32).astype(BF), (16, R))
    order = dot(numbers, onehot(row == natural))[0:1, :]
    pick = onehot((row.astype(F32) == order) & (row < lengths[0]))
    get_frames.wait()
    out1[...] = contract_rows(pick, frames[...]).astype(BF)

    pl.semaphore_wait(barrier, len(partners))
    for o in (4, -4):
        pl.semaphore_signal(relay, inc=1, device_id=at_z(o), device_id_type=pl.DeviceIdType.MESH)

    near = (1, -1, 2)

    def pass_near(f):
        ref = shards.at[f, cfg.pad : 2 * cfg.pad]
        for a in near:
            lo = (a + 1) * cfg.pad
            send(ref, shards.at[f, lo : lo + cfg.pad], s_wn, r_wn.at[f], at_z(a))

    def pass_far(f):
        send(mine, shards.at[f, cfg.pad : 2 * cfg.pad], s_wf, r_wf.at[f], at_z(4 * f))

    pass_near(0)
    for f in range(1, F):
        if 4 * f != Z // 2:
            pass_far(f)
    for o in around:
        t = mod(g + o, G)
        send(
            rows_of(out1, t * cfg.grow, cfg.grow), rows_of(in1, g * cfg.grow, cfg.grow),
            s_a1, r_a1, at_g(t),
        )
    rows_of(in1, g * cfg.grow, cfg.grow)[...] = rows_of(out1, g * cfg.grow, cfg.grow)[...]

    pl.semaphore_wait(relay, 2)
    pass_far(F // 2)

    to_new = (z_of * G + g_of) * cap + k_of
    drain(r_a1, in1.at[0 : (G - 1) * cfg.grow])
    out2[...] = dot(onehot(row == to_new), in1[...]).astype(BF)
    here = moved.at[y]
    position = [0] + [2 * o - 1 if o <= Z // 2 else 2 * (Z - o) for o in range(1, Z)]
    quarter = Z // 4
    edges = [0, quarter, 2 * quarter, 3 * quarter, Z - quarter // 2, Z]
    parcel_of = [sum(p >= edge for edge in edges[1:]) for p in range(Z)]
    bounds = [(lo * cfg.zrow, hi * cfg.zrow) for lo, hi in zip(edges, edges[1:])]

    def to_z(parcel_range):
        for o in sorted(range(1, Z), key=lambda o: position[Z - o]):
            p = position[Z - o]
            if parcel_of[p] in parcel_range:
                send(
                    rows_of(out2, mod(z + o, Z) * cfg.zrow, cfg.zrow),
                    here.at[p * cfg.zrow : (p + 1) * cfg.zrow],
                    s_a2, r_a2.at[parcel_of[p]], at_z(o),
                )

    to_z((0, 1))
    here[0 : cfg.zrow, :] = rows_of(out2, z * cfg.zrow, cfg.zrow)[...]

    def spread(f):
        drain(r_wn.at[f], shards.at[f, 0 : 3 * cfg.pad])
        w_own[f, 0] = unpack(cfg, shards[f])
        for k in (2, 1, 3):
            send(w_own.at[f, 0], w_own.at[f, k], s_wx, r_wx.at[f], at_x(k))

    def hand_on(f):
        drain(r_wx.at[f], w_own.at[f, 1:X])
        send(w_own.at[f], w_sib.at[f], s_sib, r_sib.at[f], sibling)

    spread(0)
    for f in (1, 3, 2):
        drain(r_wf.at[f], shards.at[f, cfg.pad : 2 * cfg.pad])
        pass_near(f)
    to_z((2, 3, 4))

    where = lax.div(place, cfg.zrow)
    away = jnp.where(lax.rem(where, 2) == 1, lax.div(where + 1, 2), lax.rem(Z - lax.div(where, 2), Z))
    k_at, g_at = lax.rem(place, cap), lax.rem(lax.div(place, cap), G)
    natural = (
        (lax.div(g_at, CORES) * Z + lax.rem(z + away, Z)) * CORES + lax.rem(g_at, CORES)
    ) * cap + k_at
    back = onehot(row == natural)
    get_cotangent.wait()
    cot[...] = contract_rows(back, cotangent[...]).astype(BF)

    def share(j):
        lo, hi = bounds[j]
        drain(r_a2.at[j], here.at[(lo if j else cfg.zrow) : hi])
        ref = here.at[lo:hi]
        for d in (2, 1, 3):
            send(ref, ref, s_ag, r_ag.at[j], at_y(d))

    def normalize(j):
        start, stop = bounds[j]
        drain(r_ag.at[j], moved.at[0, 0 : (Y - 1) * (stop - start)])
        lines = min(32, stop - start)
        for lo in range(start, stop, lines):
            span = slice(lo, lo + lines)
            parts = [moved[c, span, :].astype(F32) for c in range(Y)]
            mean = sum(jnp.sum(p, axis=1, keepdims=True) for p in parts) / cfg.width
            parts = [p - mean for p in parts]
            var = sum(jnp.sum(jnp.square(p), axis=1, keepdims=True) for p in parts) / cfg.width
            scale = lax.rsqrt(var + 1e-05)
            for c in range(Y):
                normed[span, c * cfg.part : (c + 1) * cfg.part] = (parts[c] * scale).astype(BF)

    q = iota((1, CORES * cfg.comb), 1)
    side = lax.div(q, cfg.comb)
    core_of = core + side - 2 * core * side
    line = lax.div(lax.rem(q, cfg.comb), cfg.own) * cfg.pair + core_of * cfg.own + lax.rem(q, cfg.own)
    spot = onehot(iota((CORES * cfg.comb, CORES * cfg.comb), 0) == line)
    span = Z * cfg.pair

    def put_weights(f):
        drain(r_sib.at[f], w_sib.at[f])
        for k in range(X):
            lines = dot(spot, jnp.concatenate([w_own[f, k], w_sib[f, k]], axis=0))
            for n in range(4):
                chip = mod(x - k, X) * Z + lax.rem(z - (n - 1) - 4 * f + 2 * Z, Z)
                rows_of(staged, chip * cfg.pair, cfg.pair, 8)[...] = lines[n * cfg.pair : (n + 1) * cfg.pair]

    share(0)
    spread(1)
    spread(3)
    share(1)
    spread(2)
    hand_on(0)
    share(2)
    hand_on(1)
    normalize(0)
    share(3)
    hand_on(3)
    hand_on(2)
    share(4)
    normalize(1)
    put_weights(0)
    put_weights(1)
    normalize(2)
    put_weights(3)
    put_weights(2)
    weights[...] = staged[:, : 2 * U].astype(BF)

    normalize(3)
    normalize(4)

    both = dot(normed[...], weights[...])
    down[...] = staged[:, 2 * U :].astype(BF)
    dglu = dot(cot[...], down[...])
    value, gate = both[:, :U], both[:, U : 2 * U]
    sig = jax.nn.sigmoid(gate)
    glu = (value * sig).astype(BF)
    d_value = (dglu * sig).astype(BF)
    d_gate = (dglu * value * sig * (1.0 - sig)).astype(BF)

    d_both = jnp.concatenate([d_value, d_gate], axis=1)
    J = Z // 2 // 4
    steps = (0, 1, -1, 2)
    Q = cfg.pair

    def chunk(o, half, a):
        r = lax.rem(z + a + Z, 4)
        return jnp.concatenate(
            [rows_of(block.at[o], (half * (Z // 2) + r + 4 * j) * Q, Q, 8)[...] for j in range(J)], axis=0
        )

    for o in (2, 1, 3, 0):
        cols = pl.ds(pl.multiple_of(mod(x + o, X) * span, 128), span)
        block[o] = jnp.concatenate(
            [contract_rows(normed[:, cols], d_both), contract_rows(cot[:, cols], glu)], axis=1
        )
        for i, a in enumerate(steps):
            pair_out[o, i] = chunk(o, other, a).astype(BF)
        send(pair_out.at[o], pair_in.at[o], s_pair, r_pair.at[o], sibling)

    B = cfg.yrow
    half_b = B // 2

    def gather(h):
        drain(r_y.at[h], y_in.at[h])
        lines = y_own[h * half_b : (h + 1) * half_b, :]
        for k in range(Y - 1):
            lines = lines + y_in[h, k].astype(F32)
        ref = rows_of(result, y * B + h * half_b, half_b)
        ref[...] = lines.astype(BF)
        for d in (2, 1, 3):
            send(ref, ref, s_yg, r_yg.at[h], at_y(d))

    def put_out(h):
        drain(r_yg.at[h], result.at[0 : (Y - 1) * half_b])
        for i in range(Y):
            lo = i * B + h * half_b
            pltpu.make_async_copy(
                result.at[lo : lo + half_b], branch.at[lo : lo + half_b], s_put
            ).start()

    def to_x(i, o):
        x_out[i, o - 1] = (chunk(o, core, steps[i]) + pair_in[o, i].astype(F32)).astype(BF)
        send(x_out.at[i, o - 1], x_in.at[i, o - 1], s_x, r_x.at[i], at_x(o))

    for o in (2, 1, 3):
        drain(r_pair.at[o], pair_in.at[o])
        to_x(0, o)

    glu_rows[...] = dot(back, glu).astype(BF)
    for d in (2, 1, 3):
        some = rows_of(glu_rows, mod(y + d, Y) * B, B)[...]
        theirs = contract_cols(some, down[...]).astype(BF)
        for h in range(2):
            y_out[h, d - 1] = theirs[h * half_b : (h + 1) * half_b]
    for h in range(2):
        for d in (2, 1, 3):
            send(y_out.at[h, d - 1], y_in.at[h, d - 1], s_y, r_y.at[h], at_y(d))
    y_own[...] = contract_cols(rows_of(glu_rows, y * B, B)[...], down[...])

    for i in range(1, 4):
        for o in (2, 1, 3):
            to_x(i, o)
    drain(r_pair.at[0], pair_in.at[0])

    def summed(i, a):
        drain(r_x.at[i], x_in.at[i])
        total = chunk(0, core, a) + pair_in[0, i].astype(F32)
        for k in range(X - 1):
            total = total + x_in[i, k].astype(F32)
        return total

    O = cfg.own
    sends = []

    def to_owners(i):
        a = steps[i]
        total = summed(i, a)
        z_out[i] = pack(cfg, total.astype(BF))
        for j in range(J):
            t = core * (Z // 2) + 4 * j + lax.rem(z + a + Z, 4)
            for c in range(CORES):
                lo = j * CORES + c
                copy = pltpu.make_async_remote_copy(
                    src_ref=z_out.at[i, lo * cfg.pad : (lo + 1) * cfg.pad], dst_ref=z_in.at[mod(z - t, Z)],
                    send_sem=s_own.at[j, c] if a == 0 else s_z, recv_sem=r_z,
                    device_id=at(x, t, c), device_id_type=pl.DeviceIdType.MESH,
                )
                if a == 0:
                    acc[j, c, 0:O, :] = total[lo * O : (lo + 1) * O]
                    sends.append((t != z, copy))
                    pl.when(t != z)(copy.start)
                else:
                    copy.start()

    to_owners(0)
    gather(0)
    to_owners(1)
    to_owners(2)
    gather(1)
    to_owners(3)

    is_owner = lax.div(z, Z // 2) == core
    own_j = lax.rem(lax.div(z, 4), J)
    hand = pltpu.make_async_remote_copy(
        src_ref=acc.at[own_j, other], dst_ref=final, send_sem=s_fin, recv_sem=r_fin,
        device_id=sibling, device_id_type=pl.DeviceIdType.MESH,
    )

    @pl.when(is_owner)
    def _():
        hand.start()
        final[...] = acc[own_j, core]
        hand.wait_send()

    @pl.when(jnp.logical_not(is_owner))
    def _():
        hand.wait_recv()

    put_out(0)
    drain(r_z, z_in.at[1:Z])
    whole = z_in[1].astype(F32)
    for slot in range(2, Z):
        whole = whole + z_in[slot].astype(F32)
    rest = cfg.cols - cfg.main
    tail = []
    for r in range(O):
        lo, line = r % cfg.fold * rest, O + r // cfg.fold
        tail.append(whole[line : line + 1, lo : lo + rest])
    whole = jnp.concatenate([whole[0:O], jnp.concatenate(tail, axis=0)], axis=1)
    last[...] = whole + final[0:O, :]
    put_last = pltpu.make_async_copy(last, owned, s_in.at[0])
    put_last.start()

    put_out(1)

    drain(s_a1, out1.at[0 : (G - 1) * cfg.grow])
    drain(s_a2, out2.at[0 : (Z - 1) * cfg.zrow])
    drain(s_ag, moved.at[0 : Y - 1])
    drain(s_wf, shards.at[0, 0 : (F - 1) * cfg.pad])
    drain(s_wn, shards.at[:, 0 : 3 * cfg.pad])
    drain(s_wx, w_own.at[:, 1:X])
    drain(s_sib, w_own)
    drain(s_pair, pair_out)
    drain(s_x, x_out)
    drain(s_z, z_out.at[1:4])
    drain(s_y, y_out)
    drain(s_yg, result.at[0 : (Y - 1) * B])
    for needed, copy in sends:
        pl.when(needed)(copy.wait_send)
    drain(s_put, result)
    put_last.wait()


def place_results(units, branch_in, owned_in, branch, grad_value, grad_gate, grad_down):
    branch[...] = branch_in[...]
    grad_value[...] = owned_in[:, :units]
    grad_gate[...] = owned_in[:, units : 2 * units]
    grad_down[...] = owned_in[:, 2 * units :]


def module(cfg, frames, lengths, send_order, value_weight, gate_weight, down_weight, cotangent):
    X, Z, Y, G, R, D, U = cfg.X, cfg.Z, cfg.Y, cfg.G, cfg.rows, cfg.width, cfg.units
    C, S, B = cfg.cols, cfg.half, cfg.yrow
    vmem, hbm = pl.BlockSpec(memory_space=pltpu.VMEM), pl.BlockSpec(memory_space=pl.ANY)
    sem = pltpu.SemaphoreType.DMA
    F, J, H = cfg.far, Z // 8, Z // 8 * cfg.pair
    buffers = [
        ((R, cfg.part), BF),
        ((R, D), BF),
        ((R, cfg.part), BF),
        ((R, cfg.part), BF),
        ((R, cfg.part), BF),
        ((Y, R, cfg.part), BF),
        ((R, D), BF),
        ((R, D), BF),
        ((R, U), BF),
        ((F, 4 * cfg.pad, cfg.main), BF),
        ((F, X, cfg.comb, C), BF),
        ((F, X, cfg.comb, C), BF),
        ((D, C), F32),
        ((D, 2 * U), BF),
        ((D, U), BF),
        ((X, Z * cfg.pair, C), F32),
        ((X, 4, H, C), BF),
        ((X, 4, H, C), BF),
        ((4, X - 1, H, C), BF),
        ((4, X - 1, H, C), BF),
        ((4, J * CORES * cfg.pad, cfg.main), BF),
        ((Z, cfg.pad, cfg.main), BF),
        ((J, CORES, cfg.pad, C), F32),
        ((cfg.pad, C), F32),
        ((cfg.own, C), F32),
        ((B, D), F32),
        ((2, Y - 1, B // 2, D), BF),
        ((2, Y - 1, B // 2, D), BF),
        ((R, D), BF),
    ]
    one = ()
    sems = [
        one, one, one, (5,), one, (5,),
        one, (F,), one, (F,), one, (F,), one, (F,),
        one, (X,), one, (4,), one, one, (J, CORES), one, one,
        one, (2,), one, (2,),
    ]
    branch, owned = pl.pallas_call(
        functools.partial(kernel, cfg),
        out_shape=(jax.ShapeDtypeStruct((R, D), BF), jax.ShapeDtypeStruct((cfg.own, C), F32)),
        in_specs=[pl.BlockSpec(memory_space=pltpu.SMEM), vmem, hbm, vmem, vmem, vmem, hbm],
        out_specs=(hbm, hbm),
        scratch_shapes=[pltpu.VMEM(shape, kind) for shape, kind in buffers]
        + [sem(n) for n in sems]
        + [pltpu.SemaphoreType.REGULAR, sem((2,)), sem(one)],
        compiler_params=pltpu.CompilerParams(
            collective_id=0, has_side_effects=True, vmem_limit_bytes=56 * 1024 * 1024
        ),
    )(lengths, send_order, frames, value_weight, gate_weight, down_weight, cotangent)
    return pl.pallas_call(
        functools.partial(place_results, U),
        out_shape=(jax.ShapeDtypeStruct((R, D), BF),) + (jax.ShapeDtypeStruct((cfg.own, U), F32),) * 3,
        in_specs=[vmem] * 2,
        out_specs=(vmem,) * 4,
    )(branch, owned)


def build(mesh, X, Z):
    def shards(frames, lengths, send_order, value_weight, gate_weight, down_weight, cotangent):
        cfg = Sizes(
            X, Z, mesh.shape["mp"], frames.shape[0], frames.shape[1],
            value_weight.shape[0], value_weight.shape[1],
        )
        return module(
            cfg, frames, lengths, send_order, value_weight, gate_weight, down_weight, cotangent
        )

    return jax.shard_map(
        shards,
        mesh=mesh,
        in_specs=(
            P("dp", None),
            P("dp"),
            P("dp", None),
            P("dp", "mp"),
            P("dp", "mp"),
            P("dp", "mp"),
            P("dp", None),
        ),
        out_specs=(P("dp", None), P("dp", "mp"), P("dp", "mp"), P("dp", "mp")),
        check_vma=False,
    )


def solution(mesh):
    return build(mesh, 4, 16)
```

```python
import functools

import jax
import jax.numpy as jnp
from jax import lax
from jax.experimental import pallas as pl
from jax.experimental.pallas import tpu as pltpu
from jax.sharding import PartitionSpec as P

CORES = 2
BF = jnp.bfloat16
F32 = jnp.float32


def ceil16(rows):
    return -(-rows // 16) * 16


def iota(shape, axis):
    return lax.broadcasted_iota(jnp.int32, shape, axis)


def onehot(hit):
    return jnp.where(hit, 1.0, 0.0).astype(BF)


def dot(left, right):
    return jnp.dot(left, right, preferred_element_type=F32)


def contract_rows(left, right):
    return lax.dot_general(left, right, (((0,), (0,)), ((), ())), preferred_element_type=F32)


def contract_cols(left, right):
    return lax.dot_general(left, right, (((1,), (1,)), ((), ())), preferred_element_type=F32)


def mod(value, count):
    return lax.rem(value + count, count)


class Sizes:
    def __init__(self, X, Z, Y, rows, width, own, units):
        self.X, self.Z, self.Y = X, Z, Y
        self.G = X * CORES
        self.rows, self.width, self.own, self.units = rows, width, own, units
        self.cap = rows // (X * Z * CORES)
        self.part = width // Y
        self.pad = ceil16(own)
        self.zrow = self.G * self.cap
        self.grow = self.Z * self.cap
        self.far = Z // 4
        self.comb = 4 * own
        self.pair = CORES * own
        self.cols = 3 * units
        self.main = self.cols // 128 * 128
        self.fold = own // (self.pad - own)
        self.half = Z // 2 * self.pair
        self.yrow = rows // Y


def pack(cfg, lines):
    own, pad, main, fold = cfg.own, cfg.pad, cfg.main, cfg.fold
    count = lines.shape[0] // own
    q = iota((1, count * own), 1)
    m, r = lax.div(q, own), lax.rem(q, own)
    p = iota((count * pad, count * own), 0)
    body = dot(onehot(p == m * pad + r), lines[:, :main])
    tails = [
        dot(onehot(p == jnp.where(lax.rem(r, fold) == s, m * pad + own + lax.div(r, fold), -1)), lines[:, main:])
        for s in range(fold)
    ]
    wide = -(-fold * (cfg.cols - main) // 128) * 128
    tails.append(jnp.zeros((count * pad, wide - fold * (cfg.cols - main)), F32))
    tail = jnp.concatenate(tails, axis=1)
    return jnp.concatenate([body[:, :wide] + tail, body[:, wide:]], axis=1).astype(BF)


def unpack(cfg, lines):
    own, pad, main, fold = cfg.own, cfg.pad, cfg.main, cfg.fold
    count, rest = lines.shape[0] // pad, cfg.cols - main
    q = iota((1, count * pad), 1)
    m, r = lax.div(q, pad), lax.rem(q, pad)
    p = iota((count * own, count * pad), 0)
    body = dot(onehot(p == jnp.where(r < own, m * own + r, -1)), lines)
    tail = sum(
        dot(onehot(p == jnp.where(r < own, -1, m * own + (r - own) * fold + s)), lines[:, s * rest : (s + 1) * rest])
        for s in range(fold)
    )
    return jnp.concatenate([body, tail], axis=1).astype(BF)


def kernel(
    cfg,
    lengths, send_order, frames_all, value_w, gate_w, down_w, cotangent_all,
    branch, owned,
    frames, cotangent, out1, in1, out2, moved, normed, cot, glu_rows,
    shards, w_own, w_sib, staged, weights, down,
    block, pair_out, pair_in, x_out, x_in, z_out, z_in, acc, final, last,
    y_own, y_out, y_in, result,
    s_a1, r_a1, s_a2, r_a2, s_ag, r_ag,
    s_wf, r_wf, s_wn, r_wn, s_wx, r_wx, s_sib, r_sib,
    s_pair, r_pair, s_x, r_x, s_z, r_z, s_own, s_fin, r_fin, s_y, r_y, s_yg, r_yg,
    relay, s_in, s_put,
):
    X, Z, Y, G = cfg.X, cfg.Z, cfg.Y, cfg.G
    R, U, F, cap = cfg.rows, cfg.units, cfg.far, cfg.cap
    dp = lax.axis_index("dp")
    y = lax.axis_index("mp")
    core = lax.rem(dp, CORES)
    z = lax.rem(lax.div(dp, CORES), Z)
    x = lax.div(dp, CORES * Z)
    g = x * CORES + core
    other = 1 - core
    sibling = {"dp": dp + 1 - 2 * core, "mp": y}

    def at(x_, z_, core_):
        return {"dp": (x_ * Z + z_) * CORES + core_, "mp": y}

    def at_x(o):
        return at(mod(x + o, X), z, core)

    def at_z(o):
        return at(x, mod(z + o, Z), core)

    def at_y(o):
        return {"dp": dp, "mp": mod(y + o, Y)}

    def at_g(t):
        return at(lax.div(t, CORES), z, lax.rem(t, CORES))

    def send(src, dst, sent, arrived, where):
        copy = pltpu.make_async_remote_copy(
            src_ref=src, dst_ref=dst, send_sem=sent, recv_sem=arrived,
            device_id=where, device_id_type=pl.DeviceIdType.MESH,
        )
        copy.start()

    def drain(sem, ref):
        pltpu.make_async_copy(ref, ref, sem).wait()

    def rows_of(ref, start, size, step=16):
        return ref.at[pl.ds(pl.multiple_of(start, step), size)]

    barrier = pltpu.get_barrier_semaphore()
    around = (4, 5, 2, 3, 6, 7, 1)
    partners = [at_z(o * s) for o in (4, 3) for s in (1, -1)]
    partners += [at_g(mod(g + o, G)) for o in around]
    partners += [at_z(o * s) for o in (2, 1) for s in (1, -1)]
    partners += [at_y(o) for o in range(1, Y)]
    for who in partners:
        pl.semaphore_signal(barrier, inc=1, device_id=who, device_id_type=pl.DeviceIdType.MESH)

    columns = pl.ds(pl.multiple_of(y * cfg.part, 128), cfg.part)
    get_frames = pltpu.make_async_copy(frames_all.at[:, columns], frames, s_in.at[0])
    get_frames.start()
    get_cotangent = pltpu.make_async_copy(cotangent_all, cotangent, s_in.at[1])
    get_cotangent.start()

    packed = jnp.concatenate([value_w[...], gate_w[...], down_w[...]], axis=1)
    mine = shards.at[0, cfg.pad : 2 * cfg.pad]
    mine[...] = pack(cfg, packed)

    row, place = iota((R, R), 0), iota((1, R), 1)
    k_of, z_of, g_of = lax.rem(place, cap), lax.rem(lax.div(place, cap), Z), lax.div(place, cap * Z)
    natural = ((lax.div(g_of, CORES) * Z + z_of) * CORES + lax.rem(g_of, CORES)) * cap + k_of
    numbers = jnp.broadcast_to(send_order[...].astype(F32).astype(BF), (16, R))
    order = dot(numbers, onehot(row == natural))[0:1, :]
    pick = onehot((row.astype(F32) == order) & (row < lengths[0]))
    get_frames.wait()
    out1[...] = contract_rows(pick, frames[...]).astype(BF)

    pl.semaphore_wait(barrier, len(partners))
    for o in (4, -4):
        pl.semaphore_signal(relay, inc=1, device_id=at_z(o), device_id_type=pl.DeviceIdType.MESH)

    for o in around:
        t = mod(g + o, G)
        send(
            rows_of(out1, t * cfg.grow, cfg.grow), rows_of(in1, g * cfg.grow, cfg.grow),
            s_a1, r_a1, at_g(t),
        )
    rows_of(in1, g * cfg.grow, cfg.grow)[...] = rows_of(out1, g * cfg.grow, cfg.grow)[...]

    near = (1, -1, 2)

    def pass_near(f):
        ref = shards.at[f, cfg.pad : 2 * cfg.pad]
        for a in near:
            lo = (a + 1) * cfg.pad
            send(ref, shards.at[f, lo : lo + cfg.pad], s_wn, r_wn.at[f], at_z(a))

    def pass_far(f):
        send(mine, shards.at[f, cfg.pad : 2 * cfg.pad], s_wf, r_wf.at[f], at_z(4 * f))

    pass_near(0)
    for f in range(1, F):
        if 4 * f != Z // 2:
            pass_far(f)
    pl.semaphore_wait(relay, 2)
    pass_far(F // 2)

    where = lax.div(place, cfg.zrow)
    away = jnp.where(lax.rem(where, 2) == 1, lax.div(where + 1, 2), lax.rem(Z - lax.div(where, 2), Z))
    k_at, g_at = lax.rem(place, cap), lax.rem(lax.div(place, cap), G)
    natural = (
        (lax.div(g_at, CORES) * Z + lax.rem(z + away, Z)) * CORES + lax.rem(g_at, CORES)
    ) * cap + k_at
    back = onehot(row == natural)
    get_cotangent.wait()
    cot[...] = contract_rows(back, cotangent[...]).astype(BF)

    to_new = (z_of * G + g_of) * cap + k_of
    drain(r_a1, in1.at[0 : (G - 1) * cfg.grow])
    out2[...] = dot(onehot(row == to_new), in1[...]).astype(BF)
    here = moved.at[y]
    position = [0] + [2 * o - 1 if o <= Z // 2 else 2 * (Z - o) for o in range(1, Z)]
    quarter = Z // 4
    edges = [0, quarter, 2 * quarter, 3 * quarter, Z - quarter // 2, Z]
    parcel_of = [sum(p >= edge for edge in edges[1:]) for p in range(Z)]
    bounds = [(lo * cfg.zrow, hi * cfg.zrow) for lo, hi in zip(edges, edges[1:])]

    def to_z(parcel_range):
        for o in sorted(range(1, Z), key=lambda o: position[Z - o]):
            p = position[Z - o]
            if parcel_of[p] in parcel_range:
                send(
                    rows_of(out2, mod(z + o, Z) * cfg.zrow, cfg.zrow),
                    here.at[p * cfg.zrow : (p + 1) * cfg.zrow],
                    s_a2, r_a2.at[parcel_of[p]], at_z(o),
                )

    to_z((0, 1))
    here[0 : cfg.zrow, :] = rows_of(out2, z * cfg.zrow, cfg.zrow)[...]

    def spread(f):
        drain(r_wn.at[f], shards.at[f, 0 : 3 * cfg.pad])
        w_own[f, 0] = unpack(cfg, shards[f])
        for k in (2, 1, 3):
            send(w_own.at[f, 0], w_own.at[f, k], s_wx, r_wx.at[f], at_x(k))

    def hand_on(f):
        drain(r_wx.at[f], w_own.at[f, 1:X])
        send(w_own.at[f], w_sib.at[f], s_sib, r_sib.at[f], sibling)

    spread(0)
    for f in (1, 3, 2):
        drain(r_wf.at[f], shards.at[f, cfg.pad : 2 * cfg.pad])
        pass_near(f)
    to_z((2, 3, 4))

    def share(j):
        lo, hi = bounds[j]
        drain(r_a2.at[j], here.at[(lo if j else cfg.zrow) : hi])
        ref = here.at[lo:hi]
        for d in (2, 1, 3):
            send(ref, ref, s_ag, r_ag.at[j], at_y(d))

    def normalize(j):
        start, stop = bounds[j]
        drain(r_ag.at[j], moved.at[0, 0 : (Y - 1) * (stop - start)])
        lines = min(32, stop - start)
        for lo in range(start, stop, lines):
            span = slice(lo, lo + lines)
            parts = [moved[c, span, :].astype(F32) for c in range(Y)]
            mean = sum(jnp.sum(p, axis=1, keepdims=True) for p in parts) / cfg.width
            parts = [p - mean for p in parts]
            var = sum(jnp.sum(jnp.square(p), axis=1, keepdims=True) for p in parts) / cfg.width
            scale = lax.rsqrt(var + 1e-05)
            for c in range(Y):
                normed[span, c * cfg.part : (c + 1) * cfg.part] = (parts[c] * scale).astype(BF)

    q = iota((1, CORES * cfg.comb), 1)
    side = lax.div(q, cfg.comb)
    core_of = core + side - 2 * core * side
    line = lax.div(lax.rem(q, cfg.comb), cfg.own) * cfg.pair + core_of * cfg.own + lax.rem(q, cfg.own)
    spot = onehot(iota((CORES * cfg.comb, CORES * cfg.comb), 0) == line)
    span = Z * cfg.pair

    def put_weights(f):
        drain(r_sib.at[f], w_sib.at[f])
        for k in range(X):
            lines = dot(spot, jnp.concatenate([w_own[f, k], w_sib[f, k]], axis=0))
            for n in range(4):
                chip = mod(x - k, X) * Z + lax.rem(z - (n - 1) - 4 * f + 2 * Z, Z)
                rows_of(staged, chip * cfg.pair, cfg.pair, 8)[...] = lines[n * cfg.pair : (n + 1) * cfg.pair]

    share(0)
    spread(1)
    spread(3)
    share(1)
    spread(2)
    hand_on(0)
    share(2)
    hand_on(1)
    normalize(0)
    share(3)
    hand_on(3)
    share(4)
    hand_on(2)
    normalize(1)
    put_weights(0)
    put_weights(1)
    normalize(2)
    put_weights(3)
    put_weights(2)
    weights[...] = staged[:, : 2 * U].astype(BF)

    normalize(3)
    normalize(4)

    both = dot(normed[...], weights[...])
    down[...] = staged[:, 2 * U :].astype(BF)
    dglu = dot(cot[...], down[...])
    value, gate = both[:, :U], both[:, U : 2 * U]
    sig = jax.nn.sigmoid(gate)
    glu = (value * sig).astype(BF)
    d_value = (dglu * sig).astype(BF)
    d_gate = (dglu * value * sig * (1.0 - sig)).astype(BF)

    d_both = jnp.concatenate([d_value, d_gate], axis=1)
    J = Z // 2 // 4
    steps = (0, 1, -1, 2)
    Q = cfg.pair

    def chunk(o, half, a):
        r = lax.rem(z + a + Z, 4)
        return jnp.concatenate(
            [rows_of(block.at[o], (half * (Z // 2) + r + 4 * j) * Q, Q, 8)[...] for j in range(J)], axis=0
        )

    for o in (2, 1, 3, 0):
        cols = pl.ds(pl.multiple_of(mod(x + o, X) * span, 128), span)
        block[o] = jnp.concatenate(
            [contract_rows(normed[:, cols], d_both), contract_rows(cot[:, cols], glu)], axis=1
        )
        for i, a in enumerate(steps):
            pair_out[o, i] = chunk(o, other, a).astype(BF)
        send(pair_out.at[o], pair_in.at[o], s_pair, r_pair.at[o], sibling)

    B = cfg.yrow
    half_b = B // 2

    def gather(h):
        drain(r_y.at[h], y_in.at[h])
        lines = y_own[h * half_b : (h + 1) * half_b, :]
        for k in range(Y - 1):
            lines = lines + y_in[h, k].astype(F32)
        ref = rows_of(result, y * B + h * half_b, half_b)
        ref[...] = lines.astype(BF)
        for d in (2, 1, 3):
            send(ref, ref, s_yg, r_yg.at[h], at_y(d))

    def put_out(h):
        drain(r_yg.at[h], result.at[0 : (Y - 1) * half_b])
        for i in range(Y):
            lo = i * B + h * half_b
            pltpu.make_async_copy(
                result.at[lo : lo + half_b], branch.at[lo : lo + half_b], s_put
            ).start()

    def to_x(i, o):
        x_out[i, o - 1] = (chunk(o, core, steps[i]) + pair_in[o, i].astype(F32)).astype(BF)
        send(x_out.at[i, o - 1], x_in.at[i, o - 1], s_x, r_x.at[i], at_x(o))

    for o in (2, 1, 3):
        drain(r_pair.at[o], pair_in.at[o])
        to_x(0, o)

    glu_rows[...] = dot(back, glu).astype(BF)
    for d in (2, 1, 3):
        some = rows_of(glu_rows, mod(y + d, Y) * B, B)[...]
        theirs = contract_cols(some, down[...]).astype(BF)
        for h in range(2):
            y_out[h, d - 1] = theirs[h * half_b : (h + 1) * half_b]
    for h in range(2):
        for d in (2, 1, 3):
            send(y_out.at[h, d - 1], y_in.at[h, d - 1], s_y, r_y.at[h], at_y(d))
    y_own[...] = contract_cols(rows_of(glu_rows, y * B, B)[...], down[...])

    for i in range(1, 4):
        for o in (2, 1, 3):
            to_x(i, o)
    drain(r_pair.at[0], pair_in.at[0])

    def summed(i, a):
        drain(r_x.at[i], x_in.at[i])
        total = chunk(0, core, a) + pair_in[0, i].astype(F32)
        for k in range(X - 1):
            total = total + x_in[i, k].astype(F32)
        return total

    O = cfg.own
    sends = []

    def to_owners(i):
        a = steps[i]
        total = summed(i, a)
        z_out[i] = pack(cfg, total.astype(BF))
        for j in range(J):
            t = core * (Z // 2) + 4 * j + lax.rem(z + a + Z, 4)
            for c in range(CORES):
                lo = j * CORES + c
                copy = pltpu.make_async_remote_copy(
                    src_ref=z_out.at[i, lo * cfg.pad : (lo + 1) * cfg.pad], dst_ref=z_in.at[mod(z - t, Z)],
                    send_sem=s_own.at[j, c] if a == 0 else s_z, recv_sem=r_z,
                    device_id=at(x, t, c), device_id_type=pl.DeviceIdType.MESH,
                )
                if a == 0:
                    acc[j, c, 0:O, :] = total[lo * O : (lo + 1) * O]
                    sends.append((t != z, copy))
                    pl.when(t != z)(copy.start)
                else:
                    copy.start()

    to_owners(0)
    gather(0)
    to_owners(1)
    to_owners(2)
    gather(1)
    to_owners(3)

    is_owner = lax.div(z, Z // 2) == core
    own_j = lax.rem(lax.div(z, 4), J)
    hand = pltpu.make_async_remote_copy(
        src_ref=acc.at[own_j, other], dst_ref=final, send_sem=s_fin, recv_sem=r_fin,
        device_id=sibling, device_id_type=pl.DeviceIdType.MESH,
    )

    @pl.when(is_owner)
    def _():
        hand.start()
        final[...] = acc[own_j, core]
        hand.wait_send()

    @pl.when(jnp.logical_not(is_owner))
    def _():
        hand.wait_recv()

    put_out(0)
    drain(r_z, z_in.at[1:Z])
    whole = z_in[1].astype(F32)
    for slot in range(2, Z):
        whole = whole + z_in[slot].astype(F32)
    rest = cfg.cols - cfg.main
    tail = []
    for r in range(O):
        lo, line = r % cfg.fold * rest, O + r // cfg.fold
        tail.append(whole[line : line + 1, lo : lo + rest])
    whole = jnp.concatenate([whole[0:O], jnp.concatenate(tail, axis=0)], axis=1)
    last[...] = whole + final[0:O, :]
    put_last = pltpu.make_async_copy(last, owned, s_in.at[0])
    put_last.start()

    put_out(1)

    drain(s_a1, out1.at[0 : (G - 1) * cfg.grow])
    drain(s_a2, out2.at[0 : (Z - 1) * cfg.zrow])
    drain(s_ag, moved.at[0 : Y - 1])
    drain(s_wf, shards.at[0, 0 : (F - 1) * cfg.pad])
    drain(s_wn, shards.at[:, 0 : 3 * cfg.pad])
    drain(s_wx, w_own.at[:, 1:X])
    drain(s_sib, w_own)
    drain(s_pair, pair_out)
    drain(s_x, x_out)
    drain(s_z, z_out.at[1:4])
    drain(s_y, y_out)
    drain(s_yg, result.at[0 : (Y - 1) * B])
    for needed, copy in sends:
        pl.when(needed)(copy.wait_send)
    drain(s_put, result)
    put_last.wait()


def place_results(units, branch_in, owned_in, branch, grad_value, grad_gate, grad_down):
    branch[...] = branch_in[...]
    grad_value[...] = owned_in[:, :units]
    grad_gate[...] = owned_in[:, units : 2 * units]
    grad_down[...] = owned_in[:, 2 * units :]


def module(cfg, frames, lengths, send_order, value_weight, gate_weight, down_weight, cotangent):
    X, Z, Y, G, R, D, U = cfg.X, cfg.Z, cfg.Y, cfg.G, cfg.rows, cfg.width, cfg.units
    C, S, B = cfg.cols, cfg.half, cfg.yrow
    vmem, hbm = pl.BlockSpec(memory_space=pltpu.VMEM), pl.BlockSpec(memory_space=pl.ANY)
    sem = pltpu.SemaphoreType.DMA
    F, J, H = cfg.far, Z // 8, Z // 8 * cfg.pair
    buffers = [
        ((R, cfg.part), BF),
        ((R, D), BF),
        ((R, cfg.part), BF),
        ((R, cfg.part), BF),
        ((R, cfg.part), BF),
        ((Y, R, cfg.part), BF),
        ((R, D), BF),
        ((R, D), BF),
        ((R, U), BF),
        ((F, 4 * cfg.pad, cfg.main), BF),
        ((F, X, cfg.comb, C), BF),
        ((F, X, cfg.comb, C), BF),
        ((D, C), F32),
        ((D, 2 * U), BF),
        ((D, U), BF),
        ((X, Z * cfg.pair, C), F32),
        ((X, 4, H, C), BF),
        ((X, 4, H, C), BF),
        ((4, X - 1, H, C), BF),
        ((4, X - 1, H, C), BF),
        ((4, J * CORES * cfg.pad, cfg.main), BF),
        ((Z, cfg.pad, cfg.main), BF),
        ((J, CORES, cfg.pad, C), F32),
        ((cfg.pad, C), F32),
        ((cfg.own, C), F32),
        ((B, D), F32),
        ((2, Y - 1, B // 2, D), BF),
        ((2, Y - 1, B // 2, D), BF),
        ((R, D), BF),
    ]
    one = ()
    sems = [
        one, one, one, (5,), one, (5,),
        one, (F,), one, (F,), one, (F,), one, (F,),
        one, (X,), one, (4,), one, one, (J, CORES), one, one,
        one, (2,), one, (2,),
    ]
    branch, owned = pl.pallas_call(
        functools.partial(kernel, cfg),
        out_shape=(jax.ShapeDtypeStruct((R, D), BF), jax.ShapeDtypeStruct((cfg.own, C), F32)),
        in_specs=[pl.BlockSpec(memory_space=pltpu.SMEM), vmem, hbm, vmem, vmem, vmem, hbm],
        out_specs=(hbm, hbm),
        scratch_shapes=[pltpu.VMEM(shape, kind) for shape, kind in buffers]
        + [sem(n) for n in sems]
        + [pltpu.SemaphoreType.REGULAR, sem((2,)), sem(one)],
        compiler_params=pltpu.CompilerParams(
            collective_id=0, has_side_effects=True, vmem_limit_bytes=56 * 1024 * 1024
        ),
    )(lengths, send_order, frames, value_weight, gate_weight, down_weight, cotangent)
    return pl.pallas_call(
        functools.partial(place_results, U),
        out_shape=(jax.ShapeDtypeStruct((R, D), BF),) + (jax.ShapeDtypeStruct((cfg.own, U), F32),) * 3,
        in_specs=[vmem] * 2,
        out_specs=(vmem,) * 4,
    )(branch, owned)


def build(mesh, X, Z):
    def shards(frames, lengths, send_order, value_weight, gate_weight, down_weight, cotangent):
        cfg = Sizes(
            X, Z, mesh.shape["mp"], frames.shape[0], frames.shape[1],
            value_weight.shape[0], value_weight.shape[1],
        )
        return module(
            cfg, frames, lengths, send_order, value_weight, gate_weight, down_weight, cotangent
        )

    return jax.shard_map(
        shards,
        mesh=mesh,
        in_specs=(
            P("dp", None),
            P("dp"),
            P("dp", None),
            P("dp", "mp"),
            P("dp", "mp"),
            P("dp", "mp"),
            P("dp", None),
        ),
        out_specs=(P("dp", None), P("dp", "mp"), P("dp", "mp"), P("dp", "mp")),
        check_vma=False,
    )


def solution(mesh):
    return build(mesh, 4, 16)
```
